32 devices in a mesh: blk: 8 (over y, x, core), rep: 4 (over z).
Axes of the slice: x: 2, y: 2, z: 4, core: 2. Of those that a mesh axis runs over, the one named last changes fastest.
Arguments:
- coords: float32 [192, 4096], P('rep', 'blk'), may hold values from -4 to 4
- eigvecs: float32 [128, 4096], P(None, ('blk', 'rep')), may hold values from -0.36 to 0.36
- nbr_list: int32 [32, 8], P('blk'), may hold values from 0 to 31, as said below
- nbr_count: int32 [32], P('blk'), may hold values from 2 to 8, as said below
Outputs:
- smoothed: float32 [128, 4096], P(None, ('blk', 'rep'))
The draws below stay inside these ranges and needn't reach their ends.
Inputs may be any that keep to these rules, and one draw needn't show every extreme that they name: `nbr_count`: the largest count is exactly 8 in every draw; counts differ from block to block. `nbr_list`: the first nbr_count entries of a row are distinct block indices; entries after them are not used.
All inputs are finite; a program needn't handle non-finite values.
Results may differ from the reference program's by a relative error of at most 0.0003.
Values sent between devices are 32-bit elements; how exact they have to be, the bound alone decides.
No kernel may reach another device: no remote copies, remote signals or barrier semaphores. Data moves between devices by JAX's collectives and lax.ppermute only.
A program may use at most 64 MiB of HBM per device.

```python
import jax
import jax.numpy as jnp
from jax import lax

TRAJ_BLOCK = 128
T_SAMPLES = 64
COORDS = 3
EIG = 128
FEAT = 192
NBLOCKS = 32
NTRAJ = 4096
NBR_MAX = 8
NBR_MIN = 2


def draw_coords(key, part):
    start_key, speed_key, accel_key, noise_key = jax.random.split(jax.random.fold_in(key, 3), 4)
    times = jnp.arange(T_SAMPLES, dtype=jnp.float32) / T_SAMPLES
    start = jax.random.uniform(start_key, (COORDS, 1, NTRAJ), jnp.float32, -1.0, 1.0)
    speed = 0.4 * jnp.clip(jax.random.normal(speed_key, (COORDS, 1, NTRAJ), jnp.float32), -2.0, 2.0)
    accel = 0.3 * jnp.clip(jax.random.normal(accel_key, (COORDS, 1, NTRAJ), jnp.float32), -2.0, 2.0)
    noise = 0.25 * jnp.clip(jax.random.normal(noise_key, (COORDS, T_SAMPLES, NTRAJ), jnp.float32), -4.0, 4.0)
    values = start + speed * times[None, :, None] + accel * (times * times)[None, :, None] + noise
    return values.reshape(FEAT, NTRAJ)


def draw_nbr_count(key, part):
    base_key, factor_key, peak_key = jax.random.split(jax.random.fold_in(key, 7), 3)
    spread = jax.random.randint(base_key, (NBLOCKS,), 0, NBR_MAX - NBR_MIN + 1)
    factor = jax.random.randint(factor_key, (NBLOCKS,), 1, 5)
    counts = NBR_MIN + spread * factor // 4
    peak = jax.random.randint(peak_key, (), 0, NBLOCKS)
    return jnp.where(jnp.arange(NBLOCKS, dtype=jnp.int32) == peak, NBR_MAX, counts).astype(jnp.int32)


def draw_nbr_list(key, part):
    score_key = jax.random.fold_in(key, 11)
    scores = jax.random.randint(score_key, (NBLOCKS, NBLOCKS), 0, 262144) * NBLOCKS
    scores = scores + jnp.arange(NBLOCKS, dtype=jnp.int32)[None, :]
    picked = lax.top_k(scores, NBR_MAX)[1]
    return picked.astype(jnp.int32)


def block_scale(stream_key, extent, pieces, low, high):
    loudness, own = 1.0, jax.random.fold_in(stream_key, 6)
    for axis_at, shards_of in pieces:
        heights = jnp.exp(jax.random.uniform(jax.random.fold_in(own, axis_at), (shards_of,), jnp.float32, low / len(pieces), high / len(pieces)))
        loudness = loudness * jnp.repeat(heights, extent[axis_at] // shards_of).reshape([-1 if axis == axis_at else 1 for axis in range(len(extent))])
    return loudness


def gaussian(own_key, shape, scale, bound, cuts=(), kind=jnp.bfloat16):
    level = block_scale(own_key, shape, cuts, -0.22, 0.18) if cuts else 1.0
    array = jax.random.normal(own_key, shape, jnp.float32) * scale * level
    return jnp.minimum(jnp.maximum(array, -bound), bound).astype(kind)


def setup_inputs(seed: int = 0) -> dict:
    keys = jax.random.split(jax.random.key(seed), 5)
    coords = draw_coords(jax.random.fold_in(keys[4], 71), 0)
    eigvecs = gaussian(keys[1], (EIG, NTRAJ), 0.06, 0.36, ((1, 32),), jnp.float32)
    nbr_list = draw_nbr_list(jax.random.fold_in(keys[4], 71), 0)
    nbr_count = draw_nbr_count(jax.random.fold_in(keys[4], 71), 0)
    return dict(coords=coords, eigvecs=eigvecs, nbr_list=nbr_list, nbr_count=nbr_count)


def reference(coords, eigvecs, nbr_list, nbr_count):
    tiles = coords.reshape(FEAT, NBLOCKS, TRAJ_BLOCK)
    vec_tiles = eigvecs.reshape(EIG, NBLOCKS, TRAJ_BLOCK)
    norms = jnp.sum(tiles * tiles, axis=0)
    slot_ids = jnp.arange(NBR_MAX, dtype=jnp.int32)
    kernel_scale = FEAT * 1.0

    def one_block(inputs):
        row_id, neighbours, count = inputs
        row_x = jnp.take(tiles, row_id, axis=1)
        col_x = jnp.take(tiles, neighbours, axis=1)
        col_v = jnp.take(vec_tiles, neighbours, axis=1)
        inner_prod = jnp.einsum("ft,fku->ktu", row_x, col_x, precision=lax.Precision.HIGHEST)
        row_sq = jnp.take(norms, row_id, axis=0)
        col_sq = jnp.take(norms, neighbours, axis=0)
        dist_sq = row_sq[None, :, None] + col_sq[:, None, :] - 2.0 * inner_prod
        weight = jnp.exp(-dist_sq / kernel_scale)
        weight = jnp.where((slot_ids < count)[:, None, None], weight, 0.0)
        return jnp.einsum("ktu,eku->et", weight, col_v, precision=lax.Precision.HIGHEST)

    blocks = lax.map(one_block, (jnp.arange(NBLOCKS, dtype=jnp.int32), nbr_list, nbr_count))
    return jnp.transpose(blocks, (1, 0, 2)).reshape(EIG, NTRAJ)
```

```python
import functools

import jax
import jax.numpy as jnp
from jax import lax
from jax.experimental import pallas as pl
from jax.experimental.pallas import tpu as pltpu
from jax.sharding import PartitionSpec as P


def halves(value):
    high = value.astype(jnp.bfloat16)
    return high, (value - high.astype(jnp.float32)).astype(jnp.bfloat16)


def three_pass(lhs, rhs, dims):
    lhs_high, lhs_low = lhs
    rhs_high, rhs_low = rhs
    mul = functools.partial(
        lax.dot_general, dimension_numbers=(dims, ((), ())), preferred_element_type=jnp.float32
    )
    return mul(lhs_high, rhs_high) + (mul(lhs_high, rhs_low) + mul(lhs_low, rhs_high))


def apply_kernel(row_ref, mask_ref, *refs):
    panels, out_ref = refs[:-1], refs[-1]
    rows = row_ref[...]
    feat_count = rows.shape[0]
    row_scale = jnp.exp(jnp.sum(rows * rows, axis=0, keepdims=True) * (-1.0 / feat_count))
    row_halves = halves(rows * (2.0 / feat_count))
    total = None
    for place, panel in enumerate(panels):
        cols = panel[:feat_count, :]
        vecs = panel[feat_count:, :]
        col_scale = jnp.exp(jnp.sum(cols * cols, axis=0, keepdims=True) * (-1.0 / feat_count))
        inner = three_pass(halves(cols), row_halves, ((0,), (0,)))
        weight = jnp.exp(inner) * mask_ref[place : place + 1, :]
        part = three_pass(halves(vecs * col_scale), halves(weight), ((1,), (0,)))
        total = part if total is None else total + part
    out_ref[...] = total * row_scale


def swapped(value, step):
    count = lax.axis_size("blk")
    return lax.ppermute(value, "blk", [(source, source ^ step) for source in range(count)])


def shards(coords, eigvecs, nbr_list, nbr_count):
    cycle_size = lax.axis_size("blk")
    rep_size = lax.axis_size("rep")
    blk_index = lax.axis_index("blk")
    rep_index = lax.axis_index("rep")
    group_blocks, slot_count = nbr_list.shape
    eig_count, own_width = eigvecs.shape

    steps = jnp.arange(cycle_size, dtype=jnp.int32)
    columns = (blk_index ^ steps) * rep_size + rep_index
    used = jnp.arange(slot_count, dtype=jnp.int32)[None, :] < nbr_count[:, None]
    listed = jnp.any((nbr_list[None] == columns[:, None, None]) & used[None], axis=2)
    mask = jnp.repeat(listed.astype(jnp.float32), own_width, axis=1)

    gathered = lax.all_gather(coords, "rep", axis=0, tiled=True)
    own_coords = lax.dynamic_slice_in_dim(gathered, rep_index * own_width, own_width, 1)
    panels = {0: jnp.concatenate([own_coords, eigvecs], axis=0)}
    for step in range(2, cycle_size, 2):
        panels[step] = swapped(panels[0], step)
    for step in range(0, cycle_size, 2):
        panels[step + 1] = swapped(panels[step], 1)

    partial_value = pl.pallas_call(
        apply_kernel,
        out_shape=jax.ShapeDtypeStruct((eig_count, group_blocks * own_width), jnp.float32),
        compiler_params=pltpu.CompilerParams(vmem_limit_bytes=48 * 1024 * 1024),
    )(gathered, mask, *[panels[step] for step in range(cycle_size)])

    pieces = partial_value.reshape(eig_count, group_blocks, own_width).transpose(1, 0, 2)
    arrived = lax.all_to_all(pieces, "rep", 0, 0)
    return jnp.sum(arrived, axis=0)


def solution(mesh):
    return jax.shard_map(
        shards,
        mesh=mesh,
        in_specs=(P("rep", "blk"), P(None, ("blk", "rep")), P("blk", None), P("blk")),
        out_specs=P(None, ("blk", "rep")),
        check_vma=False,
    )
```

```python
import functools

import jax
import jax.numpy as jnp
from jax import lax
from jax.experimental import pallas as pl
from jax.experimental.pallas import tpu as pltpu
from jax.sharding import PartitionSpec as P

VMEM_BYTES = 48 * 1024 * 1024


def halves(value):
    high = value.astype(jnp.bfloat16)
    return high, (value - high.astype(jnp.float32)).astype(jnp.bfloat16)


def three_pass(lhs, rhs, dims):
    lhs_high, lhs_low = lhs
    rhs_high, rhs_low = rhs
    mul = functools.partial(
        lax.dot_general, dimension_numbers=(dims, ((), ())), preferred_element_type=jnp.float32
    )
    return mul(lhs_high, rhs_high) + (mul(lhs_high, rhs_low) + mul(lhs_low, rhs_high))


def order_kernel(rank_ref, coords_ref, own_ref, *out_refs):
    count = len(out_refs) // 2 + 1
    width = coords_ref.shape[1] // count
    for place in range(count):
        start = pl.multiple_of((rank_ref[0] ^ place) * width, width)
        block = coords_ref[:, pl.ds(start, width)]
        own_ref[:, place * width : (place + 1) * width] = block
        for step in range(1, count):
            theirs = place ^ step
            if theirs == 0:
                out_refs[2 * step - 2][...] = block
            else:
                out_refs[2 * step - 1][:, (theirs - 1) * width : theirs * width] = block


def apply_kernel(row_ref, mask_ref, *refs):
    panel_count = mask_ref.shape[0]
    col_refs, vec_refs, out_refs = refs[:panel_count], refs[panel_count : 2 * panel_count], refs[2 * panel_count :]
    rows = row_ref[...]
    feat_count = rows.shape[0]
    width = out_refs[0].shape[1]
    row_scale = jnp.exp(jnp.sum(rows * rows, axis=0, keepdims=True) * (-1.0 / feat_count))
    row_halves = halves(rows * (2.0 / feat_count))
    total = None
    for place in range(0, panel_count, 2):
        cols = jnp.concatenate([col_refs[place][...], col_refs[place + 1][...]], axis=1)
        vecs = jnp.concatenate([vec_refs[place][...], vec_refs[place + 1][...]], axis=1)
        col_scale = jnp.exp(jnp.sum(cols * cols, axis=0, keepdims=True) * (-1.0 / feat_count))
        inner = three_pass(halves(cols), row_halves, ((0,), (0,)))
        both = [
            jnp.broadcast_to(mask_ref[spot : spot + 1, :], (inner.shape[0] // 2, inner.shape[1]))
            for spot in (place, place + 1)
        ]
        weight = jnp.exp(inner) * jnp.concatenate(both, axis=0)
        part = three_pass(halves(vecs * col_scale), halves(weight), ((1,), (0,)))
        total = part if total is None else total + part
    total = total * row_scale
    for spot, out_ref in enumerate(out_refs):
        out_ref[...] = total[:, spot * width : (spot + 1) * width]


def swapped(value, axis, step):
    count = lax.axis_size(axis)
    return lax.ppermute(value, axis, [(source, source ^ step) for source in range(count)])


def shards(coords, eigvecs, nbr_list, nbr_count):
    cycle_size = lax.axis_size("blk")
    rep_size = lax.axis_size("rep")
    blk_index = lax.axis_index("blk")
    rep_index = lax.axis_index("rep")
    group_blocks, slot_count = nbr_list.shape
    eig_count, width = eigvecs.shape
    piece_feats = coords.shape[0]

    piece = jax.ShapeDtypeStruct((piece_feats, width), jnp.float32)
    others = jax.ShapeDtypeStruct((piece_feats, (rep_size - 1) * width), jnp.float32)
    vmem = pl.BlockSpec(memory_space=pltpu.VMEM)
    ordered = pl.pallas_call(
        order_kernel,
        in_specs=[pl.BlockSpec(memory_space=pltpu.SMEM), vmem],
        out_specs=[vmem] * (2 * rep_size - 1),
        out_shape=[jax.ShapeDtypeStruct(coords.shape, jnp.float32)] + [piece, others] * (rep_size - 1),
    )(rep_index.astype(jnp.int32).reshape(1), coords)
    own_pieces = [ordered[0][:, :width]]
    for step in range(1, rep_size):
        own_pieces.append(swapped(ordered[2 * step - 1], "rep", step))
    other_pieces = [ordered[0][:, width:]]
    for step in range(1, rep_size):
        other_pieces.append(swapped(ordered[2 * step], "rep", step))

    even = range(0, cycle_size, 2)
    vecs = {0: eigvecs}
    for step in even[1:]:
        vecs[step] = swapped(eigvecs, "blk", step)
    sibling = swapped(jnp.concatenate([vecs[step] for step in even], axis=0), "blk", 1)
    for place, step in enumerate(even):
        vecs[step + 1] = sibling[place * eig_count : (place + 1) * eig_count]

    own_block = jnp.concatenate(own_pieces, axis=0)
    cols = {0: own_block}
    for step in even[1:]:
        cols[step] = swapped(own_block, "blk", step)
    for step in even:
        cols[step + 1] = swapped(cols[step], "blk", 1)

    places = jnp.arange(cycle_size, dtype=jnp.int32)
    columns = (blk_index ^ places) * rep_size + rep_index
    used = jnp.arange(slot_count, dtype=jnp.int32)[None, :] < nbr_count[:, None]
    hit = (nbr_list[None] == columns[:, None, None]) & used[None]
    blocks = jnp.arange(group_blocks, dtype=jnp.int32)
    placed = (blocks[None, :] ^ rep_index) == blocks[:, None]
    listed = jnp.any(hit[:, None] & placed[None, :, :, None], axis=(2, 3))
    mask = jnp.repeat(listed.astype(jnp.float32), width, axis=1)

    col_list = [cols[step] for step in range(cycle_size)]
    vec_list = [vecs[step] for step in range(cycle_size)]
    own_rows = jnp.concatenate(own_pieces, axis=0)
    other_rows = jnp.concatenate(other_pieces, axis=0)
    rows = jnp.concatenate([own_rows, other_rows], axis=1)
    half = rep_size // 2
    tiles = {}
    for first in (half, 0):
        span = slice(first * width, (first + half) * width)
        done = pl.pallas_call(
            apply_kernel,
            out_shape=[jax.ShapeDtypeStruct((eig_count, width), jnp.float32)] * half,
            compiler_params=pltpu.CompilerParams(vmem_limit_bytes=VMEM_BYTES),
        )(rows[:, span], mask[:, span], *col_list, *vec_list)
        for spot in range(half):
            tiles[first + spot] = done[spot]

    total = tiles[0]
    for step in range(1, rep_size):
        total = total + swapped(tiles[step], "rep", step)
    return total


def solution(mesh):
    return jax.shard_map(
        shards,
        mesh=mesh,
        in_specs=(P("rep", "blk"), P(None, ("blk", "rep")), P("blk", None), P("blk")),
        out_specs=P(None, ("blk", "rep")),
        check_vma=False,
    )
```

```python
import functools

import jax
import jax.numpy as jnp
from jax import lax
from jax.experimental import pallas as pl
from jax.experimental.pallas import tpu as pltpu
from jax.sharding import PartitionSpec as P

VMEM_BYTES = 12 * 1024 * 1024


def halves(value):
    high = value.astype(jnp.bfloat16)
    return high, (value - high.astype(jnp.float32)).astype(jnp.bfloat16)


def three_pass(lhs, rhs, dims):
    lhs_high, lhs_low = lhs
    rhs_high, rhs_low = rhs
    mul = functools.partial(
        lax.dot_general, dimension_numbers=(dims, ((), ())), preferred_element_type=jnp.float32
    )
    return mul(lhs_high, rhs_high) + (mul(lhs_high, rhs_low) + mul(lhs_low, rhs_high))


def mask_kernel(rep_size, list_ref, count_ref, out_ref):
    group_blocks, slot_count = list_ref.shape
    panel_count, row_count = out_ref.shape
    width = row_count // group_blocks
    blk_index, rep_index = lax.axis_index("blk"), lax.axis_index("rep")
    places = lax.broadcasted_iota(jnp.int32, (panel_count, width), 0)
    for block in range(group_blocks):

        def add_slot(slot, found):
            listed = list_ref[block, slot]
            here = (slot < count_ref[block]) & (lax.rem(listed, rep_size) == rep_index)
            place = jnp.where(here, lax.div(listed, rep_size) ^ blk_index, -1)
            return jnp.where(places == place, 1.0, found)

        found = jnp.zeros((panel_count, width), jnp.float32)
        if slot_count <= 8:
            for slot in range(slot_count):
                found = add_slot(slot, found)
        else:
            found = lax.fori_loop(0, slot_count, add_slot, found)
        out_ref[:, block * width : (block + 1) * width] = found


def apply_kernel(first, piece_count, mask_ref, before_ref, *refs):
    panel_count = mask_ref.shape[0]
    piece_refs, refs = refs[:piece_count], refs[piece_count:]
    col_refs, vec_refs, out_refs = refs[:panel_count], refs[panel_count : 2 * panel_count], refs[2 * panel_count :]
    width = out_refs[0].shape[1]
    rank = lax.axis_index("rep")

    def tiles_of(ref):
        spans = [pl.multiple_of((rank ^ (first + spot)) * width, width) for spot in range(len(out_refs))]
        return jnp.concatenate([ref[:, pl.ds(span, width)] for span in spans], axis=1)

    rows = jnp.concatenate([tiles_of(ref) for ref in piece_refs], axis=0)
    row_mask = tiles_of(mask_ref)
    feat_count = rows.shape[0]
    row_scale = jnp.exp(jnp.sum(rows * rows, axis=0, keepdims=True) * (-1.0 / feat_count))
    row_halves = halves(rows * (2.0 / feat_count))
    total = None
    for place in range(0, panel_count, 2):
        cols = jnp.concatenate([col_refs[place][...], col_refs[place + 1][...]], axis=1)
        vecs = jnp.concatenate([vec_refs[place][...], vec_refs[place + 1][...]], axis=1)
        col_scale = jnp.exp(jnp.sum(cols * cols, axis=0, keepdims=True) * (-1.0 / feat_count))
        inner = three_pass(halves(cols), row_halves, ((0,), (0,)))
        both = [
            jnp.broadcast_to(row_mask[spot : spot + 1, :], (inner.shape[0] // 2, inner.shape[1]))
            for spot in (place, place + 1)
        ]
        weight = jnp.exp(inner) * jnp.concatenate(both, axis=0)
        part = three_pass(halves(vecs * col_scale), halves(weight), ((1,), (0,)))
        total = part if total is None else total + part
    total = total * row_scale
    for spot, out_ref in enumerate(out_refs):
        out_ref[...] = total[:, spot * width : (spot + 1) * width]


def swapped(value, axis, step):
    count = lax.axis_size(axis)
    return lax.ppermute(value, axis, [(source, source ^ step) for source in range(count)])


def shards(coords, eigvecs, nbr_list, nbr_count):
    cycle_size = lax.axis_size("blk")
    rep_size = lax.axis_size("rep")
    rep_index = lax.axis_index("rep")
    group_blocks = nbr_list.shape[0]
    eig_count, width = eigvecs.shape

    pieces = [coords]
    for step in range(1, rep_size):
        low = step & -step
        pieces.append(swapped(pieces[step ^ low], "rep", low))
    own_block = jnp.concatenate(
        [lax.dynamic_slice_in_dim(piece, rep_index * width, width, 1) for piece in pieces], axis=0
    )

    even = range(0, cycle_size, 2)
    vecs = {0: eigvecs}
    for step in even[1:]:
        vecs[step] = swapped(eigvecs, "blk", step)
    sibling = swapped(jnp.concatenate([vecs[step] for step in even], axis=0), "blk", 1)
    for place, step in enumerate(even):
        vecs[step + 1] = sibling[place * eig_count : (place + 1) * eig_count]

    cols = {0: own_block}
    for step in even[1:]:
        cols[step] = swapped(own_block, "blk", step)
    for step in even:
        cols[step + 1] = swapped(cols[step], "blk", 1)

    params = pltpu.CompilerParams(vmem_limit_bytes=VMEM_BYTES)
    smem = pl.BlockSpec(memory_space=pltpu.SMEM)
    vmem = pl.BlockSpec(memory_space=pltpu.VMEM)
    mask = pl.pallas_call(
        functools.partial(mask_kernel, rep_size),
        in_specs=[smem, smem],
        out_shape=jax.ShapeDtypeStruct((cycle_size, group_blocks * width), jnp.float32),
        compiler_params=params,
    )(nbr_list, nbr_count)

    panels = [cols[step] for step in range(cycle_size)] + [vecs[step] for step in range(cycle_size)]
    half = rep_size // 2
    tiles = {}
    before = mask
    for first in (half, 0):
        done = pl.pallas_call(
            functools.partial(apply_kernel, first, rep_size),
            in_specs=[vmem, pl.BlockSpec(memory_space=pl.ANY)] + [vmem] * (len(pieces) + len(panels)),
            out_shape=[jax.ShapeDtypeStruct((eig_count, width), jnp.float32)] * half,
            compiler_params=params,
        )(mask, before, *pieces, *panels)
        before = done[0]
        for spot in range(half):
            tiles[first + spot] = done[spot]

    total = tiles[0]
    for step in range(1, rep_size):
        total = total + swapped(tiles[step], "rep", step)
    return total


def solution(mesh):
    return jax.shard_map(
        shards,
        mesh=mesh,
        in_specs=(P("rep", "blk"), P(None, ("blk", "rep")), P("blk", None), P("blk")),
        out_specs=P(None, ("blk", "rep")),
        check_vma=False,
    )
```

```python
import functools

import jax
import jax.numpy as jnp
from jax import lax
from jax.experimental import pallas as pl
from jax.experimental.pallas import tpu as pltpu
from jax.sharding import PartitionSpec as P

def halves(value):
    high = value.astype(jnp.bfloat16)
    return high, (value - high.astype(jnp.float32)).astype(jnp.bfloat16)


def three_pass(lhs, rhs, dims):
    lhs_high, lhs_low = lhs
    rhs_high, rhs_low = rhs
    mul = functools.partial(
        lax.dot_general, dimension_numbers=(dims, ((), ())), preferred_element_type=jnp.float32
    )
    return mul(lhs_high, rhs_high) + (mul(lhs_high, rhs_low) + mul(lhs_low, rhs_high))


def mask_kernel(rep_size, list_ref, count_ref, own_ref, other_ref):
    group_blocks, slot_count = list_ref.shape
    panel_count, row_count = own_ref.shape
    width = row_count // group_blocks
    blk_index, rep_index = lax.axis_index("blk"), lax.axis_index("rep")
    places = 2 * lax.broadcasted_iota(jnp.int32, (panel_count, width), 0)
    for block in range(group_blocks):

        def add_slot(slot, found):
            own, other = found
            listed = list_ref[block, slot]
            here = (slot < count_ref[block]) & (lax.rem(listed, rep_size) == rep_index)
            place = jnp.where(here, lax.div(listed, rep_size) ^ blk_index, -1)
            return jnp.where(places == place, 1.0, own), jnp.where(places + 1 == place, 1.0, other)

        found = (jnp.zeros((panel_count, width), jnp.float32),) * 2
        if slot_count <= 8:
            for slot in range(slot_count):
                found = add_slot(slot, found)
        else:
            found = lax.fori_loop(0, slot_count, add_slot, found)
        span = slice(block * width, (block + 1) * width)
        own_ref[:, span], other_ref[:, span] = found


def apply_kernel(piece_count, panel_count, before_ref, *refs):
    piece_refs, refs = refs[:piece_count], refs[piece_count:]
    col_refs, vec_refs, out_ref = refs[:panel_count], refs[panel_count : 2 * panel_count], refs[2 * panel_count]
    feat_count, width = col_refs[0].shape
    block_count = out_ref.shape[0]
    rank = lax.axis_index("rep")
    spans = [pl.multiple_of((rank ^ spot) * width, width) for spot in range(block_count)]

    def tiles_of(ref):
        return jnp.concatenate([ref[:, pl.ds(span, width)] for span in spans], axis=1)

    rows = jnp.concatenate([tiles_of(ref) for ref in piece_refs], axis=0)
    rows, row_mask = rows[:feat_count], rows[feat_count:]
    row_scale = jnp.exp(jnp.sum(rows * rows, axis=0, keepdims=True) * (-1.0 / feat_count))
    row_halves = halves(rows * (2.0 / feat_count))
    total = None
    for place in range(0, panel_count, 2):
        cols = jnp.concatenate([col_refs[place][...], col_refs[place + 1][...]], axis=1)
        vecs = jnp.concatenate([vec_refs[place][...], vec_refs[place + 1][...]], axis=1)
        col_scale = jnp.exp(jnp.sum(cols * cols, axis=0, keepdims=True) * (-1.0 / feat_count))
        inner = three_pass(halves(cols), row_halves, ((0,), (0,)))
        both = [jnp.broadcast_to(row_mask[spot : spot + 1], (width, inner.shape[1])) for spot in (place, place + 1)]
        weight = jnp.exp(inner) * jnp.concatenate(both, axis=0)
        part = three_pass(halves(vecs * col_scale), halves(weight), ((1,), (0,)))
        total = part if total is None else total + part
    total = total * row_scale
    for spot in range(block_count):
        out_ref[spot] = total[:, spot * width : (spot + 1) * width]


def swapped(value, axis, step):
    count = lax.axis_size(axis)
    return lax.ppermute(value, axis, [(source, source ^ step) for source in range(count)])


def shards(coords, eigvecs, nbr_list, nbr_count):
    cycle_size = lax.axis_size("blk")
    rep_size = lax.axis_size("rep")
    rep_index = lax.axis_index("rep")
    group_blocks = nbr_list.shape[0]
    eig_count, width = eigvecs.shape

    pieces = [coords] + [swapped(coords, "rep", step) for step in range(1, rep_size)]
    own_block = jnp.concatenate(
        [lax.dynamic_slice_in_dim(piece, rep_index * width, width, 1) for piece in pieces], axis=0
    )

    vecs = eigvecs
    bit = 2
    while bit < cycle_size:
        vecs = jnp.concatenate([vecs, swapped(vecs, "blk", bit)], axis=0)
        bit *= 2
    panel_count = cycle_size // 2
    vec_list = [vecs[place * eig_count : (place + 1) * eig_count] for place in range(panel_count)]
    col_list = [own_block] + [swapped(own_block, "blk", step) for step in range(2, cycle_size, 2)]

    params = pltpu.CompilerParams(vmem_limit_bytes=(8 + group_blocks) * 1024 * 1024)
    smem = pl.BlockSpec(memory_space=pltpu.SMEM)
    vmem = pl.BlockSpec(memory_space=pltpu.VMEM)
    own_mask, other_mask = pl.pallas_call(
        functools.partial(mask_kernel, rep_size),
        in_specs=[smem, smem],
        out_shape=[jax.ShapeDtypeStruct((panel_count, group_blocks * width), jnp.float32)] * 2,
        compiler_params=params,
    )(nbr_list, nbr_count)

    def partial_tiles(row_pieces, before):
        return pl.pallas_call(
            functools.partial(apply_kernel, len(row_pieces), panel_count),
            in_specs=[pl.BlockSpec(memory_space=pl.ANY)] + [vmem] * (len(row_pieces) + 2 * panel_count),
            out_shape=jax.ShapeDtypeStruct((group_blocks, eig_count, width), jnp.float32),
            compiler_params=params,
        )(before, *row_pieces, *col_list, *vec_list)

    sibling_rows = swapped(jnp.concatenate([*pieces, other_mask], axis=0), "blk", 1)
    sibling_tiles = partial_tiles([sibling_rows], own_mask)
    own_tiles = partial_tiles([*pieces, own_mask], sibling_tiles)
    tiles = own_tiles + swapped(sibling_tiles, "blk", 1)

    total = tiles[0]
    for step in range(1, rep_size):
        total = total + swapped(tiles[step], "rep", step)
    return total


def solution(mesh):
    return jax.shard_map(
        shards,
        mesh=mesh,
        in_specs=(P("rep", "blk"), P(None, ("blk", "rep")), P("blk", None), P("blk")),
        out_specs=P(None, ("blk", "rep")),
        check_vma=False,
    )
```

```python
import functools

import jax
import jax.numpy as jnp
from jax import lax
from jax.experimental import pallas as pl
from jax.experimental.pallas import tpu as pltpu
from jax.sharding import PartitionSpec as P


COLUMNS_COST = 3 * 10**9


def halves(value):
    high = value.astype(jnp.bfloat16)
    return high, (value - high.astype(jnp.float32)).astype(jnp.bfloat16)


def three_pass(lhs, rhs, dims):
    lhs_high, lhs_low = lhs
    rhs_high, rhs_low = rhs
    mul = functools.partial(
        lax.dot_general, dimension_numbers=(dims, ((), ())), preferred_element_type=jnp.float32
    )
    return mul(lhs_high, rhs_high) + (mul(lhs_high, rhs_low) + mul(lhs_low, rhs_high))


def order_kernel(rep_size, coords_ref, *out_refs):
    width = coords_ref.shape[1] // rep_size
    rank = lax.axis_index("rep")
    for place in range(rep_size):
        start = pl.multiple_of((rank ^ place) * width, width)
        block = coords_ref[:, pl.ds(start, width)]
        for step in range(rep_size):
            theirs = place ^ step
            if step == 1:
                out_refs[-1][:, theirs * width : (theirs + 1) * width] = block
            elif theirs == 0:
                out_refs[2 * max(step - 1, 0)][...] = block
            else:
                out_refs[2 * max(step - 1, 0) + 1][:, (theirs - 1) * width : theirs * width] = block


def mask_kernel(rep_size, list_ref, count_ref, out_ref):
    group_blocks, slot_count = list_ref.shape
    panel_count, row_count = out_ref.shape
    width = row_count // group_blocks
    blk_index, rank = lax.axis_index("blk"), lax.axis_index("rep")
    spots = lax.broadcasted_iota(jnp.int32, (panel_count, width), 0)
    half = panel_count // 2
    places = jnp.where(spots < half, 2 * spots, 2 * (spots - half) + 1)
    for spot in range(group_blocks):
        block = rank ^ spot

        def add_slot(slot, found):
            listed = list_ref[block, slot]
            here = (slot < count_ref[block]) & (lax.rem(listed, rep_size) == rank)
            place = jnp.where(here, lax.div(listed, rep_size) ^ blk_index, -1)
            return jnp.where(places == place, 1.0, found)

        found = jnp.zeros((panel_count, width), jnp.float32)
        if slot_count <= 8:
            for slot in range(slot_count):
                found = add_slot(slot, found)
        else:
            found = lax.fori_loop(0, slot_count, add_slot, found)
        out_ref[:, spot * width : (spot + 1) * width] = found


def rows_kernel(piece_count, own_ref, mask_ref, *refs):
    rest_refs, out_ref = refs[:-1], refs[-1]
    feat_count, width = own_ref.shape
    piece_feats = feat_count // piece_count
    out_ref[:feat_count, :width] = own_ref[...]
    for piece, ref in enumerate(rest_refs):
        block = ref[:, ref.shape[1] - out_ref.shape[1] + width :]
        out_ref[piece * piece_feats : (piece + 1) * piece_feats, width:] = block
    out_ref[feat_count:, :] = mask_ref[...]


def columns_kernel(feat_count, *refs):
    panel_refs, out_refs = refs[:-4], refs[-4:]
    width = panel_refs[0].shape[1]
    for place, ref in enumerate(panel_refs):
        span = slice(place * width, (place + 1) * width)
        cols = ref[:feat_count, :]
        scale = jnp.exp(jnp.sum(cols * cols, axis=0, keepdims=True) * (-1.0 / feat_count))
        for out_ref, value in zip(out_refs, [*halves(cols), *halves(ref[feat_count:, :] * scale)]):
            out_ref[:, span] = value


def apply_kernel(tiles, mask_start, before_ref, row_ref, col_high, col_low, vec_high, vec_low, out_ref):
    feat_count, col_count = col_high.shape
    width = out_ref.shape[2]
    span = slice(tiles[0] * width, (tiles[-1] + 1) * width)
    rows = row_ref[:feat_count, span]
    row_scale = jnp.exp(jnp.sum(rows * rows, axis=0, keepdims=True) * (-1.0 / feat_count))
    row_halves = halves(rows * (2.0 / feat_count))
    total = None
    for place in range(0, col_count // width, 2):
        part = slice(place * width, (place + 2) * width)
        inner = three_pass((col_high[:, part], col_low[:, part]), row_halves, ((0,), (0,)))
        first = feat_count + mask_start + place
        both = [
            jnp.broadcast_to(row_ref[spot : spot + 1, span], (width, inner.shape[1])) for spot in (first, first + 1)
        ]
        weight = jnp.exp(inner) * jnp.concatenate(both, axis=0)
        added = three_pass((vec_high[:, part], vec_low[:, part]), halves(weight), ((1,), (0,)))
        total = added if total is None else total + added
    total = total * row_scale
    for spot in range(len(tiles)):
        out_ref[spot] = total[:, spot * width : (spot + 1) * width]


def swapped(value, axis, step):
    count = lax.axis_size(axis)
    return lax.ppermute(value, axis, [(source, source ^ step) for source in range(count)])


def shards(coords, eigvecs, nbr_list, nbr_count):
    cycle_size = lax.axis_size("blk")
    rep_size = lax.axis_size("rep")
    group_blocks = nbr_list.shape[0]
    eig_count, width = eigvecs.shape
    piece_feats = coords.shape[0]
    feat_count = rep_size * piece_feats
    panel_count = cycle_size // 2
    params = pltpu.CompilerParams(vmem_limit_bytes=(8 + group_blocks) * 1024 * 1024)
    smem = pl.BlockSpec(memory_space=pltpu.SMEM)
    vmem = pl.BlockSpec(memory_space=pltpu.VMEM)

    own_shape = jax.ShapeDtypeStruct((piece_feats, width), jnp.float32)
    rest_shape = jax.ShapeDtypeStruct((piece_feats, (rep_size - 1) * width), jnp.float32)
    ordered = pl.pallas_call(
        functools.partial(order_kernel, rep_size),
        out_shape=[own_shape, rest_shape] * (rep_size - 1) + [jax.ShapeDtypeStruct(coords.shape, jnp.float32)],
        compiler_params=params,
    )(coords)
    far = range(2, rep_size)
    own_far = [swapped(ordered[2 * step - 2], "rep", step) for step in far]
    near = swapped(ordered[-1], "rep", 1)
    own_pieces = [ordered[0], near[:, :width], *own_far]
    rest_pieces = [ordered[1], near] + [swapped(ordered[2 * step - 1], "rep", step) for step in far]

    own_block = jnp.concatenate(own_pieces, axis=0)
    panel = jnp.concatenate([own_block, eigvecs], axis=0)
    panels = [panel] + [swapped(panel, "blk", step) for step in range(2, cycle_size, 2)]

    masks = pl.pallas_call(
        functools.partial(mask_kernel, rep_size),
        in_specs=[smem, smem],
        out_shape=jax.ShapeDtypeStruct((2 * panel_count, group_blocks * width), jnp.float32),
        compiler_params=params,
    )(nbr_list, nbr_count)

    rows = pl.pallas_call(
        functools.partial(rows_kernel, rep_size),
        out_shape=jax.ShapeDtypeStruct((feat_count + 2 * panel_count, group_blocks * width), jnp.float32),
        compiler_params=params,
    )(own_block, masks, *rest_pieces)
    sibling_rows = swapped(rows, "blk", 1)

    high_low = [jax.ShapeDtypeStruct((size, panel_count * width), jnp.bfloat16) for size in (feat_count, eig_count)]
    columns = pl.pallas_call(
        functools.partial(columns_kernel, feat_count),
        out_shape=[high_low[0], high_low[0], high_low[1], high_low[1]],
        compiler_params=params,
        cost_estimate=pl.CostEstimate(flops=COLUMNS_COST, bytes_accessed=1048576, transcendentals=0),
    )(*panels)

    def partial_tiles(tiles, row_values, mask_start, before):
        return pl.pallas_call(
            functools.partial(apply_kernel, tiles, mask_start),
            in_specs=[pl.BlockSpec(memory_space=pl.ANY)] + [vmem] * 5,
            out_shape=jax.ShapeDtypeStruct((len(tiles), eig_count, width), jnp.float32),
            compiler_params=params,
        )(before, row_values, *columns)

    half = rep_size // 2
    totals = {}
    before = masks
    for first in (half, 0):
        tiles = range(first, first + half)
        theirs = partial_tiles(tiles, sibling_rows, panel_count, before)
        mine = partial_tiles(tiles, rows, 0, theirs)
        arrived = swapped(theirs, "blk", 1)
        for spot, tile in enumerate(tiles):
            totals[tile] = mine[spot] + arrived[spot]
        before = totals[tiles[-1]]

    for step in range(rep_size - 1, 0, -1):
        low = step & -step
        totals[step ^ low] = totals[step ^ low] + swapped(totals[step], "rep", low)
    return totals[0]


def solution(mesh):
    return jax.shard_map(
        shards,
        mesh=mesh,
        in_specs=(P("rep", "blk"), P(None, ("blk", "rep")), P("blk", None), P("blk")),
        out_specs=P(None, ("blk", "rep")),
        check_vma=False,
    )
```

```python
import functools

import jax
import jax.numpy as jnp
from jax import lax
from jax.experimental import pallas as pl
from jax.experimental.pallas import tpu as pltpu
from jax.sharding import PartitionSpec as P


TRANSFER_FLOPS = 3 * 10**9


def halves(value):
    high = value.astype(jnp.bfloat16)
    return high, (value - high.astype(jnp.float32)).astype(jnp.bfloat16)


def three_pass(lhs, rhs, dims):
    lhs_high, lhs_low = lhs
    rhs_high, rhs_low = rhs
    mul = functools.partial(
        lax.dot_general, dimension_numbers=(dims, ((), ())), preferred_element_type=jnp.float32
    )
    return mul(lhs_high, rhs_high) + (mul(lhs_high, rhs_low) + mul(lhs_low, rhs_high))


def lists_kernel(list_ref, count_ref, out_ref):
    rank = lax.axis_index("rep")
    for slot in range(out_ref.shape[0]):
        listed = jnp.where(slot < count_ref[rank], list_ref[rank, slot], -1)
        out_ref[slot : slot + 1, :] = jnp.full((1, out_ref.shape[1]), listed.astype(jnp.float32))


def columns_kernel(*refs):
    piece_refs, (high_ref, low_ref, scale_ref) = refs[:-3], refs[-3:]
    cols = jnp.concatenate([ref[...] for ref in piece_refs], axis=0)
    scale_ref[...] = jnp.exp(jnp.sum(cols * cols, axis=0, keepdims=True) * (-1.0 / cols.shape[0]))
    high_ref[...], low_ref[...] = halves(cols.T)


def rows_kernel(feat_count, *refs):
    panel_refs, (high_ref, low_ref, scale_ref, mask_ref) = refs[:-4], refs[-4:]
    width = panel_refs[0].shape[1]
    group_blocks = mask_ref.shape[0] // 2
    blk_index = lax.axis_index("blk")
    for place, ref in enumerate(panel_refs):
        span = slice(place * width, (place + 1) * width)
        rows = ref[:feat_count, :]
        scale_ref[:, span] = jnp.exp(jnp.sum(rows * rows, axis=0, keepdims=True) * (-1.0 / feat_count))
        high_ref[:, span], low_ref[:, span] = halves(rows * (2.0 / feat_count))
        lists = ref[feat_count:, :]
        for spot in range(2 * group_blocks):
            column = (blk_index ^ (spot // group_blocks)) * group_blocks + spot % group_blocks
            hits = jnp.where(lists == column.astype(jnp.float32), 1.0, 0.0)
            mask_ref[spot : spot + 1, span] = jnp.max(hits, axis=0, keepdims=True)


def vectors_kernel(before_ref, own_ref, sibling_ref, own_scale, sibling_scale, high_ref, low_ref):
    eig_count, group_cols = high_ref.shape[0], own_scale.shape[1]
    width = own_ref.shape[1]
    rank = lax.axis_index("rep")
    for group, (vec_ref, scale_ref) in enumerate(((own_ref, own_scale), (sibling_ref, sibling_scale))):
        for spot in range(group_cols // width):
            start = pl.multiple_of((rank ^ spot) * width, width)
            block = vec_ref[spot * eig_count : (spot + 1) * eig_count, :] * scale_ref[:, pl.ds(start, width)]
            there = pl.ds(group * group_cols + start, width)
            high_ref[:, there], low_ref[:, there] = halves(block)


def apply_kernel(first, count, before_ref, row_high, row_low, row_scale, mask_ref, *refs):
    own_high, own_low, sibling_high, sibling_low, vec_high, vec_low, *out_refs = refs
    width = out_refs[0].shape[1]
    group_cols = own_high.shape[0]
    span = slice(first * width, (first + count) * width)
    row_halves = row_high[:, span], row_low[:, span]
    total = None
    for group, (col_high, col_low) in enumerate(((own_high, own_low), (sibling_high, sibling_low))):
        for start in range(0, group_cols, 2 * width):
            part = slice(start, start + 2 * width)
            inner = three_pass((col_high[part, :], col_low[part, :]), row_halves, ((1,), (0,)))
            at = (group * group_cols + start) // width
            both = [jnp.broadcast_to(mask_ref[spot : spot + 1, span], (width, count * width)) for spot in (at, at + 1)]
            weight = jnp.exp(inner) * jnp.concatenate(both, axis=0)
            there = slice(group * group_cols + start, group * group_cols + start + 2 * width)
            added = three_pass((vec_high[:, there], vec_low[:, there]), halves(weight), ((1,), (0,)))
            total = added if total is None else total + added
    total = total * row_scale[:, span]
    for spot, out_ref in enumerate(out_refs):
        out_ref[...] = total[:, spot * width : (spot + 1) * width]


def add_kernel(*refs):
    total = refs[0][...]
    for ref in refs[1:-1]:
        total = total + ref[...]
    refs[-1][...] = total


def swapped(value, axis, step):
    count = lax.axis_size(axis)
    return lax.ppermute(value, axis, [(source, source ^ step) for source in range(count)])


def shards(coords, eigvecs, nbr_list, nbr_count):
    cycle_size = lax.axis_size("blk")
    rep_size = lax.axis_size("rep")
    rep_index = lax.axis_index("rep")
    group_blocks, slot_count = nbr_list.shape
    eig_count, width = eigvecs.shape
    feat_count = rep_size * coords.shape[0]
    params = pltpu.CompilerParams(vmem_limit_bytes=(8 + group_blocks) * 1024 * 1024)
    smem = pl.BlockSpec(memory_space=pltpu.SMEM)
    vmem = pl.BlockSpec(memory_space=pltpu.VMEM)
    anywhere = pl.BlockSpec(memory_space=pl.ANY)
    hint = pl.CostEstimate(flops=TRANSFER_FLOPS, bytes_accessed=1024 * 1024, transcendentals=0)

    pieces = [coords] + [swapped(coords, "rep", step) for step in range(1, rep_size)]
    own_block = jnp.concatenate(
        [lax.dynamic_slice_in_dim(piece, rep_index * width, width, 1) for piece in pieces], axis=0
    )
    vecs = eigvecs
    bit = 1
    while bit < rep_size:
        vecs = jnp.concatenate([vecs, swapped(vecs, "rep", bit)], axis=0)
        bit *= 2

    lists = pl.pallas_call(
        lists_kernel,
        in_specs=[smem, smem],
        out_shape=jax.ShapeDtypeStruct((slot_count, width), jnp.float32),
        compiler_params=params,
    )(nbr_list, nbr_count)
    panel = jnp.concatenate([own_block, lists], axis=0)
    panels = {0: panel}
    for step in range(2, cycle_size, 2):
        panels[step] = swapped(panel, "blk", step)

    f32, bf16 = jnp.float32, jnp.bfloat16
    group_cols = group_blocks * width
    row_count = len(panels) * width

    def columns_of(group_pieces):
        shape = jax.ShapeDtypeStruct((group_cols, feat_count), bf16)
        return pl.pallas_call(
            columns_kernel,
            out_shape=[shape, shape, jax.ShapeDtypeStruct((1, group_cols), f32)],
            compiler_params=params,
        )(*group_pieces)

    sibling_cols = swapped(jnp.concatenate(pieces, axis=0), "blk", 1)
    sibling_vecs = swapped(vecs, "blk", 1)
    own_high, own_low, own_scale = columns_of(pieces)
    sibling_high, sibling_low, sibling_scale = columns_of([sibling_cols])

    steps = list(range(0, cycle_size, 2))
    high_low = jax.ShapeDtypeStruct((feat_count, row_count), bf16)
    rows = pl.pallas_call(
        functools.partial(rows_kernel, feat_count),
        out_shape=[
            high_low,
            high_low,
            jax.ShapeDtypeStruct((1, row_count), f32),
            jax.ShapeDtypeStruct((2 * group_blocks, row_count), f32),
        ],
        compiler_params=params,
        cost_estimate=hint,
    )(*[panels[step] for step in steps])
    high_low = jax.ShapeDtypeStruct((eig_count, 2 * group_cols), bf16)
    vectors = pl.pallas_call(
        vectors_kernel,
        in_specs=[anywhere] + [vmem] * 4,
        out_shape=[high_low, high_low],
        compiler_params=params,
    )(rows[2], vecs, sibling_vecs, own_scale, sibling_scale)

    half = len(steps) // 2
    tiles = {}
    before = rows[2]
    for first in (half, 0):
        done = pl.pallas_call(
            functools.partial(apply_kernel, first, half),
            in_specs=[anywhere] + [vmem] * 10,
            out_shape=[jax.ShapeDtypeStruct((eig_count, width), f32)] * half,
            compiler_params=params,
        )(before, *rows, own_high, own_low, sibling_high, sibling_low, *vectors)
        before = done[0]
        for spot in range(half):
            tiles[steps[first + spot]] = done[spot]

    arrived = [swapped(tiles[step], "blk", step) for step in steps[1:]]
    far = pl.pallas_call(
        add_kernel,
        out_shape=jax.ShapeDtypeStruct((eig_count, width), f32),
        compiler_params=params,
        cost_estimate=hint,
    )(*arrived[half - 1 :])
    total = tiles[0]
    for tile in arrived[: half - 1]:
        total = total + tile
    return total + far


def solution(mesh):
    return jax.shard_map(
        shards,
        mesh=mesh,
        in_specs=(P("rep", "blk"), P(None, ("blk", "rep")), P("blk", None), P("blk")),
        out_specs=P(None, ("blk", "rep")),
        check_vma=False,
    )
```

```python
import functools

import jax
import jax.numpy as jnp
from jax import lax
from jax.experimental import pallas as pl
from jax.experimental.pallas import tpu as pltpu
from jax.sharding import PartitionSpec as P


TRANSFER_FLOPS = 7 * 10**9


def halves(value):
    high = value.astype(jnp.bfloat16)
    return high, (value - high.astype(jnp.float32)).astype(jnp.bfloat16)


def stacked(value, order, axis):
    high, low = halves(value)
    return jnp.concatenate([{"h": high, "l": low}[letter] for letter in order], axis=axis)


def lists_kernel(list_ref, count_ref, out_ref):
    rank = lax.axis_index("rep")
    for slot in range(out_ref.shape[0]):
        listed = jnp.where(slot < count_ref[rank], list_ref[rank, slot], -1)
        out_ref[slot : slot + 1, :] = jnp.full((1, out_ref.shape[1]), listed.astype(jnp.float32))


def near_kernel(coords_ref, vecs_ref, out_ref):
    piece_feats, group_cols = coords_ref.shape
    eig_count, width = vecs_ref.shape
    rows = eig_count * width // group_cols
    out_ref[:piece_feats, :] = coords_ref[...]
    for part in range(group_cols // width):
        out_ref[piece_feats:, part * width : (part + 1) * width] = vecs_ref[part * rows : (part + 1) * rows, :]


def pair_kernel(piece_feats, vecs_ref, near_ref, out_ref):
    eig_count, width = vecs_ref.shape
    rows = near_ref.shape[0] - piece_feats
    out_ref[:eig_count, :] = vecs_ref[...]
    for part in range(eig_count // rows):
        near = near_ref[piece_feats:, part * width : (part + 1) * width]
        out_ref[eig_count + part * rows : eig_count + (part + 1) * rows, :] = near


def group_kernel(piece_count, *refs):
    piece_refs, vec_refs, out_ref = refs[:piece_count], refs[piece_count:-1], refs[-1]
    piece_feats = piece_refs[0].shape[0]
    width = vec_refs[0].shape[1]
    feat_count = piece_count * piece_feats
    eig_count = out_ref.shape[0] - feat_count
    rank = lax.axis_index("rep")
    for piece, ref in enumerate(piece_refs):
        out_ref[piece * piece_feats : (piece + 1) * piece_feats, :] = ref[:piece_feats, :]
    spot = 0
    for ref in vec_refs:
        for start in range(0, ref.shape[0], eig_count):
            span = pl.ds(pl.multiple_of((rank ^ spot) * width, width), width)
            out_ref[feat_count:, span] = ref[start : start + eig_count, :]
            spot += 1


def columns_kernel(feat_count, group_ref, col_ref, vec_ref):
    chunk = 2 * vec_ref.shape[0]
    cols = group_ref[:feat_count, :]
    col_ref[...] = stacked(cols.T, "hhl", 1)
    vecs = group_ref[feat_count:, :] * jnp.exp(jnp.sum(cols * cols, axis=0, keepdims=True) * (-1.0 / feat_count))
    for start in range(0, cols.shape[1], chunk):
        vec_ref[:, 3 * start : 3 * (start + chunk)] = stacked(vecs[:, start : start + chunk], "hhl", 1)


def rows_kernel(feat_count, *refs):
    panel_refs, (row_ref, scale_ref, mask_ref) = refs[:-3], refs[-3:]
    width = panel_refs[0].shape[1]
    group_blocks = mask_ref.shape[0] // 2
    blk_index = lax.axis_index("blk")
    for place, ref in enumerate(panel_refs):
        span = slice(place * width, (place + 1) * width)
        rows = ref[:feat_count, :]
        scale_ref[:, span] = jnp.exp(jnp.sum(rows * rows, axis=0, keepdims=True) * (-1.0 / feat_count))
        row_ref[:, span] = stacked(rows * (2.0 / feat_count), "hlh", 0)
        lists = ref[feat_count:, :]
        for spot in range(2 * group_blocks):
            column = (blk_index ^ (spot // group_blocks)) * group_blocks + spot % group_blocks
            hits = jnp.where(lists == column.astype(jnp.float32), 1.0, 0.0)
            mask_ref[spot : spot + 1, span] = jnp.max(hits, axis=0, keepdims=True)


def apply_kernel(row_ref, scale_ref, mask_ref, *refs):
    own_cols, own_vecs, sibling_cols, sibling_vecs, *out_refs = refs
    eig_count, width = out_refs[0].shape
    group_cols = own_cols.shape[0]
    chunk = 2 * width
    rows = row_ref[...]
    total = None
    for group, (col_ref, vec_ref) in enumerate(((own_cols, own_vecs), (sibling_cols, sibling_vecs))):
        for start in range(0, group_cols, chunk):
            inner = jnp.dot(col_ref[start : start + chunk, :], rows, preferred_element_type=jnp.float32)
            at = (group * group_cols + start) // width
            both = [jnp.broadcast_to(mask_ref[spot : spot + 1, :], (width, rows.shape[1])) for spot in (at, at + 1)]
            weight = stacked(jnp.exp(inner) * jnp.concatenate(both, axis=0), "hlh", 0)
            vecs = vec_ref[:, 3 * start : 3 * (start + chunk)]
            added = jnp.dot(vecs, weight, preferred_element_type=jnp.float32)
            total = added if total is None else total + added
    total = total * scale_ref[...]
    for spot, out_ref in enumerate(out_refs):
        out_ref[...] = total[:, spot * width : (spot + 1) * width]


def swapped(value, axis, step):
    count = lax.axis_size(axis)
    return lax.ppermute(value, axis, [(source, source ^ step) for source in range(count)])


def shards(coords, eigvecs, nbr_list, nbr_count):
    cycle_size = lax.axis_size("blk")
    rep_size = lax.axis_size("rep")
    rep_index = lax.axis_index("rep")
    group_blocks, slot_count = nbr_list.shape
    eig_count, width = eigvecs.shape
    piece_feats, group_cols = coords.shape
    feat_count = rep_size * piece_feats
    f32, bf16 = jnp.float32, jnp.bfloat16
    shape = jax.ShapeDtypeStruct
    smem = pl.BlockSpec(memory_space=pltpu.SMEM)
    params = pltpu.CompilerParams(vmem_limit_bytes=(8 + group_blocks) * 1024 * 1024)
    hint = pl.CostEstimate(flops=TRANSFER_FLOPS, bytes_accessed=1024 * 1024, transcendentals=0)

    far = range(2, rep_size)
    far_coords = [swapped(coords, "rep", step) for step in far]
    near = pl.pallas_call(
        near_kernel,
        out_shape=shape((piece_feats + eig_count * width // group_cols, group_cols), f32),
        compiler_params=params,
    )(coords, eigvecs)
    near = swapped(near, "rep", 1)
    vecs = [
        pl.pallas_call(
            functools.partial(pair_kernel, piece_feats),
            out_shape=shape((2 * eig_count, width), f32),
            compiler_params=params,
        )(eigvecs, near)
    ]
    bit = 2
    while bit < rep_size:
        vecs.append(swapped(jnp.concatenate(vecs, axis=0), "rep", bit))
        bit *= 2
    lists = pl.pallas_call(
        lists_kernel,
        in_specs=[smem, smem],
        out_shape=shape((slot_count, width), f32),
        compiler_params=params,
    )(nbr_list, nbr_count)

    pieces = [coords, near[:piece_feats], *far_coords]
    own_block = [lax.dynamic_slice_in_dim(piece, rep_index * width, width, 1) for piece in pieces]
    panel = jnp.concatenate([*own_block, lists], axis=0)
    steps = list(range(0, cycle_size, 2))
    panels = [panel] + [swapped(panel, "blk", step) for step in steps[1:]]

    own_group = pl.pallas_call(
        functools.partial(group_kernel, rep_size),
        out_shape=shape((feat_count + eig_count, group_cols), f32),
        compiler_params=params,
    )(coords, near, *far_coords, *vecs)
    sibling_group = swapped(own_group, "blk", 1)

    def columns_of(group):
        return pl.pallas_call(
            functools.partial(columns_kernel, feat_count),
            out_shape=[shape((group_cols, 3 * feat_count), bf16), shape((eig_count, 3 * group_cols), bf16)],
            compiler_params=params,
        )(group)

    row_count = len(panels) * width
    rows = pl.pallas_call(
        functools.partial(rows_kernel, feat_count),
        out_shape=[
            shape((3 * feat_count, row_count), bf16),
            shape((1, row_count), f32),
            shape((2 * group_blocks, row_count), f32),
        ],
        compiler_params=params,
        cost_estimate=hint,
    )(*panels)
    tiles = pl.pallas_call(
        apply_kernel,
        out_shape=[shape((eig_count, width), f32)] * len(panels),
        compiler_params=params,
    )(*rows, *columns_of(own_group), *columns_of(sibling_group))

    total = tiles[0]
    for tile, step in zip(tiles[1:], steps[1:]):
        total = total + swapped(tile, "blk", step)
    return total


def solution(mesh):
    return jax.shard_map(
        shards,
        mesh=mesh,
        in_specs=(P("rep", "blk"), P(None, ("blk", "rep")), P("blk", None), P("blk")),
        out_specs=P(None, ("blk", "rep")),
        check_vma=False,
    )
```

```python
import functools

import jax
import jax.numpy as jnp
from jax import lax
from jax.experimental import pallas as pl
from jax.experimental.pallas import tpu as pltpu
from jax.sharding import PartitionSpec as P


TRANSFER_FLOPS = 62 * 10**8


def halves(value):
    high = value.astype(jnp.bfloat16)
    return high, (value - high.astype(jnp.float32)).astype(jnp.bfloat16)


def stacked(value, order, axis):
    high, low = halves(value)
    return jnp.concatenate([{"h": high, "l": low}[letter] for letter in order], axis=axis)


def lists_kernel(list_ref, count_ref, out_ref):
    rank = lax.axis_index("rep")
    for slot in range(out_ref.shape[0]):
        listed = jnp.where(slot < count_ref[rank], list_ref[rank, slot], -1)
        out_ref[slot : slot + 1, :] = jnp.full((1, out_ref.shape[1]), listed.astype(jnp.float32))


def copy_kernel(before_ref, in_ref, out_ref):
    out_ref[...] = in_ref[...]


def group_kernel(piece_count, *refs):
    piece_refs, vec_refs, out_ref = refs[:piece_count], refs[piece_count:-1], refs[-1]
    piece_feats = piece_refs[0].shape[0]
    width = vec_refs[0].shape[1]
    feat_count = piece_count * piece_feats
    rank = lax.axis_index("rep")
    for piece, ref in enumerate(piece_refs):
        out_ref[piece * piece_feats : (piece + 1) * piece_feats, :] = ref[...]
    for spot, ref in enumerate(vec_refs[::-1]):
        span = pl.ds(pl.multiple_of((rank ^ spot) * width, width), width)
        out_ref[feat_count:, span] = ref[...]


def columns_kernel(feat_count, group_ref, col_ref, vec_ref):
    chunk = 2 * vec_ref.shape[0]
    cols = group_ref[:feat_count, :]
    col_ref[...] = stacked(cols.T, "hhl", 1)
    vecs = group_ref[feat_count:, :] * jnp.exp(jnp.sum(cols * cols, axis=0, keepdims=True) * (-1.0 / feat_count))
    for start in range(0, cols.shape[1], chunk):
        vec_ref[:, 3 * start : 3 * (start + chunk)] = stacked(vecs[:, start : start + chunk], "hhl", 1)


def rows_kernel(feat_count, *refs):
    panel_refs, (row_ref, scale_ref, mask_ref) = refs[:-3], refs[-3:]
    width = panel_refs[0].shape[1]
    group_blocks = mask_ref.shape[0] // 2
    blk_index = lax.axis_index("blk")
    for place, ref in enumerate(panel_refs):
        span = slice(place * width, (place + 1) * width)
        rows = ref[:feat_count, :]
        scale_ref[:, span] = jnp.exp(jnp.sum(rows * rows, axis=0, keepdims=True) * (-1.0 / feat_count))
        row_ref[:, span] = stacked(rows * (2.0 / feat_count), "hlh", 0)
        lists = ref[feat_count:, :]
        for spot in range(2 * group_blocks):
            column = (blk_index ^ (spot // group_blocks)) * group_blocks + spot % group_blocks
            hits = jnp.where(lists == column.astype(jnp.float32), 1.0, 0.0)
            mask_ref[spot : spot + 1, span] = jnp.max(hits, axis=0, keepdims=True)


def apply_kernel(first, count, before_ref, row_ref, scale_ref, mask_ref, *refs):
    own_cols, own_vecs, sibling_cols, sibling_vecs, *out_refs = refs
    width = out_refs[0].shape[1]
    group_cols = own_cols.shape[0]
    chunk = 2 * width
    span = slice(first * width, (first + count) * width)
    rows = row_ref[:, span]
    total = None
    for group, (col_ref, vec_ref) in enumerate(((own_cols, own_vecs), (sibling_cols, sibling_vecs))):
        for start in range(0, group_cols, chunk):
            inner = jnp.dot(col_ref[start : start + chunk, :], rows, preferred_element_type=jnp.float32)
            at = (group * group_cols + start) // width
            both = [jnp.broadcast_to(mask_ref[spot : spot + 1, span], (width, count * width)) for spot in (at, at + 1)]
            weight = stacked(jnp.exp(inner) * jnp.concatenate(both, axis=0), "hlh", 0)
            vecs = vec_ref[:, 3 * start : 3 * (start + chunk)]
            added = jnp.dot(vecs, weight, preferred_element_type=jnp.float32)
            total = added if total is None else total + added
    total = total * scale_ref[:, span]
    for spot, out_ref in enumerate(out_refs):
        out_ref[...] = total[:, spot * width : (spot + 1) * width]


def add_kernel(*refs):
    total = refs[0][...]
    for ref in refs[1:-1]:
        total = total + ref[...]
    refs[-1][...] = total


def swapped(value, axis, step):
    count = lax.axis_size(axis)
    return lax.ppermute(value, axis, [(source, source ^ step) for source in range(count)])


def shards(coords, eigvecs, nbr_list, nbr_count):
    cycle_size = lax.axis_size("blk")
    rep_size = lax.axis_size("rep")
    rep_index = lax.axis_index("rep")
    group_blocks, slot_count = nbr_list.shape
    eig_count, width = eigvecs.shape
    piece_feats, group_cols = coords.shape
    feat_count = rep_size * piece_feats
    f32, bf16 = jnp.float32, jnp.bfloat16
    shape = jax.ShapeDtypeStruct
    smem = pl.BlockSpec(memory_space=pltpu.SMEM)
    vmem = pl.BlockSpec(memory_space=pltpu.VMEM)
    anywhere = pl.BlockSpec(memory_space=pl.ANY)
    params = pltpu.CompilerParams(vmem_limit_bytes=(8 + group_blocks) * 1024 * 1024)
    hint = pl.CostEstimate(flops=TRANSFER_FLOPS, bytes_accessed=1024 * 1024, transcendentals=0)

    pieces = [coords] + [swapped(coords, "rep", step) for step in range(1, rep_size)]
    late_vecs = pl.pallas_call(
        copy_kernel,
        in_specs=[anywhere, vmem],
        out_shape=shape(eigvecs.shape, f32),
        compiler_params=params,
    )(pieces[1], eigvecs)
    vecs = [swapped(late_vecs, "rep", step) for step in range(rep_size - 1, 0, -1)] + [late_vecs]
    lists = pl.pallas_call(
        lists_kernel,
        in_specs=[smem, smem],
        out_shape=shape((slot_count, width), f32),
        compiler_params=params,
    )(nbr_list, nbr_count)

    own_block = [lax.dynamic_slice_in_dim(piece, rep_index * width, width, 1) for piece in pieces]
    panel = jnp.concatenate([*own_block, lists], axis=0)
    steps = list(range(0, cycle_size, 2))
    panels = [panel] + [swapped(panel, "blk", step) for step in steps[1:]]

    own_group = pl.pallas_call(
        functools.partial(group_kernel, rep_size),
        out_shape=shape((feat_count + eig_count, group_cols), f32),
        compiler_params=params,
    )(*pieces, *vecs)
    sibling_group = swapped(own_group, "blk", 1)

    def columns_of(group):
        return pl.pallas_call(
            functools.partial(columns_kernel, feat_count),
            out_shape=[shape((group_cols, 3 * feat_count), bf16), shape((eig_count, 3 * group_cols), bf16)],
            compiler_params=params,
        )(group)

    row_count = len(panels) * width
    rows = pl.pallas_call(
        functools.partial(rows_kernel, feat_count),
        out_shape=[
            shape((3 * feat_count, row_count), bf16),
            shape((1, row_count), f32),
            shape((2 * group_blocks, row_count), f32),
        ],
        compiler_params=params,
        cost_estimate=hint,
    )(*panels)
    columns = [*columns_of(own_group), *columns_of(sibling_group)]
    half = len(steps) // 2
    tiles = {}
    before = rows[1]
    for first in (half, 0):
        done = pl.pallas_call(
            functools.partial(apply_kernel, first, half),
            in_specs=[anywhere] + [vmem] * 7,
            out_shape=[shape((eig_count, width), f32)] * half,
            compiler_params=params,
        )(before, *rows, *columns)
        before = done[0]
        for spot in range(half):
            tiles[first + spot] = done[spot]

    arrived = [swapped(tiles[place], "blk", steps[place]) for place in range(1, len(steps))]
    far = pl.pallas_call(
        add_kernel,
        out_shape=shape((eig_count, width), f32),
        compiler_params=params,
        cost_estimate=hint,
    )(*arrived[half - 1 :])
    total = tiles[0]
    for tile in arrived[: half - 1]:
        total = total + tile
    return total + far


def solution(mesh):
    return jax.shard_map(
        shards,
        mesh=mesh,
        in_specs=(P("rep", "blk"), P(None, ("blk", "rep")), P("blk", None), P("blk")),
        out_specs=P(None, ("blk", "rep")),
        check_vma=False,
    )
```

```python
import functools

import jax
import jax.numpy as jnp
from jax import lax
from jax.experimental import pallas as pl
from jax.experimental.pallas import tpu as pltpu
from jax.sharding import PartitionSpec as P


COLUMNS_FLOPS = 300 * 10**7
PAIR_FLOPS = 200 * 10**7
VECTORS_FLOPS = 300 * 10**7


def halves(value):
    high = value.astype(jnp.bfloat16)
    return high, (value - high.astype(jnp.float32)).astype(jnp.bfloat16)


def stacked(value, order, axis):
    high, low = halves(value)
    return jnp.concatenate([{"h": high, "l": low}[letter] for letter in order], axis=axis)


def lists_kernel(list_ref, count_ref, out_ref):
    rank = lax.axis_index("rep")
    for slot in range(out_ref.shape[0]):
        listed = jnp.where(slot < count_ref[rank], list_ref[rank, slot], -1)
        out_ref[slot : slot + 1, :] = jnp.full((1, out_ref.shape[1]), listed.astype(jnp.float32))


def below_kernel(before_ref, *refs):
    start = 0
    for ref in refs[:-1]:
        refs[-1][start : start + ref.shape[0], :] = ref[...]
        start += ref.shape[0]


def columns_kernel(order, *refs):
    piece_refs, (col_ref, bias_ref) = refs[:-2], refs[-2:]
    width = bias_ref.shape[1]
    rank = lax.axis_index("rep")
    for place, spot in enumerate(order):
        here = pl.ds(pl.multiple_of((rank ^ spot) * width, width), width)
        cols = jnp.concatenate([ref[:, here] for ref in piece_refs], axis=0).T
        there = slice(place * width, (place + 1) * width)
        bias = jnp.sum(cols * cols, axis=1, keepdims=True) * (-1.0 / cols.shape[1])
        bias_ref[there, :] = jnp.broadcast_to(bias, (width, width))
        col_ref[there, :] = stacked(cols, "hhl", 1)


def vectors_kernel(*refs):
    vec_refs, out_ref = refs[:-1], refs[-1]
    eig_count = out_ref.shape[0]
    blocks = [ref[top : top + eig_count, :] for ref in vec_refs for top in range(0, ref.shape[0], eig_count)]
    chunk = 2 * blocks[0].shape[1]
    for pair in range(len(blocks) // 2):
        vecs = jnp.concatenate(blocks[2 * pair : 2 * pair + 2], axis=1)
        out_ref[:, 3 * pair * chunk : 3 * (pair + 1) * chunk] = stacked(vecs, "hhl", 1)


def rows_kernel(feat_count, order, *refs):
    panel_refs, (row_ref, scale_ref, mask_ref) = refs[:-3], refs[-3:]
    width = panel_refs[0].shape[1]
    panel_size = sum(ref.shape[0] for ref in panel_refs) * width // row_ref.shape[1]
    blk_index, rank = lax.axis_index("blk"), lax.axis_index("rep")
    place = 0
    for ref in panel_refs:
        for top in range(0, ref.shape[0], panel_size):
            span = slice(place * width, (place + 1) * width)
            rows = ref[top : top + feat_count, :]
            scale_ref[:, span] = jnp.exp(jnp.sum(rows * rows, axis=0, keepdims=True) * (-1.0 / feat_count))
            row_ref[:, span] = stacked(rows * (2.0 / feat_count), "hlh", 0)
            lists = ref[top + feat_count : top + panel_size, :]
            for at, spot in enumerate(order):
                column = (blk_index * len(order) + (rank ^ spot)).astype(jnp.float32)
                hits = jnp.where(lists == column, 1.0, 0.0)
                mask_ref[at : at + 1, span] = jnp.max(hits, axis=0, keepdims=True)
            place += 1


def apply_kernel(before_ref, row_ref, scale_ref, mask_ref, col_ref, bias_ref, vec_ref, out_ref):
    width = out_ref.shape[2]
    chunk = 2 * width
    rows = row_ref[...]
    total = None
    for start in range(0, col_ref.shape[0], chunk):
        inner = jnp.dot(col_ref[start : start + chunk, :], rows, preferred_element_type=jnp.float32)
        at = start // width
        both = [jnp.broadcast_to(mask_ref[spot : spot + 1, :], (width, rows.shape[1])) for spot in (at, at + 1)]
        bias = jnp.concatenate([bias_ref[start : start + chunk, :]] * (rows.shape[1] // width), axis=1)
        weight = stacked(jnp.exp(inner + bias) * jnp.concatenate(both, axis=0), "hlh", 0)
        vecs = vec_ref[:, 3 * start : 3 * (start + chunk)]
        added = jnp.dot(vecs, weight, preferred_element_type=jnp.float32)
        total = added if total is None else total + added
    total = total * scale_ref[...]
    for spot in range(out_ref.shape[0]):
        out_ref[spot] = total[:, spot * width : (spot + 1) * width]


def swapped(value, axis, step):
    count = lax.axis_size(axis)
    return lax.ppermute(value, axis, [(source, source ^ step) for source in range(count)])


def shards(coords, eigvecs, nbr_list, nbr_count):
    cycle_size = lax.axis_size("blk")
    rep_size = lax.axis_size("rep")
    rep_index = lax.axis_index("rep")
    group_blocks, slot_count = nbr_list.shape
    eig_count, width = eigvecs.shape
    piece_feats, group_cols = coords.shape
    feat_count = rep_size * piece_feats
    f32, bf16 = jnp.float32, jnp.bfloat16
    shape = jax.ShapeDtypeStruct
    smem = pl.BlockSpec(memory_space=pltpu.SMEM)
    vmem = pl.BlockSpec(memory_space=pltpu.VMEM)
    anywhere = pl.BlockSpec(memory_space=pl.ANY)
    params = pltpu.CompilerParams(vmem_limit_bytes=(8 + group_blocks) * 1024 * 1024)

    def hint(flops):
        return pl.CostEstimate(flops=flops, bytes_accessed=1024 * 1024, transcendentals=0)

    def block_of(piece, block):
        return lax.dynamic_slice_in_dim(piece, block * width, width, 1)

    pieces, own_block = [coords], [block_of(coords, rep_index)]
    for step in range(1, rep_size):
        low = step & -step
        pieces.append(swapped(pieces[step ^ low], "rep", low))
        if step == low:
            own_block.append(block_of(pieces[step], rep_index))
        else:
            own_block.append(swapped(block_of(coords, rep_index ^ step), "rep", step))

    lists = pl.pallas_call(
        lists_kernel,
        in_specs=[smem, smem],
        out_shape=shape((slot_count, width), f32),
        compiler_params=params,
    )(nbr_list, nbr_count)
    panel = jnp.concatenate([*own_block, lists], axis=0)
    steps = list(range(0, cycle_size, 2))
    panels = [panel] + [swapped(panel, "blk", step) for step in steps[1:]]

    def below(before, values, **estimate):
        return pl.pallas_call(
            below_kernel,
            in_specs=[anywhere] + [vmem] * len(values),
            out_shape=shape((sum(value.shape[0] for value in values), width), f32),
            compiler_params=params,
            **estimate,
        )(before, *values)

    vecs, order = [eigvecs], [0]
    bit = rep_size // 2
    while bit:
        if len(vecs) > 1:
            vecs = [below(panels[1], [vecs[0], below(lists, vecs[1:], cost_estimate=hint(PAIR_FLOPS))])]
        vecs.append(swapped(vecs[0], "rep", bit))
        order += [spot ^ bit for spot in order]
        bit //= 2

    cols = pl.pallas_call(
        functools.partial(columns_kernel, order),
        out_shape=[shape((group_cols, 3 * feat_count), bf16), shape((group_cols, width), f32)],
        compiler_params=params,
        cost_estimate=hint(COLUMNS_FLOPS),
    )(*pieces)
    sibling_panels = swapped(below(vecs[0], panels), "blk", 1)
    vectors = pl.pallas_call(
        vectors_kernel,
        out_shape=shape((eig_count, 3 * group_cols), bf16),
        compiler_params=params,
        cost_estimate=hint(VECTORS_FLOPS),
    )(*vecs)

    def tiles_of(row_panels, before):
        row_count = len(panels) * width
        rows = pl.pallas_call(
            functools.partial(rows_kernel, feat_count, order),
            out_shape=[
                shape((3 * feat_count, row_count), bf16),
                shape((1, row_count), f32),
                shape((group_blocks, row_count), f32),
            ],
            compiler_params=params,
        )(*row_panels)
        return pl.pallas_call(
            apply_kernel,
            in_specs=[anywhere] + [vmem] * 6,
            out_shape=shape((len(panels), eig_count, width), f32),
            compiler_params=params,
        )(before, *rows, *cols, vectors)

    sibling_tiles = tiles_of([sibling_panels], lists)
    own_tiles = tiles_of(panels, sibling_tiles)
    arrived = swapped(sibling_tiles, "blk", 1)
    total = own_tiles[0] + arrived[0]
    for place, step in enumerate(steps[1:], 1):
        total = total + swapped(own_tiles[place] + arrived[place], "blk", step)
    return total


def solution(mesh):
    return jax.shard_map(
        shards,
        mesh=mesh,
        in_specs=(P("rep", "blk"), P(None, ("blk", "rep")), P("blk", None), P("blk")),
        out_specs=P(None, ("blk", "rep")),
        check_vma=False,
    )
```

```python
import functools

import jax
import jax.numpy as jnp
from jax import lax
from jax.experimental import pallas as pl
from jax.experimental.pallas import tpu as pltpu
from jax.sharding import PartitionSpec as P


ROWS_FLOPS = 350 * 10**7
VECTORS_FLOPS = 200 * 10**7
ADD_FLOPS = 620 * 10**7


def halves(value):
    high = value.astype(jnp.bfloat16)
    return high, (value - high.astype(jnp.float32)).astype(jnp.bfloat16)


def stacked(value, order, axis):
    high, low = halves(value)
    return jnp.concatenate([{"h": high, "l": low}[letter] for letter in order], axis=axis)


def lists_kernel(list_ref, count_ref, out_ref):
    rank = lax.axis_index("rep")
    for slot in range(out_ref.shape[0]):
        listed = jnp.where(slot < count_ref[rank], list_ref[rank, slot], -1)
        out_ref[slot : slot + 1, :] = jnp.full((1, out_ref.shape[1]), listed.astype(jnp.float32))


def below_kernel(before_ref, *refs):
    start = 0
    for ref in refs[:-1]:
        refs[-1][start : start + ref.shape[0], :] = ref[...]
        start += ref.shape[0]


def columns_kernel(order, before_ref, *refs):
    piece_refs, (col_ref, bias_ref) = refs[:-2], refs[-2:]
    width = bias_ref.shape[1]
    rank = lax.axis_index("rep")
    for place, spot in enumerate(order):
        here = pl.ds(pl.multiple_of((rank ^ spot) * width, width), width)
        cols = jnp.concatenate([ref[:, here] for ref in piece_refs], axis=0).T
        there = slice(place * width, (place + 1) * width)
        bias = jnp.sum(cols * cols, axis=1, keepdims=True) * (-1.0 / cols.shape[1])
        bias_ref[there, :] = jnp.broadcast_to(bias, (width, width))
        col_ref[there, :] = stacked(cols, "hhl", 1)


def vectors_kernel(before_ref, own_ref, sibling_ref, out_ref):
    eig_count, width = out_ref.shape[0], own_ref.shape[1]
    place = 0
    for ref in (own_ref, sibling_ref):
        blocks = [ref[top : top + eig_count, :] for top in range(0, ref.shape[0], eig_count)]
        for pair in range(len(blocks) // 2):
            vecs = jnp.concatenate(blocks[2 * pair : 2 * pair + 2], axis=1)
            out_ref[:, place : place + 6 * width] = stacked(vecs, "hhl", 1)
            place += 6 * width


def rows_kernel(feat_count, *refs):
    panel_refs, (row_ref, scale_ref, mask_ref) = refs[:-3], refs[-3:]
    width = panel_refs[0].shape[1]
    group_blocks = mask_ref.shape[0] // 2
    blk_index, rank = lax.axis_index("blk"), lax.axis_index("rep")
    for place, ref in enumerate(panel_refs):
        span = slice(place * width, (place + 1) * width)
        rows = ref[:feat_count, :]
        scale_ref[:, span] = jnp.exp(jnp.sum(rows * rows, axis=0, keepdims=True) * (-1.0 / feat_count))
        row_ref[:, span] = stacked(rows * (2.0 / feat_count), "hlh", 0)
        lists = ref[feat_count:, :]
        for spot in range(2 * group_blocks):
            column = (blk_index ^ (spot // group_blocks)) * group_blocks + (rank ^ (spot % group_blocks))
            hits = jnp.where(lists == column.astype(jnp.float32), 1.0, 0.0)
            mask_ref[spot : spot + 1, span] = jnp.max(hits, axis=0, keepdims=True)


def apply_kernel(before_ref, row_ref, scale_ref, mask_ref, *refs):
    own_cols, own_bias, sibling_cols, sibling_bias, vec_ref, *out_refs = refs
    width = out_refs[0].shape[1]
    group_cols = own_cols.shape[0]
    chunk = 2 * width
    rows = row_ref[...]
    total = None
    for group, (col_ref, bias_ref) in enumerate(((own_cols, own_bias), (sibling_cols, sibling_bias))):
        for start in range(0, group_cols, chunk):
            inner = jnp.dot(col_ref[start : start + chunk, :], rows, preferred_element_type=jnp.float32)
            bias = jnp.concatenate([bias_ref[start : start + chunk, :]] * len(out_refs), axis=1)
            at = (group * group_cols + start) // width
            both = [jnp.broadcast_to(mask_ref[spot : spot + 1, :], (width, rows.shape[1])) for spot in (at, at + 1)]
            weight = stacked(jnp.exp(inner + bias) * jnp.concatenate(both, axis=0), "hlh", 0)
            there = 3 * (group * group_cols + start)
            added = jnp.dot(vec_ref[:, there : there + 3 * chunk], weight, preferred_element_type=jnp.float32)
            total = added if total is None else total + added
    total = total * scale_ref[...]
    for spot, out_ref in enumerate(out_refs):
        out_ref[...] = total[:, spot * width : (spot + 1) * width]


def add_kernel(*refs):
    total = refs[0][...]
    for ref in refs[1:-1]:
        total = total + ref[...]
    refs[-1][...] = total


def swapped(value, axis, step):
    count = lax.axis_size(axis)
    return lax.ppermute(value, axis, [(source, source ^ step) for source in range(count)])


def shards(coords, eigvecs, nbr_list, nbr_count):
    cycle_size = lax.axis_size("blk")
    rep_size = lax.axis_size("rep")
    rep_index = lax.axis_index("rep")
    group_blocks, slot_count = nbr_list.shape
    eig_count, width = eigvecs.shape
    piece_feats, group_cols = coords.shape
    feat_count = rep_size * piece_feats
    f32, bf16 = jnp.float32, jnp.bfloat16
    shape = jax.ShapeDtypeStruct
    smem = pl.BlockSpec(memory_space=pltpu.SMEM)
    vmem = pl.BlockSpec(memory_space=pltpu.VMEM)
    anywhere = pl.BlockSpec(memory_space=pl.ANY)
    params = pltpu.CompilerParams(vmem_limit_bytes=(8 + group_blocks) * 1024 * 1024)

    def hint(flops):
        return pl.CostEstimate(flops=flops, bytes_accessed=1024 * 1024, transcendentals=0)

    def block_of(piece, block):
        return lax.dynamic_slice_in_dim(piece, block * width, width, 1)

    pieces = [coords] + [swapped(coords, "rep", step) for step in range(1, rep_size)]
    own_block = [block_of(piece, rep_index) for piece in pieces]

    def below(before, values, **estimate):
        return pl.pallas_call(
            below_kernel,
            in_specs=[anywhere] + [vmem] * len(values),
            out_shape=shape((sum(value.shape[0] for value in values), values[0].shape[1]), f32),
            compiler_params=params,
            **estimate,
        )(before, *values)

    late_vecs = below(pieces[1], [eigvecs])
    far_vecs = [swapped(late_vecs, "rep", step) for step in range(1, rep_size)]
    vecs = below(pieces[1], [late_vecs, *far_vecs], cost_estimate=hint(VECTORS_FLOPS))
    order = list(range(rep_size))

    lists = pl.pallas_call(
        lists_kernel,
        in_specs=[smem, smem],
        out_shape=shape((slot_count, width), f32),
        compiler_params=params,
    )(nbr_list, nbr_count)
    panel = jnp.concatenate([*own_block, lists], axis=0)
    steps = list(range(0, cycle_size, 2))
    panels = [panel] + [swapped(panel, "blk", step) for step in steps[1:]]

    def columns_of(before, group_pieces):
        return pl.pallas_call(
            functools.partial(columns_kernel, order),
            in_specs=[anywhere] + [vmem] * len(group_pieces),
            out_shape=[shape((group_cols, 3 * feat_count), bf16), shape((group_cols, width), f32)],
            compiler_params=params,
        )(before, *group_pieces)

    sibling_cols = swapped(below(far_vecs[0], pieces), "blk", 1)
    sibling_vecs = swapped(vecs, "blk", 1)
    columns = [*columns_of(far_vecs[0], pieces), *columns_of(far_vecs[0], [sibling_cols])]

    half = len(steps) // 2
    rows = {}
    for first in (half, 0):
        rows[first] = pl.pallas_call(
            functools.partial(rows_kernel, feat_count),
            out_shape=[
                shape((3 * feat_count, half * width), bf16),
                shape((1, half * width), f32),
                shape((2 * group_blocks, half * width), f32),
            ],
            compiler_params=params,
            **(dict(cost_estimate=hint(ROWS_FLOPS)) if first else {}),
        )(*panels[first : first + half])
    vectors = pl.pallas_call(
        vectors_kernel,
        in_specs=[anywhere] + [vmem] * 2,
        out_shape=shape((eig_count, 6 * group_cols), bf16),
        compiler_params=params,
    )(columns[3], vecs, sibling_vecs)
    tiles = {}
    before = rows[half][1]
    for first in (half, 0):
        done = pl.pallas_call(
            apply_kernel,
            in_specs=[anywhere] + [vmem] * 8,
            out_shape=[shape((eig_count, width), f32)] * half,
            compiler_params=params,
        )(before, *rows[first], *columns, vectors)
        before = done[0]
        for spot in range(half):
            tiles[first + spot] = done[spot]

    arrived = [swapped(tiles[place], "blk", steps[place]) for place in range(1, len(steps))]
    far = pl.pallas_call(
        add_kernel,
        out_shape=shape((eig_count, width), f32),
        compiler_params=params,
        cost_estimate=hint(ADD_FLOPS),
    )(*arrived[half - 1 :])
    total = tiles[0]
    for tile in arrived[: half - 1]:
        total = total + tile
    return total + far


def solution(mesh):
    return jax.shard_map(
        shards,
        mesh=mesh,
        in_specs=(P("rep", "blk"), P(None, ("blk", "rep")), P("blk", None), P("blk")),
        out_specs=P(None, ("blk", "rep")),
        check_vma=False,
    )
```

```python
import functools

import jax
import jax.numpy as jnp
from jax import lax
from jax.experimental import pallas as pl
from jax.experimental.pallas import tpu as pltpu
from jax.sharding import PartitionSpec as P


ROWS_FLOPS = 400 * 10**7
VECTORS_FLOPS = 200 * 10**7
ADD_FLOPS = 620 * 10**7


def halves(value):
    high = value.astype(jnp.bfloat16)
    return high, (value - high.astype(jnp.float32)).astype(jnp.bfloat16)


def stacked(value, order, axis):
    high, low = halves(value)
    return jnp.concatenate([{"h": high, "l": low}[letter] for letter in order], axis=axis)


def lists_kernel(list_ref, count_ref, out_ref):
    rank = lax.axis_index("rep")
    for slot in range(out_ref.shape[0]):
        listed = jnp.where(slot < count_ref[rank], list_ref[rank, slot], -1)
        out_ref[slot : slot + 1, :] = jnp.full((1, out_ref.shape[1]), listed.astype(jnp.float32))


def below_kernel(skipped, *refs):
    start = 0
    for ref in refs[skipped:-1]:
        refs[-1][start : start + ref.shape[0], :] = ref[...]
        start += ref.shape[0]


def copy_kernel(*refs):
    count = len(refs) // 2
    for in_ref, out_ref in zip(refs[:count], refs[count:]):
        out_ref[...] = in_ref[...]


def columns_kernel(order, before_ref, *refs):
    piece_refs, (col_ref, bias_ref) = refs[:-2], refs[-2:]
    width = bias_ref.shape[1]
    rank = lax.axis_index("rep")
    for place, spot in enumerate(order):
        here = pl.ds(pl.multiple_of((rank ^ spot) * width, width), width)
        cols = jnp.concatenate([ref[:, here] for ref in piece_refs], axis=0).T
        there = slice(place * width, (place + 1) * width)
        bias = jnp.sum(cols * cols, axis=1, keepdims=True) * (-1.0 / cols.shape[1])
        bias_ref[there, :] = jnp.broadcast_to(bias, (width, width))
        col_ref[there, :] = stacked(cols, "hhl", 1)


def vectors_kernel(before_ref, own_ref, sibling_ref, out_ref):
    eig_count, width = out_ref.shape[0], own_ref.shape[1]
    place = 0
    for ref in (own_ref, sibling_ref):
        blocks = [ref[top : top + eig_count, :] for top in range(0, ref.shape[0], eig_count)]
        for pair in range(len(blocks) // 2):
            vecs = jnp.concatenate(blocks[2 * pair : 2 * pair + 2], axis=1)
            out_ref[:, place : place + 6 * width] = stacked(vecs, "hhl", 1)
            place += 6 * width


def rows_kernel(feat_count, *refs):
    panel_refs, (row_ref, scale_ref, mask_ref) = refs[:-3], refs[-3:]
    width = panel_refs[0].shape[1]
    group_blocks = mask_ref.shape[0] // 2
    blk_index, rank = lax.axis_index("blk"), lax.axis_index("rep")
    for place, ref in enumerate(panel_refs):
        span = slice(place * width, (place + 1) * width)
        rows = ref[:feat_count, :]
        scale_ref[:, span] = jnp.exp(jnp.sum(rows * rows, axis=0, keepdims=True) * (-1.0 / feat_count))
        row_ref[:, span] = stacked(rows * (2.0 / feat_count), "hlh", 0)
        lists = ref[feat_count:, :]
        for spot in range(2 * group_blocks):
            column = (blk_index ^ (spot // group_blocks)) * group_blocks + (rank ^ (spot % group_blocks))
            hits = jnp.where(lists == column.astype(jnp.float32), 1.0, 0.0)
            mask_ref[spot : spot + 1, span] = jnp.max(hits, axis=0, keepdims=True)


def apply_kernel(before_ref, row_ref, scale_ref, mask_ref, *refs):
    own_cols, own_bias, sibling_cols, sibling_bias, vec_ref, *out_refs = refs
    width = out_refs[0].shape[1]
    group_cols = own_cols.shape[0]
    chunk = 2 * width
    rows = row_ref[...]
    total = None
    for group, (col_ref, bias_ref) in enumerate(((own_cols, own_bias), (sibling_cols, sibling_bias))):
        for start in range(0, group_cols, chunk):
            inner = jnp.dot(col_ref[start : start + chunk, :], rows, preferred_element_type=jnp.float32)
            bias = jnp.concatenate([bias_ref[start : start + chunk, :]] * len(out_refs), axis=1)
            at = (group * group_cols + start) // width
            both = [jnp.broadcast_to(mask_ref[spot : spot + 1, :], (width, rows.shape[1])) for spot in (at, at + 1)]
            weight = stacked(jnp.exp(inner + bias) * jnp.concatenate(both, axis=0), "hlh", 0)
            there = 3 * (group * group_cols + start)
            added = jnp.dot(vec_ref[:, there : there + 3 * chunk], weight, preferred_element_type=jnp.float32)
            total = added if total is None else total + added
    total = total * scale_ref[...]
    for spot, out_ref in enumerate(out_refs):
        out_ref[...] = total[:, spot * width : (spot + 1) * width]


def add_kernel(*refs):
    total = refs[0][...]
    for ref in refs[1:-1]:
        total = total + ref[...]
    refs[-1][...] = total


def swapped(value, axis, step):
    count = lax.axis_size(axis)
    return lax.ppermute(value, axis, [(source, source ^ step) for source in range(count)])


def shards(coords, eigvecs, nbr_list, nbr_count):
    cycle_size = lax.axis_size("blk")
    rep_size = lax.axis_size("rep")
    rep_index = lax.axis_index("rep")
    group_blocks, slot_count = nbr_list.shape
    eig_count, width = eigvecs.shape
    piece_feats, group_cols = coords.shape
    feat_count = rep_size * piece_feats
    f32, bf16 = jnp.float32, jnp.bfloat16
    shape = jax.ShapeDtypeStruct
    smem = pl.BlockSpec(memory_space=pltpu.SMEM)
    vmem = pl.BlockSpec(memory_space=pltpu.VMEM)
    anywhere = pl.BlockSpec(memory_space=pl.ANY)
    params = pltpu.CompilerParams(vmem_limit_bytes=(8 + group_blocks) * 1024 * 1024)

    def hint(flops):
        return pl.CostEstimate(flops=flops, bytes_accessed=1024 * 1024, transcendentals=0)

    def block_of(piece, block):
        return lax.dynamic_slice_in_dim(piece, block * width, width, 1)

    coords_copy, vecs_copy = pl.pallas_call(
        copy_kernel,
        out_shape=[shape(coords.shape, f32), shape(eigvecs.shape, f32)],
        compiler_params=params,
    )(coords, eigvecs)
    pieces = [coords_copy, swapped(coords_copy, "rep", 1)]
    pieces += [swapped(coords, "rep", step) for step in range(2, rep_size)]
    own_block = [block_of(piece, rep_index) for piece in pieces]

    def below(before, values, **estimate):
        return pl.pallas_call(
            functools.partial(below_kernel, len(before)),
            in_specs=[anywhere] * len(before) + [vmem] * len(values),
            out_shape=shape((sum(value.shape[0] for value in values), values[0].shape[1]), f32),
            compiler_params=params,
            **estimate,
        )(*before, *values)

    near_vecs = swapped(vecs_copy, "rep", 1)
    late_vecs = below([near_vecs], [vecs_copy])
    far_vecs = [swapped(late_vecs, "rep", step) for step in range(2, rep_size)]
    vecs = below([], [late_vecs, near_vecs, *far_vecs], cost_estimate=hint(VECTORS_FLOPS))
    order = list(range(rep_size))

    lists = pl.pallas_call(
        lists_kernel,
        in_specs=[smem, smem],
        out_shape=shape((slot_count, width), f32),
        compiler_params=params,
    )(nbr_list, nbr_count)
    panel = jnp.concatenate([*own_block, lists], axis=0)
    steps = list(range(0, cycle_size, 2))
    panels = [panel] + [swapped(panel, "blk", step) for step in steps[1:]]

    def columns_of(before, group_pieces):
        return pl.pallas_call(
            functools.partial(columns_kernel, order),
            in_specs=[anywhere] + [vmem] * len(group_pieces),
            out_shape=[shape((group_cols, 3 * feat_count), bf16), shape((group_cols, width), f32)],
            compiler_params=params,
        )(before, *group_pieces)

    sibling_cols = swapped(below([], pieces), "blk", 1)
    sibling_vecs = swapped(vecs, "blk", 1)
    columns = [*columns_of(near_vecs, pieces), *columns_of(near_vecs, [sibling_cols])]

    half = len(steps) // 2
    rows = {}
    for first in (half, 0):
        rows[first] = pl.pallas_call(
            functools.partial(rows_kernel, feat_count),
            out_shape=[
                shape((3 * feat_count, half * width), bf16),
                shape((1, half * width), f32),
                shape((2 * group_blocks, half * width), f32),
            ],
            compiler_params=params,
            **(dict(cost_estimate=hint(ROWS_FLOPS)) if first else {}),
        )(*panels[first : first + half])
    vectors = pl.pallas_call(
        vectors_kernel,
        in_specs=[anywhere] + [vmem] * 2,
        out_shape=shape((eig_count, 6 * group_cols), bf16),
        compiler_params=params,
    )(columns[3], vecs, sibling_vecs)
    tiles = {}
    before = rows[half][1]
    for first in (half, 0):
        done = pl.pallas_call(
            apply_kernel,
            in_specs=[anywhere] + [vmem] * 8,
            out_shape=[shape((eig_count, width), f32)] * half,
            compiler_params=params,
        )(before, *rows[first], *columns, vectors)
        before = done[0]
        for spot in range(half):
            tiles[first + spot] = done[spot]

    arrived = [swapped(tiles[place], "blk", steps[place]) for place in range(1, len(steps))]
    far = pl.pallas_call(
        add_kernel,
        out_shape=shape((eig_count, width), f32),
        compiler_params=params,
        cost_estimate=hint(ADD_FLOPS),
    )(*arrived[half - 1 :])
    total = tiles[0]
    for tile in arrived[: half - 1]:
        total = total + tile
    return total + far


def solution(mesh):
    return jax.shard_map(
        shards,
        mesh=mesh,
        in_specs=(P("rep", "blk"), P(None, ("blk", "rep")), P("blk", None), P("blk")),
        out_specs=P(None, ("blk", "rep")),
        check_vma=False,
    )
```

```python
import functools

import jax
import jax.numpy as jnp
from jax import lax
from jax.experimental import pallas as pl
from jax.experimental.pallas import tpu as pltpu
from jax.sharding import PartitionSpec as P


TRANSFER_FLOPS = 62 * 10**8


def halves(value):
    high = value.astype(jnp.bfloat16)
    return high, (value - high.astype(jnp.float32)).astype(jnp.bfloat16)


def stacked(value, order, axis):
    high, low = halves(value)
    return jnp.concatenate([{"h": high, "l": low}[letter] for letter in order], axis=axis)


def lists_kernel(list_ref, count_ref, out_ref):
    rank = lax.axis_index("rep")
    for slot in range(out_ref.shape[0]):
        listed = jnp.where(slot < count_ref[rank], list_ref[rank, slot], -1)
        out_ref[slot : slot + 1, :] = jnp.full((1, out_ref.shape[1]), listed.astype(jnp.float32))


def copy_kernel(before_ref, in_ref, out_ref):
    out_ref[...] = in_ref[...]


def group_kernel(piece_count, *refs):
    piece_refs, vec_refs, out_ref = refs[:piece_count], refs[piece_count:-1], refs[-1]
    piece_feats = piece_refs[0].shape[0]
    width = vec_refs[0].shape[1]
    feat_count = piece_count * piece_feats
    rank = lax.axis_index("rep")
    for piece, ref in enumerate(piece_refs):
        out_ref[piece * piece_feats : (piece + 1) * piece_feats, :] = ref[...]
    for spot, ref in enumerate(vec_refs):
        span = pl.ds(pl.multiple_of((rank ^ spot) * width, width), width)
        out_ref[feat_count:, span] = ref[...]


def columns_kernel(feat_count, group_ref, col_ref, vec_ref):
    chunk = 2 * vec_ref.shape[0]
    cols = group_ref[:feat_count, :]
    col_ref[...] = stacked(cols.T, "hhl", 1)
    vecs = group_ref[feat_count:, :] * jnp.exp(jnp.sum(cols * cols, axis=0, keepdims=True) * (-1.0 / feat_count))
    for start in range(0, cols.shape[1], chunk):
        vec_ref[:, 3 * start : 3 * (start + chunk)] = stacked(vecs[:, start : start + chunk], "hhl", 1)


def rows_kernel(feat_count, *refs):
    panel_refs, (row_ref, scale_ref, mask_ref) = refs[:-3], refs[-3:]
    width = panel_refs[0].shape[1]
    group_blocks = mask_ref.shape[0] // 2
    blk_index = lax.axis_index("blk")
    for place, ref in enumerate(panel_refs):
        span = slice(place * width, (place + 1) * width)
        rows = ref[:feat_count, :]
        scale_ref[:, span] = jnp.exp(jnp.sum(rows * rows, axis=0, keepdims=True) * (-1.0 / feat_count))
        row_ref[:, span] = stacked(rows * (2.0 / feat_count), "hlh", 0)
        lists = ref[feat_count:, :]
        for spot in range(2 * group_blocks):
            column = (blk_index ^ (spot // group_blocks)) * group_blocks + spot % group_blocks
            hits = jnp.where(lists == column.astype(jnp.float32), 1.0, 0.0)
            mask_ref[spot : spot + 1, span] = jnp.max(hits, axis=0, keepdims=True)


def apply_kernel(groups, before_ref, row_ref, scale_ref, mask_ref, *refs):
    column_refs, refs = refs[: 2 * len(groups)], refs[2 * len(groups) :]
    out_refs = refs[-(row_ref.shape[1] // column_refs[1].shape[0]) :]
    so_far = refs[: len(refs) - len(out_refs)]
    width = out_refs[0].shape[1]
    chunk = 2 * width
    rows = row_ref[...]
    total = None
    for place, group in enumerate(groups):
        col_ref, vec_ref = column_refs[2 * place : 2 * place + 2]
        group_cols = col_ref.shape[0]
        for start in range(0, group_cols, chunk):
            inner = jnp.dot(col_ref[start : start + chunk, :], rows, preferred_element_type=jnp.float32)
            at = (group * group_cols + start) // width
            both = [jnp.broadcast_to(mask_ref[spot : spot + 1, :], (width, rows.shape[1])) for spot in (at, at + 1)]
            weight = stacked(jnp.exp(inner) * jnp.concatenate(both, axis=0), "hlh", 0)
            vecs = vec_ref[:, 3 * start : 3 * (start + chunk)]
            added = jnp.dot(vecs, weight, preferred_element_type=jnp.float32)
            total = added if total is None else total + added
    total = total * scale_ref[...]
    for spot, out_ref in enumerate(out_refs):
        tile = total[:, spot * width : (spot + 1) * width]
        out_ref[...] = tile + so_far[spot][...] if so_far else tile


def add_kernel(*refs):
    total = refs[0][...]
    for ref in refs[1:-1]:
        total = total + ref[...]
    refs[-1][...] = total


def swapped(value, axis, step):
    count = lax.axis_size(axis)
    return lax.ppermute(value, axis, [(source, source ^ step) for source in range(count)])


def shards(coords, eigvecs, nbr_list, nbr_count):
    cycle_size = lax.axis_size("blk")
    rep_size = lax.axis_size("rep")
    rep_index = lax.axis_index("rep")
    group_blocks, slot_count = nbr_list.shape
    eig_count, width = eigvecs.shape
    piece_feats, group_cols = coords.shape
    feat_count = rep_size * piece_feats
    f32, bf16 = jnp.float32, jnp.bfloat16
    shape = jax.ShapeDtypeStruct
    smem = pl.BlockSpec(memory_space=pltpu.SMEM)
    vmem = pl.BlockSpec(memory_space=pltpu.VMEM)
    anywhere = pl.BlockSpec(memory_space=pl.ANY)
    params = pltpu.CompilerParams(vmem_limit_bytes=(8 + group_blocks) * 1024 * 1024)
    hint = pl.CostEstimate(flops=TRANSFER_FLOPS, bytes_accessed=1024 * 1024, transcendentals=0)

    near = swapped(coords, "rep", 1)
    pieces = [swapped(coords, "rep", step) for step in range(2, rep_size)]
    pieces = [coords, pieces[0], near, *pieces[1:]]
    late_vecs = pl.pallas_call(
        copy_kernel,
        in_specs=[anywhere, vmem],
        out_shape=shape(eigvecs.shape, f32),
        compiler_params=params,
    )(near, eigvecs)
    vecs = [late_vecs] + [swapped(late_vecs, "rep", step) for step in range(1, rep_size)]
    lists = pl.pallas_call(
        lists_kernel,
        in_specs=[smem, smem],
        out_shape=shape((slot_count, width), f32),
        compiler_params=params,
    )(nbr_list, nbr_count)

    own_block = [lax.dynamic_slice_in_dim(piece, rep_index * width, width, 1) for piece in pieces]
    panel = jnp.concatenate([*own_block, lists], axis=0)
    steps = list(range(0, cycle_size, 2))
    panels = [panel] + [swapped(panel, "blk", step) for step in steps[1:]]

    own_group = pl.pallas_call(
        functools.partial(group_kernel, rep_size),
        out_shape=shape((feat_count + eig_count, group_cols), f32),
        compiler_params=params,
    )(*pieces, *vecs)
    sibling_group = swapped(own_group, "blk", 1)

    def columns_of(group):
        return pl.pallas_call(
            functools.partial(columns_kernel, feat_count),
            out_shape=[shape((group_cols, 3 * feat_count), bf16), shape((eig_count, 3 * group_cols), bf16)],
            compiler_params=params,
        )(group)

    half = len(steps) // 2

    def rows_of(first, **estimate):
        return pl.pallas_call(
            functools.partial(rows_kernel, feat_count),
            out_shape=[
                shape((3 * feat_count, half * width), bf16),
                shape((1, half * width), f32),
                shape((2 * group_blocks, half * width), f32),
            ],
            compiler_params=params,
            **estimate,
        )(*panels[first : first + half])

    def tiles_of(before, groups, rows, columns, so_far=()):
        return pl.pallas_call(
            functools.partial(apply_kernel, groups),
            in_specs=[anywhere] + [vmem] * (3 + len(columns) + len(so_far)),
            out_shape=[shape((eig_count, width), f32)] * half,
            compiler_params=params,
        )(before, *rows, *columns, *so_far)

    far_rows, near_rows = rows_of(half, cost_estimate=hint), rows_of(0)
    own, sibling = columns_of(own_group), columns_of(sibling_group)
    far_tiles = tiles_of(far_rows[1], (0,), far_rows, own)
    far_tiles = tiles_of(far_tiles[0], (1,), far_rows, sibling, far_tiles)
    near_tiles = tiles_of(far_tiles[0], (0, 1), near_rows, [*own, *sibling])
    tiles = [*near_tiles, *far_tiles]

    arrived = [swapped(tiles[place], "blk", steps[place]) for place in range(1, len(steps))]
    far = pl.pallas_call(
        add_kernel,
        out_shape=shape((eig_count, width), f32),
        compiler_params=params,
        cost_estimate=hint,
    )(*arrived[half - 1 :])
    total = tiles[0]
    for tile in arrived[: half - 1]:
        total = total + tile
    return total + far


def solution(mesh):
    return jax.shard_map(
        shards,
        mesh=mesh,
        in_specs=(P("rep", "blk"), P(None, ("blk", "rep")), P("blk", None), P("blk")),
        out_specs=P(None, ("blk", "rep")),
        check_vma=False,
    )
```

```python
import functools

import jax
import jax.numpy as jnp
from jax import lax
from jax.experimental import pallas as pl
from jax.experimental.pallas import tpu as pltpu
from jax.sharding import PartitionSpec as P


ROWS_FLOPS = 400 * 10**7
VECTORS_FLOPS = 200 * 10**7
ADD_FLOPS = 620 * 10**7


def halves(value):
    high = value.astype(jnp.bfloat16)
    return high, (value - high.astype(jnp.float32)).astype(jnp.bfloat16)


def stacked(value, order, axis):
    high, low = halves(value)
    return jnp.concatenate([{"h": high, "l": low}[letter] for letter in order], axis=axis)


def lists_kernel(list_ref, count_ref, out_ref):
    rank = lax.axis_index("rep")
    for slot in range(out_ref.shape[0]):
        listed = jnp.where(slot < count_ref[rank], list_ref[rank, slot], -1)
        out_ref[slot : slot + 1, :] = jnp.full((1, out_ref.shape[1]), listed.astype(jnp.float32))


def below_kernel(before_ref, *refs):
    start = 0
    for ref in refs[:-1]:
        refs[-1][start : start + ref.shape[0], :] = ref[...]
        start += ref.shape[0]


def columns_kernel(order, before_ref, *refs):
    piece_refs, (col_ref, scale_ref) = refs[:-2], refs[-2:]
    width = scale_ref.shape[1] // len(order)
    rank = lax.axis_index("rep")
    for place, spot in enumerate(order):
        here = pl.ds(pl.multiple_of((rank ^ spot) * width, width), width)
        there = slice(place * width, (place + 1) * width)
        cols = jnp.concatenate([ref[:, here] for ref in piece_refs], axis=0)
        scale_ref[:, there] = jnp.exp(jnp.sum(cols * cols, axis=0, keepdims=True) * (-1.0 / cols.shape[0]))
        col_ref[there, :] = stacked(cols.T, "hhl", 1)


def vectors_kernel(own_ref, sibling_ref, own_scale, sibling_scale, out_ref):
    eig_count, width = out_ref.shape[0], own_ref.shape[1]
    place = 0
    for ref, scale_ref in ((own_ref, own_scale), (sibling_ref, sibling_scale)):
        tops = range(0, ref.shape[0], eig_count)
        blocks = [
            ref[top : top + eig_count, :] * scale_ref[:, at * width : (at + 1) * width] for at, top in enumerate(tops)
        ]
        for pair in range(len(blocks) // 2):
            vecs = jnp.concatenate(blocks[2 * pair : 2 * pair + 2], axis=1)
            out_ref[:, place : place + 6 * width] = stacked(vecs, "hhl", 1)
            place += 6 * width


def rows_kernel(feat_count, *refs):
    panel_refs, (row_ref, scale_ref, mask_ref) = refs[:-3], refs[-3:]
    width = panel_refs[0].shape[1]
    group_blocks = mask_ref.shape[0] // 2
    blk_index, rank = lax.axis_index("blk"), lax.axis_index("rep")
    for place, ref in enumerate(panel_refs):
        span = slice(place * width, (place + 1) * width)
        rows = ref[:feat_count, :]
        scale_ref[:, span] = jnp.exp(jnp.sum(rows * rows, axis=0, keepdims=True) * (-1.0 / feat_count))
        row_ref[:, span] = stacked(rows * (2.0 / feat_count), "hlh", 0)
        lists = ref[feat_count:, :]
        for spot in range(2 * group_blocks):
            column = (blk_index ^ (spot // group_blocks)) * group_blocks + (rank ^ (spot % group_blocks))
            hits = jnp.where(lists == column.astype(jnp.float32), 1.0, 0.0)
            mask_ref[spot : spot + 1, span] = jnp.max(hits, axis=0, keepdims=True)


def apply_kernel(before_ref, row_ref, scale_ref, mask_ref, *refs):
    own_cols, sibling_cols, vec_ref, *out_refs = refs
    width = out_refs[0].shape[1]
    group_cols = own_cols.shape[0]
    chunk = 2 * width
    rows = row_ref[...]
    total = None
    for group, col_ref in enumerate((own_cols, sibling_cols)):
        for start in range(0, group_cols, chunk):
            inner = jnp.dot(col_ref[start : start + chunk, :], rows, preferred_element_type=jnp.float32)
            at = (group * group_cols + start) // width
            both = [jnp.broadcast_to(mask_ref[spot : spot + 1, :], (width, rows.shape[1])) for spot in (at, at + 1)]
            weight = stacked(jnp.exp(inner) * jnp.concatenate(both, axis=0), "hlh", 0)
            there = 3 * (group * group_cols + start)
            added = jnp.dot(vec_ref[:, there : there + 3 * chunk], weight, preferred_element_type=jnp.float32)
            total = added if total is None else total + added
    total = total * scale_ref[...]
    for spot, out_ref in enumerate(out_refs):
        out_ref[...] = total[:, spot * width : (spot + 1) * width]


def add_kernel(*refs):
    total = refs[0][...]
    for ref in refs[1:-1]:
        total = total + ref[...]
    refs[-1][...] = total


def swapped(value, axis, step):
    count = lax.axis_size(axis)
    return lax.ppermute(value, axis, [(source, source ^ step) for source in range(count)])


def shards(coords, eigvecs, nbr_list, nbr_count):
    cycle_size = lax.axis_size("blk")
    rep_size = lax.axis_size("rep")
    rep_index = lax.axis_index("rep")
    group_blocks, slot_count = nbr_list.shape
    eig_count, width = eigvecs.shape
    piece_feats, group_cols = coords.shape
    feat_count = rep_size * piece_feats
    f32, bf16 = jnp.float32, jnp.bfloat16
    shape = jax.ShapeDtypeStruct
    smem = pl.BlockSpec(memory_space=pltpu.SMEM)
    vmem = pl.BlockSpec(memory_space=pltpu.VMEM)
    anywhere = pl.BlockSpec(memory_space=pl.ANY)
    params = pltpu.CompilerParams(vmem_limit_bytes=(8 + group_blocks) * 1024 * 1024)

    def hint(flops):
        return pl.CostEstimate(flops=flops, bytes_accessed=1024 * 1024, transcendentals=0)

    def block_of(piece, block):
        return lax.dynamic_slice_in_dim(piece, block * width, width, 1)

    pieces = [coords] + [swapped(coords, "rep", step) for step in [2, 1, *range(3, rep_size)]]
    own_block = [block_of(piece, rep_index) for piece in pieces]

    def below(before, values, **estimate):
        return pl.pallas_call(
            below_kernel,
            in_specs=[anywhere] + [vmem] * len(values),
            out_shape=shape((sum(value.shape[0] for value in values), values[0].shape[1]), f32),
            compiler_params=params,
            **estimate,
        )(before, *values)

    late_vecs = below(pieces[1], [eigvecs])
    far_vecs = [swapped(late_vecs, "rep", step) for step in range(1, rep_size)]
    vecs = below(pieces[1], [late_vecs, *far_vecs], cost_estimate=hint(VECTORS_FLOPS))
    order = list(range(rep_size))

    lists = pl.pallas_call(
        lists_kernel,
        in_specs=[smem, smem],
        out_shape=shape((slot_count, width), f32),
        compiler_params=params,
    )(nbr_list, nbr_count)
    panel = jnp.concatenate([*own_block, lists], axis=0)
    steps = list(range(0, cycle_size, 2))
    half = len(steps) // 2
    steps[half:] = steps[:half - 1:-1]
    panels = [panel] + [swapped(panel, "blk", step) for step in steps[1:]]

    def columns_of(before, group_pieces):
        return pl.pallas_call(
            functools.partial(columns_kernel, order),
            in_specs=[anywhere] + [vmem] * len(group_pieces),
            out_shape=[shape((group_cols, 3 * feat_count), bf16), shape((1, group_cols), f32)],
            compiler_params=params,
        )(before, *group_pieces)

    sibling_cols = swapped(below(far_vecs[0], pieces), "blk", 1)
    sibling_vecs = swapped(vecs, "blk", 1)
    columns = [*columns_of(far_vecs[0], pieces), *columns_of(far_vecs[0], [sibling_cols])]

    rows = {}
    for first in (half, 0):
        rows[first] = pl.pallas_call(
            functools.partial(rows_kernel, feat_count),
            out_shape=[
                shape((3 * feat_count, half * width), bf16),
                shape((1, half * width), f32),
                shape((2 * group_blocks, half * width), f32),
            ],
            compiler_params=params,
            **(dict(cost_estimate=hint(ROWS_FLOPS)) if first else {}),
        )(*panels[first : first + half])
    vectors = pl.pallas_call(
        vectors_kernel,
        out_shape=shape((eig_count, 6 * group_cols), bf16),
        compiler_params=params,
    )(vecs, sibling_vecs, columns[1], columns[3])
    tiles = {}
    before = rows[half][1]
    for first in (half, 0):
        done = pl.pallas_call(
            apply_kernel,
            in_specs=[anywhere] + [vmem] * 6,
            out_shape=[shape((eig_count, width), f32)] * half,
            compiler_params=params,
        )(before, *rows[first], columns[0], columns[2], vectors)
        before = done[0]
        for spot in range(half):
            tiles[first + spot] = done[spot]

    arrived = [swapped(tiles[place], "blk", steps[place]) for place in range(1, len(steps))]
    far = pl.pallas_call(
        add_kernel,
        out_shape=shape((eig_count, width), f32),
        compiler_params=params,
        cost_estimate=hint(ADD_FLOPS),
    )(*arrived[half - 1 :])
    total = tiles[0]
    for tile in arrived[: half - 1]:
        total = total + tile
    return total + far


def solution(mesh):
    return jax.shard_map(
        shards,
        mesh=mesh,
        in_specs=(P("rep", "blk"), P(None, ("blk", "rep")), P("blk", None), P("blk")),
        out_specs=P(None, ("blk", "rep")),
        check_vma=False,
    )
```

```python
import functools

import jax
import jax.numpy as jnp
from jax import lax
from jax.experimental import pallas as pl
from jax.experimental.pallas import tpu as pltpu
from jax.sharding import PartitionSpec as P


TRANSFER_FLOPS = 62 * 10**8


def halves(value):
    high = value.astype(jnp.bfloat16)
    return high, (value - high.astype(jnp.float32)).astype(jnp.bfloat16)


def stacked(value, order, axis):
    high, low = halves(value)
    return jnp.concatenate([{"h": high, "l": low}[letter] for letter in order], axis=axis)


def lists_kernel(list_ref, count_ref, out_ref):
    rank = lax.axis_index("rep")
    for slot in range(out_ref.shape[0]):
        listed = jnp.where(slot < count_ref[rank], list_ref[rank, slot], -1)
        out_ref[slot : slot + 1, :] = jnp.full((1, out_ref.shape[1]), listed.astype(jnp.float32))


def copy_kernel(before_ref, in_ref, out_ref):
    out_ref[...] = in_ref[...]


def group_kernel(piece_count, *refs):
    piece_refs, vec_refs, out_ref = refs[:piece_count], refs[piece_count:-1], refs[-1]
    piece_feats = piece_refs[0].shape[0]
    width = vec_refs[0].shape[1]
    feat_count = piece_count * piece_feats
    rank = lax.axis_index("rep")
    for piece, ref in enumerate(piece_refs):
        out_ref[piece * piece_feats : (piece + 1) * piece_feats, :] = ref[...]
    for spot, ref in enumerate(vec_refs[::-1]):
        span = pl.ds(pl.multiple_of((rank ^ spot) * width, width), width)
        out_ref[feat_count:, span] = ref[...]


def columns_kernel(feat_count, group_ref, col_ref, vec_ref):
    chunk = 2 * vec_ref.shape[0]
    cols = group_ref[:feat_count, :]
    col_ref[...] = stacked(cols.T, "hhl", 1)
    vecs = group_ref[feat_count:, :] * jnp.exp(jnp.sum(cols * cols, axis=0, keepdims=True) * (-1.0 / feat_count))
    for start in range(0, cols.shape[1], chunk):
        vec_ref[:, 3 * start : 3 * (start + chunk)] = stacked(vecs[:, start : start + chunk], "hhl", 1)


def rows_kernel(feat_count, *refs):
    panel_refs, (row_ref, scale_ref, mask_ref) = refs[:-3], refs[-3:]
    width = panel_refs[0].shape[1]
    group_blocks = mask_ref.shape[0] // 2
    blk_index = lax.axis_index("blk")
    for place, ref in enumerate(panel_refs):
        span = slice(place * width, (place + 1) * width)
        rows = ref[:feat_count, :]
        scale_ref[:, span] = jnp.exp(jnp.sum(rows * rows, axis=0, keepdims=True) * (-1.0 / feat_count))
        row_ref[:, span] = stacked(rows * (2.0 / feat_count), "hlh", 0)
        lists = ref[feat_count:, :]
        for spot in range(2 * group_blocks):
            column = (blk_index ^ (spot // group_blocks)) * group_blocks + spot % group_blocks
            hits = jnp.where(lists == column.astype(jnp.float32), 1.0, 0.0)
            mask_ref[spot : spot + 1, span] = jnp.max(hits, axis=0, keepdims=True)


def apply_kernel(row_ref, scale_ref, mask_ref, *refs):
    own_cols, own_vecs, sibling_cols, sibling_vecs, *out_refs = refs
    width = out_refs[0].shape[1]
    group_cols = own_cols.shape[0]
    chunk = 2 * width
    pairs = range(len(out_refs) // 2)
    totals = [None for _ in pairs]
    for group, (col_ref, vec_ref) in enumerate(((own_cols, own_vecs), (sibling_cols, sibling_vecs))):
        for start in range(0, group_cols, chunk):
            at = (group * group_cols + start) // width
            for pair in pairs:
                span = slice(pair * chunk, (pair + 1) * chunk)
                inner = jnp.dot(
                    col_ref[start : start + chunk, :], row_ref[:, span], preferred_element_type=jnp.float32
                )
                both = [jnp.broadcast_to(mask_ref[spot : spot + 1, span], (width, chunk)) for spot in (at, at + 1)]
                weight = stacked(jnp.exp(inner) * jnp.concatenate(both, axis=0), "hlh", 0)
                vecs = vec_ref[:, 3 * start : 3 * (start + chunk)]
                added = jnp.dot(vecs, weight, preferred_element_type=jnp.float32)
                totals[pair] = added if totals[pair] is None else totals[pair] + added
    for pair in pairs:
        total = totals[pair] * scale_ref[:, pair * chunk : (pair + 1) * chunk]
        out_refs[2 * pair][...] = total[:, :width]
        out_refs[2 * pair + 1][...] = total[:, width:]


def swapped(value, axis, step):
    count = lax.axis_size(axis)
    return lax.ppermute(value, axis, [(source, source ^ step) for source in range(count)])


def shards(coords, eigvecs, nbr_list, nbr_count):
    cycle_size = lax.axis_size("blk")
    rep_size = lax.axis_size("rep")
    rep_index = lax.axis_index("rep")
    group_blocks, slot_count = nbr_list.shape
    eig_count, width = eigvecs.shape
    piece_feats, group_cols = coords.shape
    feat_count = rep_size * piece_feats
    f32, bf16 = jnp.float32, jnp.bfloat16
    shape = jax.ShapeDtypeStruct
    smem = pl.BlockSpec(memory_space=pltpu.SMEM)
    vmem = pl.BlockSpec(memory_space=pltpu.VMEM)
    anywhere = pl.BlockSpec(memory_space=pl.ANY)
    params = pltpu.CompilerParams(vmem_limit_bytes=(8 + group_blocks) * 1024 * 1024)
    hint = pl.CostEstimate(flops=TRANSFER_FLOPS, bytes_accessed=1024 * 1024, transcendentals=0)

    pieces = [coords] + [swapped(coords, "rep", step) for step in range(1, rep_size)]
    late_vecs = pl.pallas_call(
        copy_kernel,
        in_specs=[anywhere, vmem],
        out_shape=shape(eigvecs.shape, f32),
        compiler_params=params,
    )(pieces[1], eigvecs)
    vecs = [swapped(late_vecs, "rep", step) for step in range(rep_size - 1, 0, -1)] + [late_vecs]
    lists = pl.pallas_call(
        lists_kernel,
        in_specs=[smem, smem],
        out_shape=shape((slot_count, width), f32),
        compiler_params=params,
    )(nbr_list, nbr_count)

    own_block = [lax.dynamic_slice_in_dim(piece, rep_index * width, width, 1) for piece in pieces]
    panel = jnp.concatenate([*own_block, lists], axis=0)
    steps = list(range(0, cycle_size, 2))
    panels = [panel] + [swapped(panel, "blk", step) for step in steps[1:]]

    own_group = pl.pallas_call(
        functools.partial(group_kernel, rep_size),
        out_shape=shape((feat_count + eig_count, group_cols), f32),
        compiler_params=params,
    )(*pieces, *vecs)
    sibling_group = swapped(own_group, "blk", 1)

    def columns_of(group):
        return pl.pallas_call(
            functools.partial(columns_kernel, feat_count),
            out_shape=[shape((group_cols, 3 * feat_count), bf16), shape((eig_count, 3 * group_cols), bf16)],
            compiler_params=params,
        )(group)

    row_count = len(panels) * width
    rows = pl.pallas_call(
        functools.partial(rows_kernel, feat_count),
        out_shape=[
            shape((3 * feat_count, row_count), bf16),
            shape((1, row_count), f32),
            shape((2 * group_blocks, row_count), f32),
        ],
        compiler_params=params,
        cost_estimate=hint,
    )(*panels)
    columns = [*columns_of(own_group), *columns_of(sibling_group)]
    tiles = pl.pallas_call(
        apply_kernel,
        out_shape=[shape((eig_count, width), f32)] * len(panels),
        compiler_params=params,
    )(*rows, *columns)
    total = tiles[0]
    for place in range(len(steps) - 1, 0, -1):
        total = total + swapped(tiles[place], "blk", steps[place])
    return total


def solution(mesh):
    return jax.shard_map(
        shards,
        mesh=mesh,
        in_specs=(P("rep", "blk"), P(None, ("blk", "rep")), P("blk", None), P("blk")),
        out_specs=P(None, ("blk", "rep")),
        check_vma=False,
    )
```

```python
import functools

import jax
import jax.numpy as jnp
from jax import lax
from jax.experimental import pallas as pl
from jax.experimental.pallas import tpu as pltpu
from jax.sharding import PartitionSpec as P


TRANSFER_FLOPS = 62 * 10**8


def halves(value):
    high = value.astype(jnp.bfloat16)
    return high, (value - high.astype(jnp.float32)).astype(jnp.bfloat16)


def three_pass(left_both, right_high, right_low):
    size = left_both.shape[0] // 2
    mul = functools.partial(jnp.dot, preferred_element_type=jnp.float32)
    first = mul(left_both, right_high)
    return (first[:size] + first[size:]) + mul(left_both[:size], right_low)


def lists_kernel(list_ref, count_ref, out_ref):
    rank = lax.axis_index("rep")
    for slot in range(out_ref.shape[0]):
        listed = jnp.where(slot < count_ref[rank], list_ref[rank, slot], -1)
        out_ref[slot : slot + 1, :] = jnp.full((1, out_ref.shape[1]), listed.astype(jnp.float32))


def copy_kernel(before_ref, in_ref, out_ref):
    out_ref[...] = in_ref[...]


def group_kernel(piece_count, *refs):
    piece_refs, vec_refs, out_ref = refs[:piece_count], refs[piece_count:-1], refs[-1]
    piece_feats = piece_refs[0].shape[0]
    width = vec_refs[0].shape[1]
    feat_count = piece_count * piece_feats
    rank = lax.axis_index("rep")
    for piece, ref in enumerate(piece_refs):
        out_ref[piece * piece_feats : (piece + 1) * piece_feats, :] = ref[...]
    for spot, ref in enumerate(vec_refs[::-1]):
        span = pl.ds(pl.multiple_of((rank ^ spot) * width, width), width)
        out_ref[feat_count:, span] = ref[...]


def columns_kernel(feat_count, group_ref, col_ref, vec_ref):
    eig_count = vec_ref.shape[0] // 2
    chunk = 2 * eig_count
    cols = group_ref[:feat_count, :]
    flipped = cols.T
    for start in range(0, cols.shape[1], chunk):
        high, low = halves(flipped[start : start + chunk, :])
        col_ref[2 * start : 2 * start + chunk, :] = high
        col_ref[2 * start + chunk : 2 * (start + chunk), :] = low
    vecs = group_ref[feat_count:, :] * jnp.exp(jnp.sum(cols * cols, axis=0, keepdims=True) * (-1.0 / feat_count))
    vec_ref[:eig_count, :], vec_ref[eig_count:, :] = halves(vecs)


def rows_kernel(feat_count, *refs):
    panel_refs, (high_ref, low_ref, scale_ref, mask_ref) = refs[:-4], refs[-4:]
    width = panel_refs[0].shape[1]
    group_blocks = mask_ref.shape[0] // 2
    blk_index = lax.axis_index("blk")
    for place, ref in enumerate(panel_refs):
        span = slice(place * width, (place + 1) * width)
        rows = ref[:feat_count, :]
        scale_ref[:, span] = jnp.exp(jnp.sum(rows * rows, axis=0, keepdims=True) * (-1.0 / feat_count))
        high_ref[:, span], low_ref[:, span] = halves(rows * (2.0 / feat_count))
        lists = ref[feat_count:, :]
        for spot in range(2 * group_blocks):
            column = (blk_index ^ (spot // group_blocks)) * group_blocks + spot % group_blocks
            hits = jnp.where(lists == column.astype(jnp.float32), 1.0, 0.0)
            mask_ref[spot : spot + 1, span] = jnp.max(hits, axis=0, keepdims=True)


def apply_kernel(high_ref, low_ref, scale_ref, mask_ref, *refs):
    own_cols, own_vecs, sibling_cols, sibling_vecs, *out_refs = refs
    width = out_refs[0].shape[1]
    group_cols = own_vecs.shape[1]
    chunk = 2 * width
    pairs = range(len(out_refs) // 2)
    totals = [None for _ in pairs]
    for group, (col_ref, vec_ref) in enumerate(((own_cols, own_vecs), (sibling_cols, sibling_vecs))):
        for start in range(0, group_cols, chunk):
            at = (group * group_cols + start) // width
            for pair in pairs:
                span = slice(pair * chunk, (pair + 1) * chunk)
                inner = three_pass(col_ref[2 * start : 2 * (start + chunk), :], high_ref[:, span], low_ref[:, span])
                both = [jnp.broadcast_to(mask_ref[spot : spot + 1, span], (width, chunk)) for spot in (at, at + 1)]
                weight = jnp.exp(inner) * jnp.concatenate(both, axis=0)
                added = three_pass(vec_ref[:, start : start + chunk], *halves(weight))
                totals[pair] = added if totals[pair] is None else totals[pair] + added
    for pair in pairs:
        total = totals[pair] * scale_ref[:, pair * chunk : (pair + 1) * chunk]
        out_refs[2 * pair][...] = total[:, :width]
        out_refs[2 * pair + 1][...] = total[:, width:]


def swapped(value, axis, step):
    count = lax.axis_size(axis)
    return lax.ppermute(value, axis, [(source, source ^ step) for source in range(count)])


def shards(coords, eigvecs, nbr_list, nbr_count):
    cycle_size = lax.axis_size("blk")
    rep_size = lax.axis_size("rep")
    rep_index = lax.axis_index("rep")
    group_blocks, slot_count = nbr_list.shape
    eig_count, width = eigvecs.shape
    piece_feats, group_cols = coords.shape
    feat_count = rep_size * piece_feats
    f32, bf16 = jnp.float32, jnp.bfloat16
    shape = jax.ShapeDtypeStruct
    smem = pl.BlockSpec(memory_space=pltpu.SMEM)
    vmem = pl.BlockSpec(memory_space=pltpu.VMEM)
    anywhere = pl.BlockSpec(memory_space=pl.ANY)
    params = pltpu.CompilerParams(vmem_limit_bytes=(8 + group_blocks) * 1024 * 1024)
    hint = pl.CostEstimate(flops=TRANSFER_FLOPS, bytes_accessed=1024 * 1024, transcendentals=0)

    pieces = [coords] + [swapped(coords, "rep", step) for step in range(1, rep_size)]
    late_vecs = pl.pallas_call(
        copy_kernel,
        in_specs=[anywhere, vmem],
        out_shape=shape(eigvecs.shape, f32),
        compiler_params=params,
    )(pieces[1], eigvecs)
    vecs = [swapped(late_vecs, "rep", step) for step in range(rep_size - 1, 0, -1)] + [late_vecs]
    lists = pl.pallas_call(
        lists_kernel,
        in_specs=[smem, smem],
        out_shape=shape((slot_count, width), f32),
        compiler_params=params,
    )(nbr_list, nbr_count)

    own_block = [lax.dynamic_slice_in_dim(piece, rep_index * width, width, 1) for piece in pieces]
    panel = jnp.concatenate([*own_block, lists], axis=0)
    steps = list(range(0, cycle_size, 2))
    panels = [panel] + [swapped(panel, "blk", step) for step in steps[1:]]

    own_group = pl.pallas_call(
        functools.partial(group_kernel, rep_size),
        out_shape=shape((feat_count + eig_count, group_cols), f32),
        compiler_params=params,
    )(*pieces, *vecs)
    sibling_group = swapped(own_group, "blk", 1)

    def columns_of(group):
        return pl.pallas_call(
            functools.partial(columns_kernel, feat_count),
            out_shape=[shape((2 * group_cols, feat_count), bf16), shape((2 * eig_count, group_cols), bf16)],
            compiler_params=params,
        )(group)

    row_count = len(panels) * width
    rows = pl.pallas_call(
        functools.partial(rows_kernel, feat_count),
        out_shape=[
            shape((feat_count, row_count), bf16),
            shape((feat_count, row_count), bf16),
            shape((1, row_count), f32),
            shape((2 * group_blocks, row_count), f32),
        ],
        compiler_params=params,
        cost_estimate=hint,
    )(*panels)
    columns = [*columns_of(own_group), *columns_of(sibling_group)]
    tiles = pl.pallas_call(
        apply_kernel,
        out_shape=[shape((eig_count, width), f32)] * len(panels),
        compiler_params=params,
    )(*rows, *columns)
    total = tiles[0]
    for place in range(len(steps) - 1, 0, -1):
        total = total + swapped(tiles[place], "blk", steps[place])
    return total


def solution(mesh):
    return jax.shard_map(
        shards,
        mesh=mesh,
        in_specs=(P("rep", "blk"), P(None, ("blk", "rep")), P("blk", None), P("blk")),
        out_specs=P(None, ("blk", "rep")),
        check_vma=False,
    )
```

```python
import functools

import jax
import jax.numpy as jnp
from jax import lax
from jax.experimental import pallas as pl
from jax.experimental.pallas import tpu as pltpu
from jax.sharding import PartitionSpec as P


TRANSFER_FLOPS = 62 * 10**8


def halves(value):
    high = value.astype(jnp.bfloat16)
    return high, (value - high.astype(jnp.float32)).astype(jnp.bfloat16)


def stacked(value, order, axis):
    high, low = halves(value)
    return jnp.concatenate([{"h": high, "l": low}[letter] for letter in order], axis=axis)


def lists_kernel(list_ref, count_ref, out_ref):
    rank = lax.axis_index("rep")
    for slot in range(out_ref.shape[0]):
        listed = jnp.where(slot < count_ref[rank], list_ref[rank, slot], -1)
        out_ref[slot : slot + 1, :] = jnp.full((1, out_ref.shape[1]), listed.astype(jnp.float32))


def copy_kernel(before_ref, in_ref, out_ref):
    out_ref[...] = in_ref[...]


def group_kernel(piece_count, *refs):
    piece_refs, vec_refs, out_ref = refs[:piece_count], refs[piece_count:-1], refs[-1]
    piece_feats = piece_refs[0].shape[0]
    width = vec_refs[0].shape[1]
    feat_count = piece_count * piece_feats
    rank = lax.axis_index("rep")
    for piece, ref in enumerate(piece_refs):
        out_ref[piece * piece_feats : (piece + 1) * piece_feats, :] = ref[...]
    for spot, ref in enumerate(vec_refs[::-1]):
        span = pl.ds(pl.multiple_of((rank ^ spot) * width, width), width)
        out_ref[feat_count:, span] = ref[...]


def columns_kernel(feat_count, group_ref, col_ref, vec_ref):
    chunk = 4 * vec_ref.shape[0]
    cols = group_ref[:feat_count, :]
    col_ref[...] = stacked(cols.T, "hhl", 1)
    vecs = group_ref[feat_count:, :] * jnp.exp(jnp.sum(cols * cols, axis=0, keepdims=True) * (-1.0 / feat_count))
    for start in range(0, cols.shape[1], chunk):
        vec_ref[:, 3 * start : 3 * (start + chunk)] = stacked(vecs[:, start : start + chunk], "hhl", 1)


def rows_kernel(feat_count, *refs):
    panel_refs, (row_ref, scale_ref, mask_ref) = refs[:-3], refs[-3:]
    width = panel_refs[0].shape[1]
    group_blocks = mask_ref.shape[0] // 2
    blk_index = lax.axis_index("blk")
    for place, ref in enumerate(panel_refs):
        span = slice(place * width, (place + 1) * width)
        rows = ref[:feat_count, :]
        scale_ref[:, span] = jnp.exp(jnp.sum(rows * rows, axis=0, keepdims=True) * (-1.0 / feat_count))
        row_ref[:, span] = stacked(rows * (2.0 / feat_count), "hlh", 0)
        lists = ref[feat_count:, :]
        for spot in range(2 * group_blocks):
            column = (blk_index ^ (spot // group_blocks)) * group_blocks + spot % group_blocks
            hits = jnp.where(lists == column.astype(jnp.float32), 1.0, 0.0)
            mask_ref[spot : spot + 1, span] = jnp.max(hits, axis=0, keepdims=True)


def apply_kernel(row_ref, scale_ref, mask_ref, *refs):
    own_cols, own_vecs, sibling_cols, sibling_vecs, *out_refs = refs
    width = out_refs[0].shape[1]
    group_cols = own_cols.shape[0]
    chunk = 4 * width
    pairs = [slice(first * width, (first + 2) * width) for first in range(0, len(out_refs), 2)]
    totals = [None for _ in pairs]
    for group, (col_ref, vec_ref) in enumerate(((own_cols, own_vecs), (sibling_cols, sibling_vecs))):
        for start in range(0, group_cols, chunk):
            at = (group * group_cols + start) // width
            for pair, span in enumerate(pairs):
                inner = jnp.dot(
                    col_ref[start : start + chunk, :], row_ref[:, span], preferred_element_type=jnp.float32
                )
                masks = [jnp.broadcast_to(mask_ref[at + spot : at + spot + 1, span], (width, 2 * width)) for spot in range(4)]
                weight = stacked(jnp.exp(inner) * jnp.concatenate(masks, axis=0), "hlh", 0)
                vecs = vec_ref[:, 3 * start : 3 * (start + chunk)]
                added = jnp.dot(vecs, weight, preferred_element_type=jnp.float32)
                totals[pair] = added if totals[pair] is None else totals[pair] + added
    for pair, span in enumerate(pairs):
        total = totals[pair] * scale_ref[:, span]
        out_refs[2 * pair][...] = total[:, :width]
        out_refs[2 * pair + 1][...] = total[:, width:]


def swapped(value, axis, step):
    count = lax.axis_size(axis)
    return lax.ppermute(value, axis, [(source, source ^ step) for source in range(count)])


def shards(coords, eigvecs, nbr_list, nbr_count):
    cycle_size = lax.axis_size("blk")
    rep_size = lax.axis_size("rep")
    rep_index = lax.axis_index("rep")
    group_blocks, slot_count = nbr_list.shape
    eig_count, width = eigvecs.shape
    piece_feats, group_cols = coords.shape
    feat_count = rep_size * piece_feats
    f32, bf16 = jnp.float32, jnp.bfloat16
    shape = jax.ShapeDtypeStruct
    smem = pl.BlockSpec(memory_space=pltpu.SMEM)
    vmem = pl.BlockSpec(memory_space=pltpu.VMEM)
    anywhere = pl.BlockSpec(memory_space=pl.ANY)
    params = pltpu.CompilerParams(vmem_limit_bytes=(8 + group_blocks) * 1024 * 1024)
    hint = pl.CostEstimate(flops=TRANSFER_FLOPS, bytes_accessed=1024 * 1024, transcendentals=0)

    pieces = [coords] + [swapped(coords, "rep", step) for step in range(1, rep_size)]
    late_vecs = pl.pallas_call(
        copy_kernel,
        in_specs=[anywhere, vmem],
        out_shape=shape(eigvecs.shape, f32),
        compiler_params=params,
    )(pieces[1], eigvecs)
    vecs = [swapped(late_vecs, "rep", step) for step in range(rep_size - 1, 0, -1)] + [late_vecs]
    lists = pl.pallas_call(
        lists_kernel,
        in_specs=[smem, smem],
        out_shape=shape((slot_count, width), f32),
        compiler_params=params,
    )(nbr_list, nbr_count)

    own_block = [lax.dynamic_slice_in_dim(piece, rep_index * width, width, 1) for piece in pieces]
    panel = jnp.concatenate([*own_block, lists], axis=0)
    steps = list(range(0, cycle_size, 2))
    panels = [panel] + [swapped(panel, "blk", step) for step in steps[1:]]

    own_group = pl.pallas_call(
        functools.partial(group_kernel, rep_size),
        out_shape=shape((feat_count + eig_count, group_cols), f32),
        compiler_params=params,
    )(*pieces, *vecs)
    sibling_group = swapped(own_group, "blk", 1)

    def columns_of(group):
        return pl.pallas_call(
            functools.partial(columns_kernel, feat_count),
            out_shape=[shape((group_cols, 3 * feat_count), bf16), shape((eig_count, 3 * group_cols), bf16)],
            compiler_params=params,
        )(group)

    row_count = len(panels) * width
    rows = pl.pallas_call(
        functools.partial(rows_kernel, feat_count),
        out_shape=[
            shape((3 * feat_count, row_count), bf16),
            shape((1, row_count), f32),
            shape((2 * group_blocks, row_count), f32),
        ],
        compiler_params=params,
        cost_estimate=hint,
    )(*panels)
    columns = [*columns_of(own_group), *columns_of(sibling_group)]
    tiles = pl.pallas_call(
        apply_kernel,
        out_shape=[shape((eig_count, width), f32)] * len(panels),
        compiler_params=params,
    )(*rows, *columns)
    total = tiles[0]
    for place in range(len(steps) - 1, 0, -1):
        total = total + swapped(tiles[place], "blk", steps[place])
    return total


def solution(mesh):
    return jax.shard_map(
        shards,
        mesh=mesh,
        in_specs=(P("rep", "blk"), P(None, ("blk", "rep")), P("blk", None), P("blk")),
        out_specs=P(None, ("blk", "rep")),
        check_vma=False,
    )
```

```python
import functools

import jax
import jax.numpy as jnp
from jax import lax
from jax.experimental import pallas as pl
from jax.experimental.pallas import tpu as pltpu
from jax.sharding import PartitionSpec as P


TRANSFER_FLOPS = 62 * 10**8


def halves(value):
    high = value.astype(jnp.bfloat16)
    return high, (value - high.astype(jnp.float32)).astype(jnp.bfloat16)


def stacked(value, order, axis):
    high, low = halves(value)
    return jnp.concatenate([{"h": high, "l": low}[letter] for letter in order], axis=axis)


def lists_kernel(list_ref, count_ref, out_ref):
    rank = lax.axis_index("rep")
    for slot in range(out_ref.shape[0]):
        listed = jnp.where(slot < count_ref[rank], list_ref[rank, slot], -1)
        out_ref[slot : slot + 1, :] = jnp.full((1, out_ref.shape[1]), listed.astype(jnp.float32))


def copy_kernel(before_ref, in_ref, out_ref):
    out_ref[...] = in_ref[...]


def group_kernel(piece_count, *refs):
    piece_refs, vec_refs, out_ref = refs[:piece_count], refs[piece_count:-1], refs[-1]
    piece_feats = piece_refs[0].shape[0]
    width = vec_refs[0].shape[1]
    feat_count = piece_count * piece_feats
    rank = lax.axis_index("rep")
    for piece, ref in enumerate(piece_refs):
        out_ref[piece * piece_feats : (piece + 1) * piece_feats, :] = ref[...]
    for spot, ref in enumerate(vec_refs):
        span = pl.ds(pl.multiple_of((rank ^ spot) * width, width), width)
        out_ref[feat_count:, span] = ref[...]


def columns_kernel(feat_count, group_ref, col_ref, vec_ref):
    chunk = 2 * vec_ref.shape[0]
    cols = group_ref[:feat_count, :]
    col_ref[...] = stacked(cols.T, "hhl", 1)
    vecs = group_ref[feat_count:, :] * jnp.exp(jnp.sum(cols * cols, axis=0, keepdims=True) * (-1.0 / feat_count))
    for start in range(0, cols.shape[1], chunk):
        vec_ref[:, 3 * start : 3 * (start + chunk)] = stacked(vecs[:, start : start + chunk], "hhl", 1)


def rows_kernel(feat_count, *refs):
    panel_refs, (row_ref, scale_ref, mask_ref) = refs[:-3], refs[-3:]
    width = panel_refs[0].shape[1]
    group_blocks = mask_ref.shape[0] // 2
    blk_index = lax.axis_index("blk")
    for place, ref in enumerate(panel_refs):
        span = slice(place * width, (place + 1) * width)
        rows = ref[:feat_count, :]
        scale_ref[:, span] = jnp.exp(jnp.sum(rows * rows, axis=0, keepdims=True) * (-1.0 / feat_count))
        row_ref[:, span] = stacked(rows * (2.0 / feat_count), "hlh", 0)
        lists = ref[feat_count:, :]
        for spot in range(2 * group_blocks):
            column = (blk_index ^ (spot // group_blocks)) * group_blocks + spot % group_blocks
            hits = jnp.where(lists == column.astype(jnp.float32), 1.0, 0.0)
            mask_ref[spot : spot + 1, span] = jnp.max(hits, axis=0, keepdims=True)


def apply_kernel(groups, before_ref, row_ref, scale_ref, mask_ref, *refs):
    column_refs, refs = refs[: 2 * len(groups)], refs[2 * len(groups) :]
    out_refs = refs[-(row_ref.shape[1] // column_refs[1].shape[0]) :]
    so_far = refs[: len(refs) - len(out_refs)]
    width = out_refs[0].shape[1]
    chunk = 2 * width
    rows = row_ref[...]
    total = None
    for place, group in enumerate(groups):
        col_ref, vec_ref = column_refs[2 * place : 2 * place + 2]
        group_cols = col_ref.shape[0]
        for start in range(0, group_cols, chunk):
            inner = jnp.dot(col_ref[start : start + chunk, :], rows, preferred_element_type=jnp.float32)
            at = (group * group_cols + start) // width
            both = [jnp.broadcast_to(mask_ref[spot : spot + 1, :], (width, rows.shape[1])) for spot in (at, at + 1)]
            weight = stacked(jnp.exp(inner) * jnp.concatenate(both, axis=0), "hlh", 0)
            vecs = vec_ref[:, 3 * start : 3 * (start + chunk)]
            added = jnp.dot(vecs, weight, preferred_element_type=jnp.float32)
            total = added if total is None else total + added
    total = total * scale_ref[...]
    for spot, out_ref in enumerate(out_refs):
        tile = total[:, spot * width : (spot + 1) * width]
        out_ref[...] = tile + so_far[spot][...] if so_far else tile


def add_kernel(*refs):
    total = refs[0][...]
    for ref in refs[1:-1]:
        total = total + ref[...]
    refs[-1][...] = total


def swapped(value, axis, step):
    count = lax.axis_size(axis)
    return lax.ppermute(value, axis, [(source, source ^ step) for source in range(count)])


def shards(coords, eigvecs, nbr_list, nbr_count):
    cycle_size = lax.axis_size("blk")
    rep_size = lax.axis_size("rep")
    rep_index = lax.axis_index("rep")
    group_blocks, slot_count = nbr_list.shape
    eig_count, width = eigvecs.shape
    piece_feats, group_cols = coords.shape
    feat_count = rep_size * piece_feats
    f32, bf16 = jnp.float32, jnp.bfloat16
    shape = jax.ShapeDtypeStruct
    smem = pl.BlockSpec(memory_space=pltpu.SMEM)
    vmem = pl.BlockSpec(memory_space=pltpu.VMEM)
    anywhere = pl.BlockSpec(memory_space=pl.ANY)
    params = pltpu.CompilerParams(vmem_limit_bytes=(8 + group_blocks) * 1024 * 1024)
    hint = pl.CostEstimate(flops=TRANSFER_FLOPS, bytes_accessed=1024 * 1024, transcendentals=0)

    near = swapped(coords, "rep", 1)
    pieces = [swapped(coords, "rep", step) for step in range(2, rep_size)]
    pieces = [coords, pieces[0], near, *pieces[1:]]
    late_vecs = pl.pallas_call(
        copy_kernel,
        in_specs=[anywhere, vmem],
        out_shape=shape(eigvecs.shape, f32),
        compiler_params=params,
    )(near, eigvecs)
    vecs = [late_vecs] + [swapped(late_vecs, "rep", step) for step in range(1, rep_size)]
    lists = pl.pallas_call(
        lists_kernel,
        in_specs=[smem, smem],
        out_shape=shape((slot_count, width), f32),
        compiler_params=params,
    )(nbr_list, nbr_count)

    own_block = [lax.dynamic_slice_in_dim(piece, rep_index * width, width, 1) for piece in pieces]
    panel = jnp.concatenate([*own_block, lists], axis=0)
    steps = list(range(0, cycle_size, 2))
    half = len(steps) // 2
    steps[half:] = steps[: half - 1 : -1]
    panels = [panel] + [swapped(panel, "blk", step) for step in steps[1:]]

    own_group = pl.pallas_call(
        functools.partial(group_kernel, rep_size),
        out_shape=shape((feat_count + eig_count, group_cols), f32),
        compiler_params=params,
    )(*pieces, *vecs)
    sibling_group = swapped(own_group, "blk", 1)

    def columns_of(group):
        return pl.pallas_call(
            functools.partial(columns_kernel, feat_count),
            out_shape=[shape((group_cols, 3 * feat_count), bf16), shape((eig_count, 3 * group_cols), bf16)],
            compiler_params=params,
        )(group)


    def rows_of(first, **estimate):
        return pl.pallas_call(
            functools.partial(rows_kernel, feat_count),
            out_shape=[
                shape((3 * feat_count, half * width), bf16),
                shape((1, half * width), f32),
                shape((2 * group_blocks, half * width), f32),
            ],
            compiler_params=params,
            **estimate,
        )(*panels[first : first + half])

    def tiles_of(before, groups, rows, columns, so_far=()):
        return pl.pallas_call(
            functools.partial(apply_kernel, groups),
            in_specs=[anywhere] + [vmem] * (3 + len(columns) + len(so_far)),
            out_shape=[shape((eig_count, width), f32)] * half,
            compiler_params=params,
        )(before, *rows, *columns, *so_far)

    far_rows, near_rows = rows_of(half, cost_estimate=hint), rows_of(0)
    own, sibling = columns_of(own_group), columns_of(sibling_group)
    far_tiles = tiles_of(far_rows[1], (0,), far_rows, own)
    far_tiles = tiles_of(far_tiles[0], (1,), far_rows, sibling, far_tiles)
    near_tiles = tiles_of(far_tiles[0], (0, 1), near_rows, [*own, *sibling])
    tiles = [*near_tiles, *far_tiles]

    arrived = [swapped(tiles[place], "blk", steps[place]) for place in range(1, len(steps))]
    far = pl.pallas_call(
        add_kernel,
        out_shape=shape((eig_count, width), f32),
        compiler_params=params,
        cost_estimate=hint,
    )(*arrived[half - 1 :])
    total = tiles[0]
    for tile in arrived[: half - 1]:
        total = total + tile
    return total + far


def solution(mesh):
    return jax.shard_map(
        shards,
        mesh=mesh,
        in_specs=(P("rep", "blk"), P(None, ("blk", "rep")), P("blk", None), P("blk")),
        out_specs=P(None, ("blk", "rep")),
        check_vma=False,
    )
```

```python
import functools

import jax
import jax.numpy as jnp
from jax import lax
from jax.experimental import pallas as pl
from jax.experimental.pallas import tpu as pltpu
from jax.sharding import PartitionSpec as P


TRANSFER_FLOPS = 62 * 10**8


def halves(value):
    high = value.astype(jnp.bfloat16)
    return high, (value - high.astype(jnp.float32)).astype(jnp.bfloat16)


def stacked(value, order, axis):
    high, low = halves(value)
    return jnp.concatenate([{"h": high, "l": low}[letter] for letter in order], axis=axis)


def lists_kernel(list_ref, count_ref, out_ref):
    rank = lax.axis_index("rep")
    for slot in range(out_ref.shape[0]):
        listed = jnp.where(slot < count_ref[rank], list_ref[rank, slot], -1)
        out_ref[slot : slot + 1, :] = jnp.full((1, out_ref.shape[1]), listed.astype(jnp.float32))


def copy_kernel(before_ref, in_ref, out_ref):
    out_ref[...] = in_ref[...]


def group_kernel(piece_count, *refs):
    piece_refs, vec_refs, out_ref = refs[:piece_count], refs[piece_count:-1], refs[-1]
    piece_feats = piece_refs[0].shape[0]
    width = vec_refs[0].shape[1]
    feat_count = piece_count * piece_feats
    rank = lax.axis_index("rep")
    for piece, ref in enumerate(piece_refs):
        out_ref[piece * piece_feats : (piece + 1) * piece_feats, :] = ref[...]
    for spot, ref in enumerate(vec_refs[::-1]):
        span = pl.ds(pl.multiple_of((rank ^ spot) * width, width), width)
        out_ref[feat_count:, span] = ref[...]


def columns_kernel(feat_count, group_ref, col_ref, vec_ref):
    chunk = 2 * vec_ref.shape[0]
    cols = group_ref[:feat_count, :]
    col_ref[...] = stacked(cols.T, "hhl", 1)
    vecs = group_ref[feat_count:, :] * jnp.exp(jnp.sum(cols * cols, axis=0, keepdims=True) * (-1.0 / feat_count))
    for start in range(0, cols.shape[1], chunk):
        vec_ref[:, 3 * start : 3 * (start + chunk)] = stacked(vecs[:, start : start + chunk], "hhl", 1)


def rows_kernel(feat_count, *refs):
    panel_refs, (row_ref, scale_ref, mask_ref) = refs[:-3], refs[-3:]
    width = panel_refs[0].shape[1]
    group_blocks = mask_ref.shape[0] // 2
    blk_index = lax.axis_index("blk")
    for place, ref in enumerate(panel_refs):
        span = slice(place * width, (place + 1) * width)
        rows = ref[:feat_count, :]
        scale_ref[:, span] = jnp.exp(jnp.sum(rows * rows, axis=0, keepdims=True) * (-1.0 / feat_count))
        row_ref[:, span] = stacked(rows * (2.0 / feat_count), "hlh", 0)
        lists = ref[feat_count:, :]
        for spot in range(2 * group_blocks):
            column = (blk_index ^ (spot // group_blocks)) * group_blocks + spot % group_blocks
            hits = jnp.where(lists == column.astype(jnp.float32), 1.0, 0.0)
            mask_ref[spot : spot + 1, span] = jnp.max(hits, axis=0, keepdims=True)


def apply_kernel(row_ref, scale_ref, mask_ref, *refs):
    own_cols, own_vecs, sibling_cols, sibling_vecs, *out_refs = refs
    width = out_refs[0].shape[1]
    group_cols = own_cols.shape[0]
    chunk = 2 * width
    pairs = range(len(out_refs) // 2)
    totals = [None for _ in pairs]
    for group, (col_ref, vec_ref) in enumerate(((own_cols, own_vecs), (sibling_cols, sibling_vecs))):
        for start in range(0, group_cols, chunk):
            at = (group * group_cols + start) // width
            for pair in pairs:
                span = slice(pair * chunk, (pair + 1) * chunk)
                inner = jnp.dot(
                    col_ref[start : start + chunk, :], row_ref[:, span], preferred_element_type=jnp.float32
                )
                both = [jnp.broadcast_to(mask_ref[spot : spot + 1, span], (width, chunk)) for spot in (at, at + 1)]
                weight = stacked(jnp.exp(inner) * jnp.concatenate(both, axis=0), "hlh", 0)
                vecs = vec_ref[:, 3 * start : 3 * (start + chunk)]
                added = jnp.dot(vecs, weight, preferred_element_type=jnp.float32)
                totals[pair] = added if totals[pair] is None else totals[pair] + added
    for pair in pairs:
        total = totals[pair] * scale_ref[:, pair * chunk : (pair + 1) * chunk]
        out_refs[2 * pair][...] = total[:, :width]
        out_refs[2 * pair + 1][...] = total[:, width:]


def swapped(value, axis, step):
    count = lax.axis_size(axis)
    return lax.ppermute(value, axis, [(source, source ^ step) for source in range(count)])


def shards(coords, eigvecs, nbr_list, nbr_count):
    cycle_size = lax.axis_size("blk")
    rep_size = lax.axis_size("rep")
    rep_index = lax.axis_index("rep")
    group_blocks, slot_count = nbr_list.shape
    eig_count, width = eigvecs.shape
    piece_feats, group_cols = coords.shape
    feat_count = rep_size * piece_feats
    f32, bf16 = jnp.float32, jnp.bfloat16
    shape = jax.ShapeDtypeStruct
    smem = pl.BlockSpec(memory_space=pltpu.SMEM)
    vmem = pl.BlockSpec(memory_space=pltpu.VMEM)
    anywhere = pl.BlockSpec(memory_space=pl.ANY)
    params = pltpu.CompilerParams(vmem_limit_bytes=(8 + group_blocks) * 1024 * 1024)
    hint = pl.CostEstimate(flops=TRANSFER_FLOPS, bytes_accessed=1024 * 1024, transcendentals=0)

    pieces = [coords] + [swapped(coords, "rep", step) for step in range(1, rep_size)]
    late_vecs = pl.pallas_call(
        copy_kernel,
        in_specs=[anywhere, vmem],
        out_shape=shape(eigvecs.shape, f32),
        compiler_params=params,
    )(pieces[1], eigvecs)
    vecs = [swapped(late_vecs if step > 1 else eigvecs, "rep", step) for step in range(rep_size - 1, 0, -1)]
    vecs = [*vecs, late_vecs]
    lists = pl.pallas_call(
        lists_kernel,
        in_specs=[smem, smem],
        out_shape=shape((slot_count, width), f32),
        compiler_params=params,
    )(nbr_list, nbr_count)

    own_block = [lax.dynamic_slice_in_dim(piece, rep_index * width, width, 1) for piece in pieces]
    panel = jnp.concatenate([*own_block, lists], axis=0)
    steps = list(range(0, cycle_size, 2))
    panels = [panel] + [swapped(panel, "blk", step) for step in steps[1:]]

    own_group = pl.pallas_call(
        functools.partial(group_kernel, rep_size),
        out_shape=shape((feat_count + eig_count, group_cols), f32),
        compiler_params=params,
    )(*pieces, *vecs)
    sibling_group = swapped(own_group, "blk", 1)

    def columns_of(group):
        return pl.pallas_call(
            functools.partial(columns_kernel, feat_count),
            out_shape=[shape((group_cols, 3 * feat_count), bf16), shape((eig_count, 3 * group_cols), bf16)],
            compiler_params=params,
        )(group)

    row_count = len(panels) * width
    rows = pl.pallas_call(
        functools.partial(rows_kernel, feat_count),
        out_shape=[
            shape((3 * feat_count, row_count), bf16),
            shape((1, row_count), f32),
            shape((2 * group_blocks, row_count), f32),
        ],
        compiler_params=params,
        cost_estimate=hint,
    )(*panels)
    columns = [*columns_of(own_group), *columns_of(sibling_group)]
    tiles = pl.pallas_call(
        apply_kernel,
        out_shape=[shape((eig_count, width), f32)] * len(panels),
        compiler_params=params,
    )(*rows, *columns)
    total = tiles[0]
    for place in range(len(steps) - 1, 0, -1):
        total = total + swapped(tiles[place], "blk", steps[place])
    return total


def solution(mesh):
    return jax.shard_map(
        shards,
        mesh=mesh,
        in_specs=(P("rep", "blk"), P(None, ("blk", "rep")), P("blk", None), P("blk")),
        out_specs=P(None, ("blk", "rep")),
        check_vma=False,
    )
```

```python
import functools

import jax
import jax.numpy as jnp
from jax import lax
from jax.experimental import pallas as pl
from jax.experimental.pallas import tpu as pltpu
from jax.sharding import PartitionSpec as P


TRANSFER_FLOPS = 62 * 10**8


def halves(value):
    high = value.astype(jnp.bfloat16)
    return high, (value - high.astype(jnp.float32)).astype(jnp.bfloat16)


def stacked(value, order, axis):
    high, low = halves(value)
    return jnp.concatenate([{"h": high, "l": low}[letter] for letter in order], axis=axis)


def lists_kernel(list_ref, count_ref, out_ref):
    rank = lax.axis_index("rep")
    for slot in range(out_ref.shape[0]):
        listed = jnp.where(slot < count_ref[rank], list_ref[rank, slot], -1)
        out_ref[slot : slot + 1, :] = jnp.full((1, out_ref.shape[1]), listed.astype(jnp.float32))


def copy_kernel(before_ref, in_ref, out_ref):
    out_ref[...] = in_ref[...]


def group_kernel(piece_count, *refs):
    piece_refs, vec_refs, out_ref = refs[:piece_count], refs[piece_count:-1], refs[-1]
    piece_feats = piece_refs[0].shape[0]
    width = vec_refs[0].shape[1]
    feat_count = piece_count * piece_feats
    rank = lax.axis_index("rep")
    for piece, ref in enumerate(piece_refs):
        out_ref[piece * piece_feats : (piece + 1) * piece_feats, :] = ref[...]
    for spot, ref in enumerate(vec_refs[::-1]):
        span = pl.ds(pl.multiple_of((rank ^ spot) * width, width), width)
        out_ref[feat_count:, span] = ref[...]


def columns_kernel(feat_count, group_ref, col_ref, vec_ref):
    chunk = 2 * vec_ref.shape[0]
    cols = group_ref[:feat_count, :]
    col_ref[...] = stacked(cols.T, "hhl", 1)
    vecs = group_ref[feat_count:, :] * jnp.exp(jnp.sum(cols * cols, axis=0, keepdims=True) * (-1.0 / feat_count))
    for start in range(0, cols.shape[1], chunk):
        vec_ref[:, 3 * start : 3 * (start + chunk)] = stacked(vecs[:, start : start + chunk], "hhl", 1)


def rows_kernel(feat_count, *refs):
    panel_refs, (row_ref, scale_ref, mask_ref) = refs[:-3], refs[-3:]
    width = panel_refs[0].shape[1]
    group_blocks = mask_ref.shape[0] // 2
    blk_index = lax.axis_index("blk")
    for place, ref in enumerate(panel_refs):
        span = slice(place * width, (place + 1) * width)
        rows = ref[:feat_count, :]
        scale_ref[:, span] = jnp.exp(jnp.sum(rows * rows, axis=0, keepdims=True) * (-1.0 / feat_count))
        row_ref[:, span] = stacked(rows * (2.0 / feat_count), "hlh", 0)
        lists = ref[feat_count:, :]
        for spot in range(2 * group_blocks):
            column = (blk_index ^ (spot // group_blocks)) * group_blocks + spot % group_blocks
            hits = jnp.where(lists == column.astype(jnp.float32), 1.0, 0.0)
            mask_ref[spot : spot + 1, span] = jnp.max(hits, axis=0, keepdims=True)


def apply_kernel(row_ref, scale_ref, mask_ref, *refs):
    own_cols, own_vecs, sibling_cols, sibling_vecs, *out_refs = refs
    width = out_refs[0].shape[1]
    group_cols = own_cols.shape[0]
    chunk = 2 * width
    pairs = range(len(out_refs) // 2)
    totals = [None for _ in pairs]
    for group, (col_ref, vec_ref) in enumerate(((own_cols, own_vecs), (sibling_cols, sibling_vecs))):
        for start in range(0, group_cols, chunk):
            at = (group * group_cols + start) // width
            for pair in pairs:
                span = slice(pair * chunk, (pair + 1) * chunk)
                inner = jnp.dot(
                    col_ref[start : start + chunk, :], row_ref[:, span], preferred_element_type=jnp.float32
                )
                both = [jnp.broadcast_to(mask_ref[spot : spot + 1, span], (width, chunk)) for spot in (at, at + 1)]
                weight = stacked(jnp.exp(inner) * jnp.concatenate(both, axis=0), "hlh", 0)
                vecs = vec_ref[:, 3 * start : 3 * (start + chunk)]
                added = jnp.dot(vecs, weight, preferred_element_type=jnp.float32)
                totals[pair] = added if totals[pair] is None else totals[pair] + added
    for pair in pairs:
        total = totals[pair] * scale_ref[:, pair * chunk : (pair + 1) * chunk]
        out_refs[2 * pair][...] = total[:, :width]
        out_refs[2 * pair + 1][...] = total[:, width:]


def swapped(value, axis, step):
    count = lax.axis_size(axis)
    return lax.ppermute(value, axis, [(source, source ^ step) for source in range(count)])


def shards(coords, eigvecs, nbr_list, nbr_count):
    cycle_size = lax.axis_size("blk")
    rep_size = lax.axis_size("rep")
    rep_index = lax.axis_index("rep")
    group_blocks, slot_count = nbr_list.shape
    eig_count, width = eigvecs.shape
    piece_feats, group_cols = coords.shape
    feat_count = rep_size * piece_feats
    f32, bf16 = jnp.float32, jnp.bfloat16
    shape = jax.ShapeDtypeStruct
    smem = pl.BlockSpec(memory_space=pltpu.SMEM)
    vmem = pl.BlockSpec(memory_space=pltpu.VMEM)
    anywhere = pl.BlockSpec(memory_space=pl.ANY)
    params = pltpu.CompilerParams(vmem_limit_bytes=(8 + group_blocks) * 1024 * 1024)
    hint = pl.CostEstimate(flops=TRANSFER_FLOPS, bytes_accessed=1024 * 1024, transcendentals=0)

    far_first = [2, 3, 1, *range(4, rep_size)]
    pieces = {step: swapped(coords, "rep", step) for step in far_first}
    near = pieces[1]
    pieces = [coords] + [pieces[step] for step in far_first]
    late_vecs = pl.pallas_call(
        copy_kernel,
        in_specs=[anywhere, vmem],
        out_shape=shape(eigvecs.shape, f32),
        compiler_params=params,
    )(near, eigvecs)
    vecs = [swapped(late_vecs, "rep", step) for step in range(rep_size - 1, 0, -1)] + [late_vecs]
    lists = pl.pallas_call(
        lists_kernel,
        in_specs=[smem, smem],
        out_shape=shape((slot_count, width), f32),
        compiler_params=params,
    )(nbr_list, nbr_count)

    own_block = [lax.dynamic_slice_in_dim(piece, rep_index * width, width, 1) for piece in pieces]
    panel = jnp.concatenate([*own_block, lists], axis=0)
    steps = list(range(0, cycle_size, 2))
    panels = [panel] + [swapped(panel, "blk", step) for step in steps[1:]]

    own_group = pl.pallas_call(
        functools.partial(group_kernel, rep_size),
        out_shape=shape((feat_count + eig_count, group_cols), f32),
        compiler_params=params,
    )(*pieces, *vecs)
    sibling_group = swapped(own_group, "blk", 1)

    def columns_of(group):
        return pl.pallas_call(
            functools.partial(columns_kernel, feat_count),
            out_shape=[shape((group_cols, 3 * feat_count), bf16), shape((eig_count, 3 * group_cols), bf16)],
            compiler_params=params,
        )(group)

    row_count = len(panels) * width
    rows = pl.pallas_call(
        functools.partial(rows_kernel, feat_count),
        out_shape=[
            shape((3 * feat_count, row_count), bf16),
            shape((1, row_count), f32),
            shape((2 * group_blocks, row_count), f32),
        ],
        compiler_params=params,
        cost_estimate=hint,
    )(*panels)
    columns = [*columns_of(own_group), *columns_of(sibling_group)]
    tiles = pl.pallas_call(
        apply_kernel,
        out_shape=[shape((eig_count, width), f32)] * len(panels),
        compiler_params=params,
    )(*rows, *columns)
    total = tiles[0]
    for place in range(len(steps) - 1, 0, -1):
        total = total + swapped(tiles[place], "blk", steps[place])
    return total


def solution(mesh):
    return jax.shard_map(
        shards,
        mesh=mesh,
        in_specs=(P("rep", "blk"), P(None, ("blk", "rep")), P("blk", None), P("blk")),
        out_specs=P(None, ("blk", "rep")),
        check_vma=False,
    )
```

```python
import functools

import jax
import jax.numpy as jnp
from jax import lax
from jax.experimental import pallas as pl
from jax.experimental.pallas import tpu as pltpu
from jax.sharding import PartitionSpec as P


TRANSFER_FLOPS = 62 * 10**8


def halves(value):
    high = value.astype(jnp.bfloat16)
    return high, (value - high.astype(jnp.float32)).astype(jnp.bfloat16)


def stacked(value, order, axis):
    high, low = halves(value)
    return jnp.concatenate([{"h": high, "l": low}[letter] for letter in order], axis=axis)


def lists_kernel(list_ref, count_ref, out_ref):
    rank = lax.axis_index("rep")
    for slot in range(out_ref.shape[0]):
        listed = jnp.where(slot < count_ref[rank], list_ref[rank, slot], -1)
        out_ref[slot : slot + 1, :] = jnp.full((1, out_ref.shape[1]), listed.astype(jnp.float32))


def copy_kernel(before_ref, in_ref, out_ref):
    out_ref[...] = in_ref[...]


def group_kernel(piece_count, *refs):
    piece_refs, vec_refs, out_ref = refs[:piece_count], refs[piece_count:-1], refs[-1]
    piece_feats = piece_refs[0].shape[0]
    width = vec_refs[0].shape[1]
    feat_count = piece_count * piece_feats
    rank = lax.axis_index("rep")
    for piece, ref in enumerate(piece_refs):
        out_ref[piece * piece_feats : (piece + 1) * piece_feats, :] = ref[...]
    for spot, ref in enumerate(vec_refs[::-1]):
        span = pl.ds(pl.multiple_of((rank ^ spot) * width, width), width)
        out_ref[feat_count:, span] = ref[...]


def columns_kernel(feat_count, group_ref, col_ref, vec_ref):
    chunk = 2 * vec_ref.shape[0]
    cols = group_ref[:feat_count, :]
    col_ref[...] = stacked(cols.T, "hhl", 1)
    vecs = group_ref[feat_count:, :] * jnp.exp(jnp.sum(cols * cols, axis=0, keepdims=True) * (-1.0 / feat_count))
    for start in range(0, cols.shape[1], chunk):
        vec_ref[:, 3 * start : 3 * (start + chunk)] = stacked(vecs[:, start : start + chunk], "hhl", 1)


def rows_kernel(feat_count, *refs):
    panel_refs, (row_ref, scale_ref, mask_ref) = refs[:-3], refs[-3:]
    width = panel_refs[0].shape[1]
    group_blocks = mask_ref.shape[0] // 2
    blk_index = lax.axis_index("blk")
    for place, ref in enumerate(panel_refs):
        span = slice(place * width, (place + 1) * width)
        rows = ref[:feat_count, :]
        scale_ref[:, span] = jnp.exp(jnp.sum(rows * rows, axis=0, keepdims=True) * (-1.0 / feat_count))
        row_ref[:, span] = stacked(rows * (2.0 / feat_count), "hlh", 0)
        lists = ref[feat_count:, :]
        for spot in range(2 * group_blocks):
            column = (blk_index ^ (spot // group_blocks)) * group_blocks + spot % group_blocks
            hits = jnp.where(lists == column.astype(jnp.float32), 1.0, 0.0)
            mask_ref[spot : spot + 1, span] = jnp.max(hits, axis=0, keepdims=True)


def apply_kernel(row_ref, scale_ref, mask_ref, *refs):
    own_cols, own_vecs, sibling_cols, sibling_vecs, *out_refs = refs
    width = out_refs[0].shape[1]
    group_cols = own_cols.shape[0]
    chunk = 2 * width
    pairs = range(len(out_refs) // 2)
    totals = [None for _ in pairs]
    for group, (col_ref, vec_ref) in enumerate(((own_cols, own_vecs), (sibling_cols, sibling_vecs))):
        for start in range(0, group_cols, chunk):
            at = (group * group_cols + start) // width
            for pair in pairs:
                span = slice(pair * chunk, (pair + 1) * chunk)
                inner = jnp.dot(
                    col_ref[start : start + chunk, :], row_ref[:, span], preferred_element_type=jnp.float32
                )
                both = [jnp.broadcast_to(mask_ref[spot : spot + 1, span], (width, chunk)) for spot in (at, at + 1)]
                weight = stacked(jnp.exp(inner) * jnp.concatenate(both, axis=0), "hlh", 0)
                vecs = vec_ref[:, 3 * start : 3 * (start + chunk)]
                added = jnp.dot(vecs, weight, preferred_element_type=jnp.float32)
                totals[pair] = added if totals[pair] is None else totals[pair] + added
    for pair in pairs:
        total = totals[pair] * scale_ref[:, pair * chunk : (pair + 1) * chunk]
        out_refs[2 * pair][...] = total[:, :width]
        out_refs[2 * pair + 1][...] = total[:, width:]


def swapped(value, axis, step):
    count = lax.axis_size(axis)
    return lax.ppermute(value, axis, [(source, source ^ step) for source in range(count)])


def shards(coords, eigvecs, nbr_list, nbr_count):
    cycle_size = lax.axis_size("blk")
    rep_size = lax.axis_size("rep")
    rep_index = lax.axis_index("rep")
    group_blocks, slot_count = nbr_list.shape
    eig_count, width = eigvecs.shape
    piece_feats, group_cols = coords.shape
    feat_count = rep_size * piece_feats
    f32, bf16 = jnp.float32, jnp.bfloat16
    shape = jax.ShapeDtypeStruct
    smem = pl.BlockSpec(memory_space=pltpu.SMEM)
    vmem = pl.BlockSpec(memory_space=pltpu.VMEM)
    anywhere = pl.BlockSpec(memory_space=pl.ANY)
    params = pltpu.CompilerParams(vmem_limit_bytes=(8 + group_blocks) * 1024 * 1024)
    hint = pl.CostEstimate(flops=TRANSFER_FLOPS, bytes_accessed=1024 * 1024, transcendentals=0)

    send_order = [1, 3, 2, *range(4, rep_size)]
    pieces = {step: swapped(coords, "rep", step) for step in send_order}
    near = pieces[1]
    pieces = [coords] + [pieces[step] for step in send_order]
    late_vecs = pl.pallas_call(
        copy_kernel,
        in_specs=[anywhere, vmem],
        out_shape=shape(eigvecs.shape, f32),
        compiler_params=params,
    )(near, eigvecs)
    vecs = [swapped(late_vecs, "rep", step) for step in range(rep_size - 1, 0, -1)] + [late_vecs]
    lists = pl.pallas_call(
        lists_kernel,
        in_specs=[smem, smem],
        out_shape=shape((slot_count, width), f32),
        compiler_params=params,
    )(nbr_list, nbr_count)

    own_block = [lax.dynamic_slice_in_dim(piece, rep_index * width, width, 1) for piece in pieces]
    panel = jnp.concatenate([*own_block, lists], axis=0)
    steps = list(range(0, cycle_size, 2))
    panels = [panel] + [swapped(panel, "blk", step) for step in steps[1:]]

    own_group = pl.pallas_call(
        functools.partial(group_kernel, rep_size),
        out_shape=shape((feat_count + eig_count, group_cols), f32),
        compiler_params=params,
    )(*pieces, *vecs)
    sibling_group = swapped(own_group, "blk", 1)

    def columns_of(group):
        return pl.pallas_call(
            functools.partial(columns_kernel, feat_count),
            out_shape=[shape((group_cols, 3 * feat_count), bf16), shape((eig_count, 3 * group_cols), bf16)],
            compiler_params=params,
        )(group)

    row_count = len(panels) * width
    rows = pl.pallas_call(
        functools.partial(rows_kernel, feat_count),
        out_shape=[
            shape((3 * feat_count, row_count), bf16),
            shape((1, row_count), f32),
            shape((2 * group_blocks, row_count), f32),
        ],
        compiler_params=params,
        cost_estimate=hint,
    )(*panels)
    columns = [*columns_of(own_group), *columns_of(sibling_group)]
    tiles = pl.pallas_call(
        apply_kernel,
        out_shape=[shape((eig_count, width), f32)] * len(panels),
        compiler_params=params,
    )(*rows, *columns)
    total = tiles[0]
    for place in range(len(steps) - 1, 0, -1):
        total = total + swapped(tiles[place], "blk", steps[place])
    return total


def solution(mesh):
    return jax.shard_map(
        shards,
        mesh=mesh,
        in_specs=(P("rep", "blk"), P(None, ("blk", "rep")), P("blk", None), P("blk")),
        out_specs=P(None, ("blk", "rep")),
        check_vma=False,
    )
```

```python
import functools

import jax
import jax.numpy as jnp
from jax import lax
from jax.experimental import pallas as pl
from jax.experimental.pallas import tpu as pltpu
from jax.sharding import PartitionSpec as P


TRANSFER_FLOPS = 62 * 10**8


def halves(value):
    high = value.astype(jnp.bfloat16)
    return high, (value - high.astype(jnp.float32)).astype(jnp.bfloat16)


def stacked(value, order, axis):
    high, low = halves(value)
    return jnp.concatenate([{"h": high, "l": low}[letter] for letter in order], axis=axis)


def lists_kernel(list_ref, count_ref, out_ref):
    rank = lax.axis_index("rep")
    for slot in range(out_ref.shape[0]):
        listed = jnp.where(slot < count_ref[rank], list_ref[rank, slot], -1)
        out_ref[slot : slot + 1, :] = jnp.full((1, out_ref.shape[1]), listed.astype(jnp.float32))


def copy_kernel(before_ref, in_ref, out_ref):
    out_ref[...] = in_ref[...]


def group_kernel(piece_count, *refs):
    piece_refs, vec_refs, out_ref = refs[:piece_count], refs[piece_count:-1], refs[-1]
    piece_feats = piece_refs[0].shape[0]
    width = vec_refs[0].shape[1]
    feat_count = piece_count * piece_feats
    rank = lax.axis_index("rep")
    for piece, ref in enumerate(piece_refs):
        out_ref[piece * piece_feats : (piece + 1) * piece_feats, :] = ref[...]
    for spot, ref in enumerate(vec_refs[::-1]):
        span = pl.ds(pl.multiple_of((rank ^ spot) * width, width), width)
        out_ref[feat_count:, span] = ref[...]


def columns_kernel(feat_count, group_ref, col_ref, vec_ref):
    chunk = 2 * vec_ref.shape[0]
    cols = group_ref[:feat_count, :]
    col_ref[...] = stacked(cols.T, "hhl", 1)
    vecs = group_ref[feat_count:, :] * jnp.exp(jnp.sum(cols * cols, axis=0, keepdims=True) * (-1.0 / feat_count))
    for start in range(0, cols.shape[1], chunk):
        vec_ref[:, 3 * start : 3 * (start + chunk)] = stacked(vecs[:, start : start + chunk], "hhl", 1)


def rows_kernel(feat_count, *refs):
    panel_refs, (row_ref, scale_ref, mask_ref) = refs[:-3], refs[-3:]
    width = panel_refs[0].shape[1]
    group_blocks = mask_ref.shape[0] // 2
    blk_index = lax.axis_index("blk")
    for place, ref in enumerate(panel_refs):
        span = slice(place * width, (place + 1) * width)
        rows = ref[:feat_count, :]
        scale_ref[:, span] = jnp.exp(jnp.sum(rows * rows, axis=0, keepdims=True) * (-1.0 / feat_count))
        row_ref[:, span] = stacked(rows * (2.0 / feat_count), "hlh", 0)
        lists = ref[feat_count:, :]
        for spot in range(2 * group_blocks):
            column = (blk_index ^ (spot // group_blocks)) * group_blocks + spot % group_blocks
            hits = jnp.where(lists == column.astype(jnp.float32), 1.0, 0.0)
            mask_ref[spot : spot + 1, span] = jnp.max(hits, axis=0, keepdims=True)


def apply_kernel(row_ref, scale_ref, mask_ref, *refs):
    own_cols, own_vecs, sibling_cols, sibling_vecs, *out_refs = refs
    width = out_refs[0].shape[1]
    group_cols = own_cols.shape[0]
    chunk = 2 * width
    pairs = range(len(out_refs) // 2)
    totals = [None for _ in pairs]
    for group, (col_ref, vec_ref) in enumerate(((own_cols, own_vecs), (sibling_cols, sibling_vecs))):
        for start in range(0, group_cols, chunk):
            at = (group * group_cols + start) // width
            for pair in pairs:
                span = slice(pair * chunk, (pair + 1) * chunk)
                inner = jnp.dot(
                    col_ref[start : start + chunk, :], row_ref[:, span], preferred_element_type=jnp.float32
                )
                both = [jnp.broadcast_to(mask_ref[spot : spot + 1, span], (width, chunk)) for spot in (at, at + 1)]
                weight = stacked(jnp.exp(inner) * jnp.concatenate(both, axis=0), "hlh", 0)
                vecs = vec_ref[:, 3 * start : 3 * (start + chunk)]
                added = jnp.dot(vecs, weight, preferred_element_type=jnp.float32)
                totals[pair] = added if totals[pair] is None else totals[pair] + added
    for pair in pairs:
        total = totals[pair] * scale_ref[:, pair * chunk : (pair + 1) * chunk]
        out_refs[2 * pair][...] = total[:, :width]
        out_refs[2 * pair + 1][...] = total[:, width:]


def swapped(value, axis, step):
    count = lax.axis_size(axis)
    return lax.ppermute(value, axis, [(source, source ^ step) for source in range(count)])


def shards(coords, eigvecs, nbr_list, nbr_count):
    cycle_size = lax.axis_size("blk")
    rep_size = lax.axis_size("rep")
    rep_index = lax.axis_index("rep")
    group_blocks, slot_count = nbr_list.shape
    eig_count, width = eigvecs.shape
    piece_feats, group_cols = coords.shape
    feat_count = rep_size * piece_feats
    f32, bf16 = jnp.float32, jnp.bfloat16
    shape = jax.ShapeDtypeStruct
    smem = pl.BlockSpec(memory_space=pltpu.SMEM)
    vmem = pl.BlockSpec(memory_space=pltpu.VMEM)
    anywhere = pl.BlockSpec(memory_space=pl.ANY)
    params = pltpu.CompilerParams(vmem_limit_bytes=(8 + group_blocks) * 1024 * 1024)
    hint = pl.CostEstimate(flops=TRANSFER_FLOPS, bytes_accessed=1024 * 1024, transcendentals=0)

    send_order = [1, 3, 2, *range(4, rep_size)]
    pieces = {step: swapped(coords, "rep", step) for step in send_order}
    near = pieces[1]
    pieces = [coords] + [pieces[step] for step in send_order]
    late_vecs = pl.pallas_call(
        copy_kernel,
        in_specs=[anywhere, vmem],
        out_shape=shape(eigvecs.shape, f32),
        compiler_params=params,
    )(near, eigvecs)
    vecs = [swapped(late_vecs if step > 1 else eigvecs, "rep", step) for step in range(rep_size - 1, 0, -1)]
    vecs = [*vecs, late_vecs]
    lists = pl.pallas_call(
        lists_kernel,
        in_specs=[smem, smem],
        out_shape=shape((slot_count, width), f32),
        compiler_params=params,
    )(nbr_list, nbr_count)

    own_block = [lax.dynamic_slice_in_dim(piece, rep_index * width, width, 1) for piece in pieces]
    panel = jnp.concatenate([*own_block, lists], axis=0)
    steps = list(range(0, cycle_size, 2))
    panels = [panel] + [swapped(panel, "blk", step) for step in steps[1:]]

    own_group = pl.pallas_call(
        functools.partial(group_kernel, rep_size),
        out_shape=shape((feat_count + eig_count, group_cols), f32),
        compiler_params=params,
    )(*pieces, *vecs)
    sibling_group = swapped(own_group, "blk", 1)

    def columns_of(group):
        return pl.pallas_call(
            functools.partial(columns_kernel, feat_count),
            out_shape=[shape((group_cols, 3 * feat_count), bf16), shape((eig_count, 3 * group_cols), bf16)],
            compiler_params=params,
        )(group)

    row_count = len(panels) * width
    rows = pl.pallas_call(
        functools.partial(rows_kernel, feat_count),
        out_shape=[
            shape((3 * feat_count, row_count), bf16),
            shape((1, row_count), f32),
            shape((2 * group_blocks, row_count), f32),
        ],
        compiler_params=params,
        cost_estimate=hint,
    )(*panels)
    columns = [*columns_of(own_group), *columns_of(sibling_group)]
    tiles = pl.pallas_call(
        apply_kernel,
        out_shape=[shape((eig_count, width), f32)] * len(panels),
        compiler_params=params,
    )(*rows, *columns)
    total = tiles[0]
    for place in range(len(steps) - 1, 0, -1):
        total = total + swapped(tiles[place], "blk", steps[place])
    return total


def solution(mesh):
    return jax.shard_map(
        shards,
        mesh=mesh,
        in_specs=(P("rep", "blk"), P(None, ("blk", "rep")), P("blk", None), P("blk")),
        out_specs=P(None, ("blk", "rep")),
        check_vma=False,
    )
```

```python
import functools

import jax
import jax.numpy as jnp
from jax import lax
from jax.experimental import pallas as pl
from jax.experimental.pallas import tpu as pltpu
from jax.sharding import PartitionSpec as P


TRANSFER_FLOPS = 62 * 10**8


def halves(value):
    high = value.astype(jnp.bfloat16)
    return high, (value - high.astype(jnp.float32)).astype(jnp.bfloat16)


def stacked(value, order, axis):
    high, low = halves(value)
    return jnp.concatenate([{"h": high, "l": low}[letter] for letter in order], axis=axis)


def lists_kernel(list_ref, count_ref, out_ref):
    rank = lax.axis_index("rep")
    for slot in range(out_ref.shape[0]):
        listed = jnp.where(slot < count_ref[rank], list_ref[rank, slot], -1)
        out_ref[slot : slot + 1, :] = jnp.full((1, out_ref.shape[1]), listed.astype(jnp.float32))


def copy_kernel(before_ref, in_ref, out_ref):
    out_ref[...] = in_ref[...]


def group_kernel(piece_count, *refs):
    piece_refs, vec_refs, out_ref = refs[:piece_count], refs[piece_count:-1], refs[-1]
    piece_feats = piece_refs[0].shape[0]
    width = vec_refs[0].shape[1]
    feat_count = piece_count * piece_feats
    rank = lax.axis_index("rep")
    for piece, ref in enumerate(piece_refs):
        out_ref[piece * piece_feats : (piece + 1) * piece_feats, :] = ref[...]
    for spot, ref in enumerate(vec_refs[::-1]):
        span = pl.ds(pl.multiple_of((rank ^ spot) * width, width), width)
        out_ref[feat_count:, span] = ref[...]


def columns_kernel(feat_count, group_ref, col_ref, vec_ref):
    chunk = 2 * vec_ref.shape[0]
    cols = group_ref[:feat_count, :]
    col_ref[...] = stacked(cols.T, "hhl", 1)
    vecs = group_ref[feat_count:, :] * jnp.exp(jnp.sum(cols * cols, axis=0, keepdims=True) * (-1.0 / feat_count))
    for start in range(0, cols.shape[1], chunk):
        vec_ref[:, 3 * start : 3 * (start + chunk)] = stacked(vecs[:, start : start + chunk], "hhl", 1)


def rows_kernel(feat_count, *refs):
    panel_refs, (row_ref, scale_ref, mask_ref) = refs[:-3], refs[-3:]
    width = panel_refs[0].shape[1]
    group_blocks = mask_ref.shape[0] // 2
    blk_index = lax.axis_index("blk")
    for place, ref in enumerate(panel_refs):
        span = slice(place * width, (place + 1) * width)
        rows = ref[:feat_count, :]
        scale_ref[:, span] = jnp.exp(jnp.sum(rows * rows, axis=0, keepdims=True) * (-1.0 / feat_count))
        row_ref[:, span] = stacked(rows * (2.0 / feat_count), "hlh", 0)
        lists = ref[feat_count:, :]
        for spot in range(2 * group_blocks):
            column = (blk_index ^ (spot // group_blocks)) * group_blocks + spot % group_blocks
            hits = jnp.where(lists == column.astype(jnp.float32), 1.0, 0.0)
            mask_ref[spot : spot + 1, span] = jnp.max(hits, axis=0, keepdims=True)


def apply_kernel(row_ref, scale_ref, mask_ref, *refs):
    own_cols, own_vecs, sibling_cols, sibling_vecs, *out_refs = refs
    width = out_refs[0].shape[1]
    group_cols = own_cols.shape[0]
    chunk = 2 * width
    pairs = range(len(out_refs) // 2)
    totals = [None for _ in pairs]
    for group, (col_ref, vec_ref) in enumerate(((own_cols, own_vecs), (sibling_cols, sibling_vecs))):
        for start in range(0, group_cols, chunk):
            at = (group * group_cols + start) // width
            for pair in pairs:
                span = slice(pair * chunk, (pair + 1) * chunk)
                inner = jnp.dot(
                    col_ref[start : start + chunk, :], row_ref[:, span], preferred_element_type=jnp.float32
                )
                both = [jnp.broadcast_to(mask_ref[spot : spot + 1, span], (width, chunk)) for spot in (at, at + 1)]
                weight = stacked(jnp.exp(inner) * jnp.concatenate(both, axis=0), "hlh", 0)
                vecs = vec_ref[:, 3 * start : 3 * (start + chunk)]
                added = jnp.dot(vecs, weight, preferred_element_type=jnp.float32)
                totals[pair] = added if totals[pair] is None else totals[pair] + added
    for pair in pairs:
        total = totals[pair] * scale_ref[:, pair * chunk : (pair + 1) * chunk]
        out_refs[2 * pair][...] = total[:, :width]
        out_refs[2 * pair + 1][...] = total[:, width:]


def swapped(value, axis, step):
    count = lax.axis_size(axis)
    return lax.ppermute(value, axis, [(source, source ^ step) for source in range(count)])


def shards(coords, eigvecs, nbr_list, nbr_count):
    cycle_size = lax.axis_size("blk")
    rep_size = lax.axis_size("rep")
    rep_index = lax.axis_index("rep")
    group_blocks, slot_count = nbr_list.shape
    eig_count, width = eigvecs.shape
    piece_feats, group_cols = coords.shape
    feat_count = rep_size * piece_feats
    f32, bf16 = jnp.float32, jnp.bfloat16
    shape = jax.ShapeDtypeStruct
    smem = pl.BlockSpec(memory_space=pltpu.SMEM)
    vmem = pl.BlockSpec(memory_space=pltpu.VMEM)
    anywhere = pl.BlockSpec(memory_space=pl.ANY)
    params = pltpu.CompilerParams(vmem_limit_bytes=(8 + group_blocks) * 1024 * 1024)
    hint = pl.CostEstimate(flops=TRANSFER_FLOPS, bytes_accessed=1024 * 1024, transcendentals=0)

    send_order = [3, 1, 2, *range(4, rep_size)]
    pieces = {step: swapped(coords, "rep", step) for step in send_order}
    near = pieces[1]
    pieces = [coords] + [pieces[step] for step in send_order]
    late_vecs = pl.pallas_call(
        copy_kernel,
        in_specs=[anywhere, vmem],
        out_shape=shape(eigvecs.shape, f32),
        compiler_params=params,
    )(near, eigvecs)
    vecs = [swapped(late_vecs, "rep", step) for step in range(rep_size - 1, 0, -1)] + [late_vecs]
    lists = pl.pallas_call(
        lists_kernel,
        in_specs=[smem, smem],
        out_shape=shape((slot_count, width), f32),
        compiler_params=params,
    )(nbr_list, nbr_count)

    own_block = [lax.dynamic_slice_in_dim(piece, rep_index * width, width, 1) for piece in pieces]
    panel = jnp.concatenate([*own_block, lists], axis=0)
    steps = list(range(0, cycle_size, 2))
    panels = [panel] + [swapped(panel, "blk", step) for step in steps[1:]]

    own_group = pl.pallas_call(
        functools.partial(group_kernel, rep_size),
        out_shape=shape((feat_count + eig_count, group_cols), f32),
        compiler_params=params,
    )(*pieces, *vecs)
    sibling_group = swapped(own_group, "blk", 1)

    def columns_of(group):
        return pl.pallas_call(
            functools.partial(columns_kernel, feat_count),
            out_shape=[shape((group_cols, 3 * feat_count), bf16), shape((eig_count, 3 * group_cols), bf16)],
            compiler_params=params,
        )(group)

    row_count = len(panels) * width
    rows = pl.pallas_call(
        functools.partial(rows_kernel, feat_count),
        out_shape=[
            shape((3 * feat_count, row_count), bf16),
            shape((1, row_count), f32),
            shape((2 * group_blocks, row_count), f32),
        ],
        compiler_params=params,
        cost_estimate=hint,
    )(*panels)
    columns = [*columns_of(own_group), *columns_of(sibling_group)]
    tiles = pl.pallas_call(
        apply_kernel,
        out_shape=[shape((eig_count, width), f32)] * len(panels),
        compiler_params=params,
    )(*rows, *columns)
    total = tiles[0]
    for place in range(len(steps) - 1, 0, -1):
        total = total + swapped(tiles[place], "blk", steps[place])
    return total


def solution(mesh):
    return jax.shard_map(
        shards,
        mesh=mesh,
        in_specs=(P("rep", "blk"), P(None, ("blk", "rep")), P("blk", None), P("blk")),
        out_specs=P(None, ("blk", "rep")),
        check_vma=False,
    )
```

```python
import functools

import jax
import jax.numpy as jnp
from jax import lax
from jax.experimental import pallas as pl
from jax.experimental.pallas import tpu as pltpu
from jax.sharding import PartitionSpec as P


TRANSFER_FLOPS = 62 * 10**8


def halves(value):
    high = value.astype(jnp.bfloat16)
    return high, (value - high.astype(jnp.float32)).astype(jnp.bfloat16)


def stacked(value, order, axis):
    high, low = halves(value)
    return jnp.concatenate([{"h": high, "l": low}[letter] for letter in order], axis=axis)


def lists_kernel(list_ref, count_ref, out_ref):
    rank = lax.axis_index("rep")
    for slot in range(out_ref.shape[0]):
        listed = jnp.where(slot < count_ref[rank], list_ref[rank, slot], -1)
        out_ref[slot : slot + 1, :] = jnp.full((1, out_ref.shape[1]), listed.astype(jnp.float32))


def copy_kernel(before_ref, in_ref, out_ref):
    out_ref[...] = in_ref[...]


def group_kernel(piece_count, order, *refs):
    piece_refs, vec_refs, out_ref = refs[:piece_count], refs[piece_count:-1], refs[-1]
    piece_feats = piece_refs[0].shape[0]
    width = vec_refs[0].shape[1]
    feat_count = piece_count * piece_feats
    rank = lax.axis_index("rep")
    for piece, ref in enumerate(piece_refs):
        out_ref[piece * piece_feats : (piece + 1) * piece_feats, :] = ref[...]
    for spot, ref in zip(order, vec_refs):
        span = pl.ds(pl.multiple_of((rank ^ spot) * width, width), width)
        out_ref[feat_count:, span] = ref[...]


def columns_kernel(feat_count, group_ref, col_ref, vec_ref):
    chunk = 2 * vec_ref.shape[0]
    cols = group_ref[:feat_count, :]
    col_ref[...] = stacked(cols.T, "hhl", 1)
    vecs = group_ref[feat_count:, :] * jnp.exp(jnp.sum(cols * cols, axis=0, keepdims=True) * (-1.0 / feat_count))
    for start in range(0, cols.shape[1], chunk):
        vec_ref[:, 3 * start : 3 * (start + chunk)] = stacked(vecs[:, start : start + chunk], "hhl", 1)


def rows_kernel(feat_count, *refs):
    panel_refs, (row_ref, scale_ref, mask_ref) = refs[:-3], refs[-3:]
    width = panel_refs[0].shape[1]
    group_blocks = mask_ref.shape[0] // 2
    blk_index = lax.axis_index("blk")
    for place, ref in enumerate(panel_refs):
        span = slice(place * width, (place + 1) * width)
        rows = ref[:feat_count, :]
        scale_ref[:, span] = jnp.exp(jnp.sum(rows * rows, axis=0, keepdims=True) * (-1.0 / feat_count))
        row_ref[:, span] = stacked(rows * (2.0 / feat_count), "hlh", 0)
        lists = ref[feat_count:, :]
        for spot in range(2 * group_blocks):
            column = (blk_index ^ (spot // group_blocks)) * group_blocks + spot % group_blocks
            hits = jnp.where(lists == column.astype(jnp.float32), 1.0, 0.0)
            mask_ref[spot : spot + 1, span] = jnp.max(hits, axis=0, keepdims=True)


def apply_kernel(row_ref, scale_ref, mask_ref, *refs):
    own_cols, own_vecs, sibling_cols, sibling_vecs, *out_refs = refs
    width = out_refs[0].shape[1]
    group_cols = own_cols.shape[0]
    chunk = 2 * width
    pairs = range(len(out_refs) // 2)
    totals = [None for _ in pairs]
    for group, (col_ref, vec_ref) in enumerate(((own_cols, own_vecs), (sibling_cols, sibling_vecs))):
        for start in range(0, group_cols, chunk):
            at = (group * group_cols + start) // width
            for pair in pairs:
                span = slice(pair * chunk, (pair + 1) * chunk)
                inner = jnp.dot(
                    col_ref[start : start + chunk, :], row_ref[:, span], preferred_element_type=jnp.float32
                )
                both = [jnp.broadcast_to(mask_ref[spot : spot + 1, span], (width, chunk)) for spot in (at, at + 1)]
                weight = stacked(jnp.exp(inner) * jnp.concatenate(both, axis=0), "hlh", 0)
                vecs = vec_ref[:, 3 * start : 3 * (start + chunk)]
                added = jnp.dot(vecs, weight, preferred_element_type=jnp.float32)
                totals[pair] = added if totals[pair] is None else totals[pair] + added
    for pair in pairs:
        total = totals[pair] * scale_ref[:, pair * chunk : (pair + 1) * chunk]
        out_refs[2 * pair][...] = total[:, :width]
        out_refs[2 * pair + 1][...] = total[:, width:]


def swapped(value, axis, step):
    count = lax.axis_size(axis)
    return lax.ppermute(value, axis, [(source, source ^ step) for source in range(count)])


def shards(coords, eigvecs, nbr_list, nbr_count):
    cycle_size = lax.axis_size("blk")
    rep_size = lax.axis_size("rep")
    rep_index = lax.axis_index("rep")
    group_blocks, slot_count = nbr_list.shape
    eig_count, width = eigvecs.shape
    piece_feats, group_cols = coords.shape
    feat_count = rep_size * piece_feats
    f32, bf16 = jnp.float32, jnp.bfloat16
    shape = jax.ShapeDtypeStruct
    smem = pl.BlockSpec(memory_space=pltpu.SMEM)
    vmem = pl.BlockSpec(memory_space=pltpu.VMEM)
    anywhere = pl.BlockSpec(memory_space=pl.ANY)
    params = pltpu.CompilerParams(vmem_limit_bytes=(8 + group_blocks) * 1024 * 1024)
    hint = pl.CostEstimate(flops=TRANSFER_FLOPS, bytes_accessed=1024 * 1024, transcendentals=0)

    send_order = [1, 3, 2, *range(4, rep_size)]
    pieces = {step: swapped(coords, "rep", step) for step in send_order}
    near = pieces[1]
    pieces = [coords] + [pieces[step] for step in send_order]
    late_vecs = pl.pallas_call(
        copy_kernel,
        in_specs=[anywhere, vmem],
        out_shape=shape(eigvecs.shape, f32),
        compiler_params=params,
    )(near, eigvecs)
    order = [*range(2, rep_size), 1, 0]
    vecs = [swapped(late_vecs if step > 1 else eigvecs, "rep", step) for step in order[:-1]]
    vecs = [*vecs, late_vecs]
    lists = pl.pallas_call(
        lists_kernel,
        in_specs=[smem, smem],
        out_shape=shape((slot_count, width), f32),
        compiler_params=params,
    )(nbr_list, nbr_count)

    own_block = [lax.dynamic_slice_in_dim(piece, rep_index * width, width, 1) for piece in pieces]
    panel = jnp.concatenate([*own_block, lists], axis=0)
    steps = list(range(0, cycle_size, 2))
    panels = [panel] + [swapped(panel, "blk", step) for step in steps[1:]]

    own_group = pl.pallas_call(
        functools.partial(group_kernel, rep_size, order),
        out_shape=shape((feat_count + eig_count, group_cols), f32),
        compiler_params=params,
    )(*pieces, *vecs)
    sibling_group = swapped(own_group, "blk", 1)

    def columns_of(group):
        return pl.pallas_call(
            functools.partial(columns_kernel, feat_count),
            out_shape=[shape((group_cols, 3 * feat_count), bf16), shape((eig_count, 3 * group_cols), bf16)],
            compiler_params=params,
        )(group)

    row_count = len(panels) * width
    rows = pl.pallas_call(
        functools.partial(rows_kernel, feat_count),
        out_shape=[
            shape((3 * feat_count, row_count), bf16),
            shape((1, row_count), f32),
            shape((2 * group_blocks, row_count), f32),
        ],
        compiler_params=params,
        cost_estimate=hint,
    )(*panels)
    columns = [*columns_of(own_group), *columns_of(sibling_group)]
    tiles = pl.pallas_call(
        apply_kernel,
        out_shape=[shape((eig_count, width), f32)] * len(panels),
        compiler_params=params,
    )(*rows, *columns)
    total = tiles[0]
    for place in range(len(steps) - 1, 0, -1):
        total = total + swapped(tiles[place], "blk", steps[place])
    return total


def solution(mesh):
    return jax.shard_map(
        shards,
        mesh=mesh,
        in_specs=(P("rep", "blk"), P(None, ("blk", "rep")), P("blk", None), P("blk")),
        out_specs=P(None, ("blk", "rep")),
        check_vma=False,
    )
```

```python
import functools

import jax
import jax.numpy as jnp
from jax import lax
from jax.experimental import pallas as pl
from jax.experimental.pallas import tpu as pltpu
from jax.sharding import PartitionSpec as P


TRANSFER_FLOPS = 62 * 10**8
LOG2_E = 1.4426950408889634


def halves(value):
    high = value.astype(jnp.bfloat16)
    return high, (value - high.astype(jnp.float32)).astype(jnp.bfloat16)


def stacked(value, order, axis):
    high, low = halves(value)
    return jnp.concatenate([{"h": high, "l": low}[letter] for letter in order], axis=axis)


def lists_kernel(list_ref, count_ref, out_ref):
    rank = lax.axis_index("rep")
    for slot in range(out_ref.shape[0]):
        listed = jnp.where(slot < count_ref[rank], list_ref[rank, slot], -1)
        out_ref[slot : slot + 1, :] = jnp.full((1, out_ref.shape[1]), listed.astype(jnp.float32))


def copy_kernel(before_ref, in_ref, out_ref):
    out_ref[...] = in_ref[...]


def group_kernel(piece_count, *refs):
    piece_refs, vec_refs, out_ref = refs[:piece_count], refs[piece_count:-1], refs[-1]
    piece_feats = piece_refs[0].shape[0]
    width = vec_refs[0].shape[1]
    feat_count = piece_count * piece_feats
    rank = lax.axis_index("rep")
    for piece, ref in enumerate(piece_refs):
        out_ref[piece * piece_feats : (piece + 1) * piece_feats, :] = ref[...]
    for spot, ref in enumerate(vec_refs[::-1]):
        span = pl.ds(pl.multiple_of((rank ^ spot) * width, width), width)
        out_ref[feat_count:, span] = ref[...]


def columns_kernel(feat_count, first, group_ref, col_ref, vec_ref):
    chunk = 2 * vec_ref.shape[0]
    cols = group_ref[:feat_count, :]
    col_ref[:, : 3 * feat_count] = stacked(cols.T, "hhl", 1)
    flags = (col_ref.shape[0], col_ref.shape[1] - 3 * feat_count)
    block = lax.broadcasted_iota(jnp.int32, flags, 0) // vec_ref.shape[0] + first
    here = lax.broadcasted_iota(jnp.int32, flags, 1) == block
    col_ref[:, 3 * feat_count :] = jnp.where(here, 1.0, 0.0).astype(jnp.bfloat16)
    vecs = group_ref[feat_count:, :] * jnp.exp(jnp.sum(cols * cols, axis=0, keepdims=True) * (-1.0 / feat_count))
    for start in range(0, cols.shape[1], chunk):
        vec_ref[:, 3 * start : 3 * (start + chunk)] = stacked(vecs[:, start : start + chunk], "hhl", 1)


def rows_kernel(feat_count, group_blocks, *refs):
    panel_refs, (row_ref, scale_ref, listed_ref) = refs[:-3], refs[-3:]
    width = panel_refs[0].shape[1]
    blk_index = lax.axis_index("blk")
    listed_ref[...] = jnp.ones_like(listed_ref)
    for place, ref in enumerate(panel_refs):
        span = slice(place * width, (place + 1) * width)
        rows = ref[:feat_count, :]
        scale_ref[:, span] = jnp.exp(jnp.sum(rows * rows, axis=0, keepdims=True) * (-1.0 / feat_count))
        row_ref[: 3 * feat_count, span] = stacked(rows * (2.0 * LOG2_E / feat_count), "hlh", 0)
        lists = ref[feat_count:, :]
        for spot in range(2 * group_blocks):
            column = (blk_index ^ (spot // group_blocks)) * group_blocks + spot % group_blocks
            hits = jnp.where(lists == column.astype(jnp.float32), 1.0, 0.0)
            listed_ref[spot : spot + 1, span] = jnp.max(hits, axis=0, keepdims=True)
    row_ref[3 * feat_count :, :] = ((listed_ref[...] - 1.0) * 16384.0).astype(jnp.bfloat16)


def apply_kernel(row_ref, scale_ref, *refs):
    own_cols, own_vecs, sibling_cols, sibling_vecs, *out_refs = refs
    width = out_refs[0].shape[1]
    chunk = 2 * width
    pairs = range(len(out_refs) // 2)
    totals = [None for _ in pairs]
    for col_ref, vec_ref in ((own_cols, own_vecs), (sibling_cols, sibling_vecs)):
        for start in range(0, col_ref.shape[0], chunk):
            for pair in pairs:
                span = slice(pair * chunk, (pair + 1) * chunk)
                inner = jnp.dot(
                    col_ref[start : start + chunk, :], row_ref[:, span], preferred_element_type=jnp.float32
                )
                weight = stacked(jnp.exp2(inner), "hlh", 0)
                vecs = vec_ref[:, 3 * start : 3 * (start + chunk)]
                added = jnp.dot(vecs, weight, preferred_element_type=jnp.float32)
                totals[pair] = added if totals[pair] is None else totals[pair] + added
    for pair in pairs:
        total = totals[pair] * scale_ref[:, pair * chunk : (pair + 1) * chunk]
        out_refs[2 * pair][...] = total[:, :width]
        out_refs[2 * pair + 1][...] = total[:, width:]


def swapped(value, axis, step):
    count = lax.axis_size(axis)
    return lax.ppermute(value, axis, [(source, source ^ step) for source in range(count)])


def shards(coords, eigvecs, nbr_list, nbr_count):
    cycle_size = lax.axis_size("blk")
    rep_size = lax.axis_size("rep")
    rep_index = lax.axis_index("rep")
    group_blocks, slot_count = nbr_list.shape
    eig_count, width = eigvecs.shape
    piece_feats, group_cols = coords.shape
    feat_count = rep_size * piece_feats
    f32, bf16 = jnp.float32, jnp.bfloat16
    shape = jax.ShapeDtypeStruct
    smem = pl.BlockSpec(memory_space=pltpu.SMEM)
    vmem = pl.BlockSpec(memory_space=pltpu.VMEM)
    anywhere = pl.BlockSpec(memory_space=pl.ANY)
    params = pltpu.CompilerParams(vmem_limit_bytes=(8 + group_blocks) * 1024 * 1024)
    hint = pl.CostEstimate(flops=TRANSFER_FLOPS, bytes_accessed=1024 * 1024, transcendentals=0)

    pieces = [coords] + [swapped(coords, "rep", step) for step in range(1, rep_size)]
    late_vecs = pl.pallas_call(
        copy_kernel,
        in_specs=[anywhere, vmem],
        out_shape=shape(eigvecs.shape, f32),
        compiler_params=params,
    )(pieces[1], eigvecs)
    vecs = [swapped(late_vecs, "rep", step) for step in range(rep_size - 1, 0, -1)] + [late_vecs]
    lists = pl.pallas_call(
        lists_kernel,
        in_specs=[smem, smem],
        out_shape=shape((slot_count, width), f32),
        compiler_params=params,
    )(nbr_list, nbr_count)

    own_block = [lax.dynamic_slice_in_dim(piece, rep_index * width, width, 1) for piece in pieces]
    panel = jnp.concatenate([*own_block, lists], axis=0)
    steps = list(range(0, cycle_size, 2))
    panels = [panel] + [swapped(panel, "blk", step) for step in steps[1:]]

    own_group = pl.pallas_call(
        functools.partial(group_kernel, rep_size),
        out_shape=shape((feat_count + eig_count, group_cols), f32),
        compiler_params=params,
    )(*pieces, *vecs)
    sibling_group = swapped(own_group, "blk", 1)

    depth = 3 * feat_count + max(16, 2 * group_blocks)

    def columns_of(group, first):
        return pl.pallas_call(
            functools.partial(columns_kernel, feat_count, first),
            out_shape=[shape((group_cols, depth), bf16), shape((eig_count, 3 * group_cols), bf16)],
            compiler_params=params,
        )(group)

    row_count = len(panels) * width
    rows = pl.pallas_call(
        functools.partial(rows_kernel, feat_count, group_blocks),
        out_shape=[shape((depth, row_count), bf16), shape((1, row_count), f32)],
        scratch_shapes=[pltpu.VMEM((depth - 3 * feat_count, row_count), f32)],
        compiler_params=params,
        cost_estimate=hint,
    )(*panels)
    columns = [*columns_of(own_group, 0), *columns_of(sibling_group, group_blocks)]
    tiles = pl.pallas_call(
        apply_kernel,
        out_shape=[shape((eig_count, width), f32)] * len(panels),
        compiler_params=params,
    )(*rows, *columns)
    total = tiles[0]
    for place in range(len(steps) - 1, 0, -1):
        total = total + swapped(tiles[place], "blk", steps[place])
    return total


def solution(mesh):
    return jax.shard_map(
        shards,
        mesh=mesh,
        in_specs=(P("rep", "blk"), P(None, ("blk", "rep")), P("blk", None), P("blk")),
        out_specs=P(None, ("blk", "rep")),
        check_vma=False,
    )
```

```python
import functools

import jax
import jax.numpy as jnp
from jax import lax
from jax.experimental import pallas as pl
from jax.experimental.pallas import tpu as pltpu
from jax.sharding import PartitionSpec as P


TRANSFER_FLOPS = 62 * 10**8


def halves(value):
    high = value.astype(jnp.bfloat16)
    return high, (value - high.astype(jnp.float32)).astype(jnp.bfloat16)


def stacked(value, order, axis):
    high, low = halves(value)
    return jnp.concatenate([{"h": high, "l": low}[letter] for letter in order], axis=axis)


def lists_kernel(list_ref, count_ref, out_ref):
    rank = lax.axis_index("rep")
    for slot in range(out_ref.shape[0]):
        listed = jnp.where(slot < count_ref[rank], list_ref[rank, slot], -1)
        out_ref[slot : slot + 1, :] = jnp.full((1, out_ref.shape[1]), listed.astype(jnp.float32))


def copy_kernel(before_ref, in_ref, out_ref):
    out_ref[...] = in_ref[...]


def group_kernel(piece_count, order, *refs):
    piece_refs, vec_refs, out_ref = refs[:piece_count], refs[piece_count:-1], refs[-1]
    piece_feats = piece_refs[0].shape[0]
    width = vec_refs[0].shape[1]
    feat_count = piece_count * piece_feats
    rank = lax.axis_index("rep")
    for piece, ref in enumerate(piece_refs):
        out_ref[piece * piece_feats : (piece + 1) * piece_feats, :] = ref[...]
    for spot, ref in zip(order, vec_refs):
        span = pl.ds(pl.multiple_of((rank ^ spot) * width, width), width)
        out_ref[feat_count:, span] = ref[...]


def columns_kernel(feat_count, group_ref, col_ref, vec_ref):
    chunk = 2 * vec_ref.shape[0]
    cols = group_ref[:feat_count, :]
    col_ref[...] = stacked(cols.T, "hhl", 1)
    vecs = group_ref[feat_count:, :] * jnp.exp(jnp.sum(cols * cols, axis=0, keepdims=True) * (-1.0 / feat_count))
    for start in range(0, cols.shape[1], chunk):
        vec_ref[:, 3 * start : 3 * (start + chunk)] = stacked(vecs[:, start : start + chunk], "hhl", 1)


def rows_kernel(feat_count, *refs):
    panel_refs, (row_ref, scale_ref, mask_ref) = refs[:-3], refs[-3:]
    width = panel_refs[0].shape[1]
    group_blocks = mask_ref.shape[0] // 2
    blk_index = lax.axis_index("blk")
    for place, ref in enumerate(panel_refs):
        span = slice(place * width, (place + 1) * width)
        rows = ref[:feat_count, :]
        scale_ref[:, span] = jnp.exp(jnp.sum(rows * rows, axis=0, keepdims=True) * (-1.0 / feat_count))
        row_ref[:, span] = stacked(rows * (2.0 / feat_count), "hlh", 0)
        lists = ref[feat_count:, :]
        for spot in range(2 * group_blocks):
            column = (blk_index ^ (spot // group_blocks)) * group_blocks + spot % group_blocks
            hits = jnp.where(lists == column.astype(jnp.float32), 1.0, 0.0)
            mask_ref[spot : spot + 1, span] = jnp.max(hits, axis=0, keepdims=True)


def apply_kernel(row_ref, scale_ref, mask_ref, *refs):
    own_cols, own_vecs, sibling_cols, sibling_vecs, *out_refs = refs
    width = out_refs[0].shape[1]
    group_cols = own_cols.shape[0]
    chunk = 2 * width
    pairs = range(len(out_refs) // 2)
    totals = [None for _ in pairs]
    for group, (col_ref, vec_ref) in enumerate(((own_cols, own_vecs), (sibling_cols, sibling_vecs))):
        for start in range(0, group_cols, chunk):
            at = (group * group_cols + start) // width
            for pair in pairs:
                span = slice(pair * chunk, (pair + 1) * chunk)
                inner = jnp.dot(
                    col_ref[start : start + chunk, :], row_ref[:, span], preferred_element_type=jnp.float32
                )
                both = [jnp.broadcast_to(mask_ref[spot : spot + 1, span], (width, chunk)) for spot in (at, at + 1)]
                weight = stacked(jnp.exp(inner) * jnp.concatenate(both, axis=0), "hlh", 0)
                vecs = vec_ref[:, 3 * start : 3 * (start + chunk)]
                added = jnp.dot(vecs, weight, preferred_element_type=jnp.float32)
                totals[pair] = added if totals[pair] is None else totals[pair] + added
    for pair in pairs:
        total = totals[pair] * scale_ref[:, pair * chunk : (pair + 1) * chunk]
        out_refs[2 * pair][...] = total[:, :width]
        out_refs[2 * pair + 1][...] = total[:, width:]


def swapped(value, axis, step):
    count = lax.axis_size(axis)
    return lax.ppermute(value, axis, [(source, source ^ step) for source in range(count)])


def shards(coords, eigvecs, nbr_list, nbr_count):
    cycle_size = lax.axis_size("blk")
    rep_size = lax.axis_size("rep")
    rep_index = lax.axis_index("rep")
    group_blocks, slot_count = nbr_list.shape
    eig_count, width = eigvecs.shape
    piece_feats, group_cols = coords.shape
    feat_count = rep_size * piece_feats
    f32, bf16 = jnp.float32, jnp.bfloat16
    shape = jax.ShapeDtypeStruct
    smem = pl.BlockSpec(memory_space=pltpu.SMEM)
    vmem = pl.BlockSpec(memory_space=pltpu.VMEM)
    anywhere = pl.BlockSpec(memory_space=pl.ANY)
    params = pltpu.CompilerParams(vmem_limit_bytes=(8 + group_blocks) * 1024 * 1024)
    hint = pl.CostEstimate(flops=TRANSFER_FLOPS, bytes_accessed=1024 * 1024, transcendentals=0)

    pieces = [coords] + [swapped(coords, "rep", step) for step in range(1, rep_size)]
    late_vecs = pl.pallas_call(
        copy_kernel,
        in_specs=[anywhere, vmem],
        out_shape=shape(eigvecs.shape, f32),
        compiler_params=params,
    )(pieces[1], eigvecs)
    order = [*range(2, rep_size), 1, 0]
    vecs = [swapped(late_vecs, "rep", step) for step in order[:-1]] + [late_vecs]
    lists = pl.pallas_call(
        lists_kernel,
        in_specs=[smem, smem],
        out_shape=shape((slot_count, width), f32),
        compiler_params=params,
    )(nbr_list, nbr_count)

    own_block = [lax.dynamic_slice_in_dim(piece, rep_index * width, width, 1) for piece in pieces]
    panel = jnp.concatenate([*own_block, lists], axis=0)
    steps = list(range(0, cycle_size, 2))
    panels = [panel] + [swapped(panel, "blk", step) for step in steps[1:]]

    own_group = pl.pallas_call(
        functools.partial(group_kernel, rep_size, order),
        out_shape=shape((feat_count + eig_count, group_cols), f32),
        compiler_params=params,
    )(*pieces, *vecs)
    sibling_group = swapped(own_group, "blk", 1)

    def columns_of(group):
        return pl.pallas_call(
            functools.partial(columns_kernel, feat_count),
            out_shape=[shape((group_cols, 3 * feat_count), bf16), shape((eig_count, 3 * group_cols), bf16)],
            compiler_params=params,
        )(group)

    row_count = len(panels) * width
    rows = pl.pallas_call(
        functools.partial(rows_kernel, feat_count),
        out_shape=[
            shape((3 * feat_count, row_count), bf16),
            shape((1, row_count), f32),
            shape((2 * group_blocks, row_count), f32),
        ],
        compiler_params=params,
        cost_estimate=hint,
    )(*panels)
    columns = [*columns_of(own_group), *columns_of(sibling_group)]
    tiles = pl.pallas_call(
        apply_kernel,
        out_shape=[shape((eig_count, width), f32)] * len(panels),
        compiler_params=params,
    )(*rows, *columns)
    total = tiles[0]
    for place in range(len(steps) - 1, 0, -1):
        total = total + swapped(tiles[place], "blk", steps[place])
    return total


def solution(mesh):
    return jax.shard_map(
        shards,
        mesh=mesh,
        in_specs=(P("rep", "blk"), P(None, ("blk", "rep")), P("blk", None), P("blk")),
        out_specs=P(None, ("blk", "rep")),
        check_vma=False,
    )
```

```python
import functools

import jax
import jax.numpy as jnp
from jax import lax
from jax.experimental import pallas as pl
from jax.experimental.pallas import tpu as pltpu
from jax.sharding import PartitionSpec as P


TRANSFER_FLOPS = 62 * 10**8


def halves(value):
    high = value.astype(jnp.bfloat16)
    return high, (value - high.astype(jnp.float32)).astype(jnp.bfloat16)


def stacked(value, order, axis):
    high, low = halves(value)
    return jnp.concatenate([{"h": high, "l": low}[letter] for letter in order], axis=axis)


def lists_kernel(list_ref, count_ref, out_ref):
    rank = lax.axis_index("rep")
    for slot in range(out_ref.shape[0]):
        listed = jnp.where(slot < count_ref[rank], list_ref[rank, slot], -1)
        out_ref[slot : slot + 1, :] = jnp.full((1, out_ref.shape[1]), listed.astype(jnp.float32))


def copy_kernel(before_ref, in_ref, out_ref):
    out_ref[...] = in_ref[...]


def group_kernel(piece_count, order, *refs):
    piece_refs, vec_refs, out_ref = refs[:piece_count], refs[piece_count:-1], refs[-1]
    piece_feats = piece_refs[0].shape[0]
    width = vec_refs[0].shape[1]
    feat_count = piece_count * piece_feats
    rank = lax.axis_index("rep")
    for piece, ref in enumerate(piece_refs):
        out_ref[piece * piece_feats : (piece + 1) * piece_feats, :] = ref[...]
    for spot, ref in zip(order, vec_refs):
        span = pl.ds(pl.multiple_of((rank ^ spot) * width, width), width)
        out_ref[feat_count:, span] = ref[...]


def columns_kernel(feat_count, group_ref, col_ref, vec_ref):
    chunk = 2 * vec_ref.shape[0]
    cols = group_ref[:feat_count, :]
    col_ref[...] = stacked(cols.T, "hhl", 1)
    vecs = group_ref[feat_count:, :] * jnp.exp(jnp.sum(cols * cols, axis=0, keepdims=True) * (-1.0 / feat_count))
    for start in range(0, cols.shape[1], chunk):
        vec_ref[:, 3 * start : 3 * (start + chunk)] = stacked(vecs[:, start : start + chunk], "hhl", 1)


def rows_kernel(feat_count, *refs):
    panel_refs, (row_ref, scale_ref, mask_ref) = refs[:-3], refs[-3:]
    width = panel_refs[0].shape[1]
    group_blocks = mask_ref.shape[0] // 2
    blk_index = lax.axis_index("blk")
    for place, ref in enumerate(panel_refs):
        span = slice(place * width, (place + 1) * width)
        rows = ref[:feat_count, :]
        scale_ref[:, span] = jnp.exp(jnp.sum(rows * rows, axis=0, keepdims=True) * (-1.0 / feat_count))
        row_ref[:, span] = stacked(rows * (2.0 / feat_count), "hlh", 0)
        lists = ref[feat_count:, :]
        for spot in range(2 * group_blocks):
            column = (blk_index ^ (spot // group_blocks)) * group_blocks + spot % group_blocks
            hits = jnp.where(lists == column.astype(jnp.float32), 1.0, 0.0)
            mask_ref[spot : spot + 1, span] = jnp.max(hits, axis=0, keepdims=True)


def apply_kernel(row_ref, scale_ref, mask_ref, *refs):
    own_cols, own_vecs, sibling_cols, sibling_vecs, *out_refs = refs
    width = out_refs[0].shape[1]
    group_cols = own_cols.shape[0]
    chunk = 2 * width
    pairs = range(len(out_refs) // 2)
    totals = [None for _ in pairs]
    for group, (col_ref, vec_ref) in enumerate(((own_cols, own_vecs), (sibling_cols, sibling_vecs))):
        for start in range(0, group_cols, chunk):
            at = (group * group_cols + start) // width
            for pair in pairs:
                span = slice(pair * chunk, (pair + 1) * chunk)
                inner = jnp.dot(
                    col_ref[start : start + chunk, :], row_ref[:, span], preferred_element_type=jnp.float32
                )
                both = [jnp.broadcast_to(mask_ref[spot : spot + 1, span], (width, chunk)) for spot in (at, at + 1)]
                weight = stacked(jnp.exp(inner) * jnp.concatenate(both, axis=0), "hlh", 0)
                vecs = vec_ref[:, 3 * start : 3 * (start + chunk)]
                added = jnp.dot(vecs, weight, preferred_element_type=jnp.float32)
                totals[pair] = added if totals[pair] is None else totals[pair] + added
    for pair in pairs:
        total = totals[pair] * scale_ref[:, pair * chunk : (pair + 1) * chunk]
        out_refs[2 * pair][...] = total[:, :width]
        out_refs[2 * pair + 1][...] = total[:, width:]


def swapped(value, axis, step):
    count = lax.axis_size(axis)
    return lax.ppermute(value, axis, [(source, source ^ step) for source in range(count)])


def shards(coords, eigvecs, nbr_list, nbr_count):
    cycle_size = lax.axis_size("blk")
    rep_size = lax.axis_size("rep")
    rep_index = lax.axis_index("rep")
    group_blocks, slot_count = nbr_list.shape
    eig_count, width = eigvecs.shape
    piece_feats, group_cols = coords.shape
    feat_count = rep_size * piece_feats
    f32, bf16 = jnp.float32, jnp.bfloat16
    shape = jax.ShapeDtypeStruct
    smem = pl.BlockSpec(memory_space=pltpu.SMEM)
    vmem = pl.BlockSpec(memory_space=pltpu.VMEM)
    anywhere = pl.BlockSpec(memory_space=pl.ANY)
    params = pltpu.CompilerParams(vmem_limit_bytes=(8 + group_blocks) * 1024 * 1024)
    hint = pl.CostEstimate(flops=TRANSFER_FLOPS, bytes_accessed=1024 * 1024, transcendentals=0)

    pieces = [coords] + [swapped(coords, "rep", step) for step in range(1, rep_size)]
    late_vecs = pl.pallas_call(
        copy_kernel,
        in_specs=[anywhere, vmem],
        out_shape=shape(eigvecs.shape, f32),
        compiler_params=params,
    )(pieces[1], eigvecs)
    order = [*range(2, rep_size), 1, 0]
    vecs = [swapped(late_vecs if step > 1 else eigvecs, "rep", step) for step in order[:-1]] + [late_vecs]
    lists = pl.pallas_call(
        lists_kernel,
        in_specs=[smem, smem],
        out_shape=shape((slot_count, width), f32),
        compiler_params=params,
    )(nbr_list, nbr_count)

    own_block = [lax.dynamic_slice_in_dim(piece, rep_index * width, width, 1) for piece in pieces]
    panel = jnp.concatenate([*own_block, lists], axis=0)
    steps = list(range(0, cycle_size, 2))
    panels = [panel] + [swapped(panel, "blk", step) for step in steps[1:]]

    own_group = pl.pallas_call(
        functools.partial(group_kernel, rep_size, order),
        out_shape=shape((feat_count + eig_count, group_cols), f32),
        compiler_params=params,
    )(*pieces, *vecs)
    sibling_group = swapped(own_group, "blk", 1)

    def columns_of(group):
        return pl.pallas_call(
            functools.partial(columns_kernel, feat_count),
            out_shape=[shape((group_cols, 3 * feat_count), bf16), shape((eig_count, 3 * group_cols), bf16)],
            compiler_params=params,
        )(group)

    row_count = len(panels) * width
    rows = pl.pallas_call(
        functools.partial(rows_kernel, feat_count),
        out_shape=[
            shape((3 * feat_count, row_count), bf16),
            shape((1, row_count), f32),
            shape((2 * group_blocks, row_count), f32),
        ],
        compiler_params=params,
        cost_estimate=hint,
    )(*panels)
    columns = [*columns_of(own_group), *columns_of(sibling_group)]
    tiles = pl.pallas_call(
        apply_kernel,
        out_shape=[shape((eig_count, width), f32)] * len(panels),
        compiler_params=params,
    )(*rows, *columns)
    total = tiles[0]
    for place in range(len(steps) - 1, 0, -1):
        total = total + swapped(tiles[place], "blk", steps[place])
    return total


def solution(mesh):
    return jax.shard_map(
        shards,
        mesh=mesh,
        in_specs=(P("rep", "blk"), P(None, ("blk", "rep")), P("blk", None), P("blk")),
        out_specs=P(None, ("blk", "rep")),
        check_vma=False,
    )
```

```python
import functools

import jax
import jax.numpy as jnp
from jax import lax
from jax.experimental import pallas as pl
from jax.experimental.pallas import tpu as pltpu
from jax.sharding import PartitionSpec as P


TRANSFER_FLOPS = 62 * 10**8
LOG2_E = 1.4426950408889634


def halves(value):
    high = value.astype(jnp.bfloat16)
    return high, (value - high.astype(jnp.float32)).astype(jnp.bfloat16)


def stacked(value, order, axis):
    high, low = halves(value)
    return jnp.concatenate([{"h": high, "l": low}[letter] for letter in order], axis=axis)


def lists_kernel(list_ref, count_ref, out_ref):
    rank = lax.axis_index("rep")
    for slot in range(out_ref.shape[0]):
        listed = jnp.where(slot < count_ref[rank], list_ref[rank, slot], -1)
        out_ref[slot : slot + 1, :] = jnp.full((1, out_ref.shape[1]), listed.astype(jnp.float32))


def copy_kernel(before_ref, in_ref, out_ref):
    out_ref[...] = in_ref[...]


def group_kernel(piece_count, order, *refs):
    piece_refs, vec_refs, out_ref = refs[:piece_count], refs[piece_count:-1], refs[-1]
    piece_feats = piece_refs[0].shape[0]
    width = vec_refs[0].shape[1]
    feat_count = piece_count * piece_feats
    rank = lax.axis_index("rep")
    for piece, ref in enumerate(piece_refs):
        out_ref[piece * piece_feats : (piece + 1) * piece_feats, :] = ref[...]
    for spot, ref in zip(order, vec_refs):
        span = pl.ds(pl.multiple_of((rank ^ spot) * width, width), width)
        out_ref[feat_count:, span] = ref[...]


def columns_kernel(feat_count, first, group_ref, col_ref, vec_ref):
    chunk = 2 * vec_ref.shape[0]
    cols = group_ref[:feat_count, :]
    col_ref[:, : 3 * feat_count] = stacked(cols.T, "hhl", 1)
    flags = (col_ref.shape[0], col_ref.shape[1] - 3 * feat_count)
    block = lax.broadcasted_iota(jnp.int32, flags, 0) // vec_ref.shape[0] + first
    here = lax.broadcasted_iota(jnp.int32, flags, 1) == block
    col_ref[:, 3 * feat_count :] = jnp.where(here, 1.0, 0.0).astype(jnp.bfloat16)
    vecs = group_ref[feat_count:, :] * jnp.exp(jnp.sum(cols * cols, axis=0, keepdims=True) * (-1.0 / feat_count))
    for start in range(0, cols.shape[1], chunk):
        vec_ref[:, 3 * start : 3 * (start + chunk)] = stacked(vecs[:, start : start + chunk], "hhl", 1)


def rows_kernel(feat_count, group_blocks, *refs):
    panel_refs, (row_ref, scale_ref, listed_ref) = refs[:-3], refs[-3:]
    width = panel_refs[0].shape[1]
    blk_index = lax.axis_index("blk")
    listed_ref[...] = jnp.ones_like(listed_ref)
    for place, ref in enumerate(panel_refs):
        span = slice(place * width, (place + 1) * width)
        rows = ref[:feat_count, :]
        scale_ref[:, span] = jnp.exp(jnp.sum(rows * rows, axis=0, keepdims=True) * (-1.0 / feat_count))
        row_ref[: 3 * feat_count, span] = stacked(rows * (2.0 * LOG2_E / feat_count), "hlh", 0)
        lists = ref[feat_count:, :]
        for spot in range(2 * group_blocks):
            column = (blk_index ^ (spot // group_blocks)) * group_blocks + spot % group_blocks
            hits = jnp.where(lists == column.astype(jnp.float32), 1.0, 0.0)
            listed_ref[spot : spot + 1, span] = jnp.max(hits, axis=0, keepdims=True)
    row_ref[3 * feat_count :, :] = ((listed_ref[...] - 1.0) * 16384.0).astype(jnp.bfloat16)


def apply_kernel(row_ref, scale_ref, *refs):
    own_cols, own_vecs, sibling_cols, sibling_vecs, *out_refs = refs
    width = out_refs[0].shape[1]
    chunk = 2 * width
    pairs = range(len(out_refs) // 2)
    totals = [None for _ in pairs]
    for col_ref, vec_ref in ((own_cols, own_vecs), (sibling_cols, sibling_vecs)):
        for start in range(0, col_ref.shape[0], chunk):
            for pair in pairs:
                span = slice(pair * chunk, (pair + 1) * chunk)
                inner = jnp.dot(
                    col_ref[start : start + chunk, :], row_ref[:, span], preferred_element_type=jnp.float32
                )
                weight = stacked(jnp.exp2(inner), "hlh", 0)
                vecs = vec_ref[:, 3 * start : 3 * (start + chunk)]
                added = jnp.dot(vecs, weight, preferred_element_type=jnp.float32)
                totals[pair] = added if totals[pair] is None else totals[pair] + added
    for pair in pairs:
        total = totals[pair] * scale_ref[:, pair * chunk : (pair + 1) * chunk]
        out_refs[2 * pair][...] = total[:, :width]
        out_refs[2 * pair + 1][...] = total[:, width:]


def swapped(value, axis, step):
    count = lax.axis_size(axis)
    return lax.ppermute(value, axis, [(source, source ^ step) for source in range(count)])


def shards(coords, eigvecs, nbr_list, nbr_count):
    cycle_size = lax.axis_size("blk")
    rep_size = lax.axis_size("rep")
    rep_index = lax.axis_index("rep")
    group_blocks, slot_count = nbr_list.shape
    eig_count, width = eigvecs.shape
    piece_feats, group_cols = coords.shape
    feat_count = rep_size * piece_feats
    f32, bf16 = jnp.float32, jnp.bfloat16
    shape = jax.ShapeDtypeStruct
    smem = pl.BlockSpec(memory_space=pltpu.SMEM)
    vmem = pl.BlockSpec(memory_space=pltpu.VMEM)
    anywhere = pl.BlockSpec(memory_space=pl.ANY)
    params = pltpu.CompilerParams(vmem_limit_bytes=(8 + group_blocks) * 1024 * 1024)
    hint = pl.CostEstimate(flops=TRANSFER_FLOPS, bytes_accessed=1024 * 1024, transcendentals=0)

    pieces = [coords] + [swapped(coords, "rep", step) for step in range(1, rep_size)]
    late_vecs = pl.pallas_call(
        copy_kernel,
        in_specs=[anywhere, vmem],
        out_shape=shape(eigvecs.shape, f32),
        compiler_params=params,
    )(pieces[1], eigvecs)
    order = [*range(2, rep_size), 1, 0]
    vecs = [swapped(late_vecs, "rep", step) for step in order[:-1]] + [late_vecs]
    lists = pl.pallas_call(
        lists_kernel,
        in_specs=[smem, smem],
        out_shape=shape((slot_count, width), f32),
        compiler_params=params,
    )(nbr_list, nbr_count)

    own_block = [lax.dynamic_slice_in_dim(piece, rep_index * width, width, 1) for piece in pieces]
    panel = jnp.concatenate([*own_block, lists], axis=0)
    steps = list(range(0, cycle_size, 2))
    panels = [panel] + [swapped(panel, "blk", step) for step in steps[1:]]

    own_group = pl.pallas_call(
        functools.partial(group_kernel, rep_size, order),
        out_shape=shape((feat_count + eig_count, group_cols), f32),
        compiler_params=params,
    )(*pieces, *vecs)
    sibling_group = swapped(own_group, "blk", 1)

    depth = 3 * feat_count + max(16, 2 * group_blocks)

    def columns_of(group, first):
        return pl.pallas_call(
            functools.partial(columns_kernel, feat_count, first),
            out_shape=[shape((group_cols, depth), bf16), shape((eig_count, 3 * group_cols), bf16)],
            compiler_params=params,
        )(group)

    row_count = len(panels) * width
    rows = pl.pallas_call(
        functools.partial(rows_kernel, feat_count, group_blocks),
        out_shape=[shape((depth, row_count), bf16), shape((1, row_count), f32)],
        scratch_shapes=[pltpu.VMEM((depth - 3 * feat_count, row_count), f32)],
        compiler_params=params,
        cost_estimate=hint,
    )(*panels)
    columns = [*columns_of(own_group, 0), *columns_of(sibling_group, group_blocks)]
    tiles = pl.pallas_call(
        apply_kernel,
        out_shape=[shape((eig_count, width), f32)] * len(panels),
        compiler_params=params,
    )(*rows, *columns)
    total = tiles[0]
    for place in range(len(steps) - 1, 0, -1):
        total = total + swapped(tiles[place], "blk", steps[place])
    return total


def solution(mesh):
    return jax.shard_map(
        shards,
        mesh=mesh,
        in_specs=(P("rep", "blk"), P(None, ("blk", "rep")), P("blk", None), P("blk")),
        out_specs=P(None, ("blk", "rep")),
        check_vma=False,
    )
```
